32 devices in a mesh: fsdp: 2 (over core), context: 8 (over z, y), tensor: 2 (over x).
Axes of the slice: x: 2, y: 2, z: 4, core: 2. Of those that a mesh axis runs over, the one named last changes fastest.
Arguments:
- latents: bfloat16 [8, 2048, 1152], P('fsdp', ('context', 'tensor')), may hold values from -6 to 6
- text: bfloat16 [8, 120, 1152], P('fsdp'), may hold values from -6 to 6
- time_vector: bfloat16 [8, 6912], P('fsdp'), may hold values from -1.796875 to 1.796875
- table: bfloat16 [6, 1152], P(None, ('fsdp', 'context')), may hold values from -1.796875 to 1.796875
- w_qkv: bfloat16 [1152, 3, 1152], P(('fsdp', 'context'), None, 'tensor'), may hold values from -0.1875 to 0.1875
- w_out: bfloat16 [1152, 1152], P('tensor', ('fsdp', 'context')), may hold values from -0.5 to 0.5
- w_cq: bfloat16 [1152, 1152], P(('fsdp', 'context'), 'tensor'), may hold values from -0.1875 to 0.1875
- w_ckv: bfloat16 [1152, 2, 1152], P(('fsdp', 'context'), None, 'tensor'), may hold values from -0.1875 to 0.1875
- w_co: bfloat16 [1152, 1152], P('tensor', ('fsdp', 'context')), may hold values from -0.1875 to 0.1875
- w_up: bfloat16 [1152, 4608], P(('fsdp', 'context'), 'tensor'), may hold values from -0.1875 to 0.1875
- w_down: bfloat16 [4608, 1152], P('tensor', ('fsdp', 'context')), may hold values from -0.09375 to 0.09375
- cotangent: bfloat16 [8, 2048, 1152], P('fsdp', ('context', 'tensor')), may hold values from -6 to 6
Outputs:
- output: bfloat16 [8, 2048, 1152], P('fsdp', ('context', 'tensor'))
- grad_latents: float32 [8, 2048, 1152], P('fsdp', ('context', 'tensor'))
- grad_text: float32 [8, 120, 1152], P('fsdp')
- grad_time: float32 [8, 6912], P('fsdp')
- grad_table: float32 [6, 1152], P(None, ('fsdp', 'context'))
- grad_qkv: float32 [1152, 3, 1152], P(('fsdp', 'context'), None, 'tensor')
- grad_out: float32 [1152, 1152], P('tensor', ('fsdp', 'context'))
- grad_cq: float32 [1152, 1152], P(('fsdp', 'context'), 'tensor')
- grad_ckv: float32 [1152, 2, 1152], P(('fsdp', 'context'), None, 'tensor')
- grad_co: float32 [1152, 1152], P('tensor', ('fsdp', 'context'))
- grad_up: float32 [1152, 4608], P(('fsdp', 'context'), 'tensor')
- grad_down: float32 [4608, 1152], P('tensor', ('fsdp', 'context'))
The draws below stay inside these ranges and needn't reach their ends.
All inputs are finite; a program needn't handle non-finite values.
Results may differ from the reference program's by a relative error of at most 0.033.
Values may be sent and summed in bfloat16 or wider, within the bound.
No kernel may reach another device: no remote copies, remote signals or barrier semaphores. Data moves between devices by JAX's collectives and lax.ppermute only.
A program may use at most 256 MiB of HBM per device.

```python
import jax
import jax.numpy as jnp
from jax import lax

HEADS = 16
HEAD_DIM = 72
D = 1152
FF = 4608
TEXT = 120
LATENTS = 8
SEQ = 2048


def block_scale(key, dims, cuts, smallest, largest):
    level, own = 1.0, jax.random.fold_in(key, 6)
    for position, shards_of in cuts:
        draws = jnp.exp(jax.random.uniform(jax.random.fold_in(own, position), (shards_of,), jnp.float32, smallest / len(cuts), largest / len(cuts)))
        level = level * jnp.repeat(draws, dims[position] // shards_of).reshape([-1 if axis == position else 1 for axis in range(len(dims))])
    return level


def gaussian(stream_key, extent, scale, limit, cuts=(), held_as=jnp.bfloat16):
    values = jax.random.normal(stream_key, extent, jnp.float32) * scale
    if len(cuts) > 0:
        values = block_scale(stream_key, extent, cuts, -0.22, 0.18) * values
    return jnp.clip(values, min=-limit, max=limit).astype(held_as)


def setup_inputs(seed: int = 0) -> dict:
    arg_keys = jax.random.split(jax.random.key(seed), 13)
    latents = gaussian(arg_keys[0], (LATENTS, SEQ, D), 1.0, 6.0, ((0, 2), (1, 16)))
    text = gaussian(arg_keys[1], (LATENTS, TEXT, D), 1.0, 6.0, ((0, 2),))
    time_vector = gaussian(arg_keys[2], (LATENTS, 6 * D), 0.3, 1.796875, ((0, 2),))
    table = gaussian(arg_keys[3], (6, D), 0.3, 1.796875, ((1, 16),))
    w_qkv = gaussian(arg_keys[4], (D, 3, D), D ** -0.5, 0.1875, ((0, 16), (2, 2)))
    w_out = gaussian(arg_keys[5], (D, D), (D // 8) ** -0.5, 0.5, ((0, 2), (1, 16)))
    w_cq = gaussian(arg_keys[6], (D, D), D ** -0.5, 0.1875, ((0, 16), (1, 2)))
    w_ckv = gaussian(arg_keys[7], (D, 2, D), D ** -0.5, 0.1875, ((0, 16), (2, 2)))
    w_co = gaussian(arg_keys[8], (D, D), D ** -0.5, 0.1875, ((0, 2), (1, 16)))
    w_up = gaussian(arg_keys[9], (D, FF), D ** -0.5, 0.1875, ((0, 16), (1, 2)))
    w_down = gaussian(arg_keys[10], (FF, D), FF ** -0.5, 0.09375, ((0, 2), (1, 16)))
    cotangent = gaussian(arg_keys[11], (LATENTS, SEQ, D), 1.0, 6.0, ((0, 2), (1, 16)))
    return {"latents": latents, "text": text, "time_vector": time_vector, "table": table, "w_qkv": w_qkv, "w_out": w_out, "w_cq": w_cq, "w_ckv": w_ckv, "w_co": w_co, "w_up": w_up, "w_down": w_down, "cotangent": cotangent}


HIGH = lax.Precision.HIGHEST
EPSILON = 1e-06

@jax.custom_vjp
def low(v):
    return lax.optimization_barrier(v.astype(jnp.bfloat16)).astype(jnp.float32)

@jax.custom_vjp
def low_back(v):
    return v

def low_keep(v):
    return (low(v), None)

def low_pass(kept, grad):
    return (grad,)

def back_keep(v):
    return (v, None)

def back_low(kept, grad):
    return (low(grad),)
low.defvjp(low_keep, low_pass)
low_back.defvjp(back_keep, back_low)

def matmul(left, right):
    return jnp.dot(left, right, precision=HIGH, preferred_element_type=jnp.float32)

def layer_norm(values):
    center = values - lax.optimization_barrier(jnp.mean(values, axis=-1, keepdims=True))
    return center * lax.rsqrt(lax.optimization_barrier(jnp.mean(center * center, axis=-1, keepdims=True)) + EPSILON)

def self_rows(queries, keys, values):
    factor = HEAD_DIM ** (-0.5)
    scores = low_back(jnp.einsum('qhd,khd->hqk', queries, keys, precision=HIGH) * factor)
    top = lax.optimization_barrier(jnp.max(scores, axis=-1, keepdims=True))
    weights = jnp.exp(scores - top)
    probs = low(weights / lax.optimization_barrier(jnp.sum(weights, axis=-1, keepdims=True)))
    return jnp.einsum('hqk,khd->qhd', probs, values, precision=HIGH)

def latent_forward(params, latent, caption, time_row):
    table, w_qkv, w_out, w_cq, w_ckv, w_co, w_up, w_down = params
    length = latent.shape[0]
    block = min(512, length)
    factor = HEAD_DIM ** (-0.5)
    modulate = table + time_row.reshape(6, D)
    shift_one, scale_one, gate_one = (modulate[0], modulate[1], modulate[2])
    shift_two, scale_two, gate_two = (modulate[3], modulate[4], modulate[5])
    hidden_one = low(layer_norm(latent) * (1.0 + scale_one) + shift_one)
    projected = low_back(low(matmul(hidden_one, w_qkv.reshape(D, 3 * D)))).reshape(length, 3, HEADS, HEAD_DIM)
    queries = projected[:, 0].reshape(length // block, block, HEADS, HEAD_DIM)
    keys = projected[:, 1]
    values = projected[:, 2]
    checked = jax.checkpoint(self_rows)
    attended = lax.map(lambda part: checked(part, keys, values), queries).reshape(length, D)
    attended = low_back(low(attended))
    out_one = low_back(matmul(attended, w_out))
    after_one = latent + gate_one * out_one
    cross_q = low_back(low(matmul(low(after_one), w_cq))).reshape(length, HEADS, HEAD_DIM)
    cross_kv = low_back(low(matmul(caption, w_ckv.reshape(D, 2 * D)))).reshape(TEXT, 2, HEADS, HEAD_DIM)
    cross_scores = low_back(jnp.einsum('qhd,khd->hqk', cross_q, cross_kv[:, 0], precision=HIGH) * factor)
    cross_top = lax.optimization_barrier(jnp.max(cross_scores, axis=-1, keepdims=True))
    cross_exp = jnp.exp(cross_scores - cross_top)
    cross_prob = low(cross_exp / lax.optimization_barrier(jnp.sum(cross_exp, axis=-1, keepdims=True)))
    cross_out = jnp.einsum('hqk,khd->qhd', cross_prob, cross_kv[:, 1], precision=HIGH).reshape(length, D)
    cross_out = low_back(low(cross_out))
    out_two = low_back(matmul(cross_out, w_co))
    after_two = after_one + out_two
    hidden_two = low(layer_norm(after_two) * (1.0 + scale_two) + shift_two)
    inner = low_back(matmul(hidden_two, w_up))
    active = low(jax.nn.gelu(inner, approximate=True))
    out_three = low_back(matmul(active, w_down))
    return after_two + gate_two * out_three

def reference(latents, text, time_vector, table, w_qkv, w_out, w_cq, w_ckv, w_co, w_up, w_down, cotangent):
    params = tuple((weight.astype(jnp.float32) for weight in (table, w_qkv, w_out, w_cq, w_ckv, w_co, w_up, w_down)))

    def visit(totals, sample):
        latent, caption, time_row, grad_output = sample
        result, pullback = jax.vjp(latent_forward, params, latent, caption, time_row)
        grad_params, grad_latent, grad_caption, grad_row = pullback(grad_output)
        totals = tuple((first + second for first, second in zip(totals, grad_params)))
        return (totals, (result.astype(jnp.bfloat16), grad_latent, grad_caption, grad_row))
    start = tuple((jnp.zeros_like(weight) for weight in params))
    totals, outputs = lax.scan(visit, start, (latents.astype(jnp.float32), text.astype(jnp.float32), time_vector.astype(jnp.float32), cotangent.astype(jnp.float32)))
    output, grad_latents, grad_text, grad_time = outputs
    return (output, grad_latents, grad_text, grad_time, totals[0], totals[1], totals[2], totals[3], totals[4], totals[5], totals[6], totals[7])
```

```python
import math
from functools import partial

import jax
import jax.numpy as jnp
from jax import lax
from jax.experimental import pallas as pl
from jax.experimental.pallas import tpu as pltpu
from jax.sharding import Mesh
from jax.sharding import PartitionSpec as P

HEAD_DIM = 72
EPSILON = 1e-06
LANES = 128
FACTOR = HEAD_DIM ** (-0.5)
FACTOR2 = FACTOR * math.log2(math.e)
VMEM_LIMIT = 56 * 1024 * 1024

f32 = jnp.float32
bf16 = jnp.bfloat16

NT = (((1,), (1,)), ((), ()))
NN = (((1,), (0,)), ((), ()))
TN = (((0,), (0,)), ((), ()))

EVERY = ("tensor", "fsdp", "lat", "sr", "hr")
PLANE = ("sr", "hr", "tensor")
HEAD_GROUP = ("hr", "tensor")


def dot(left, right, dims=NN):
    return lax.dot_general(left, right, dims, preferred_element_type=f32)


def norm_parts(values):
    center = values - jnp.mean(values, axis=-1, keepdims=True)
    inverse = lax.rsqrt(jnp.mean(center * center, axis=-1, keepdims=True) + EPSILON)
    return (center * inverse, inverse)


def norm_back(grad_hat, normed, inverse):
    first = jnp.mean(grad_hat, axis=-1, keepdims=True)
    second = jnp.mean(grad_hat * normed, axis=-1, keepdims=True)
    return inverse * (grad_hat - first - normed * second)


def send_xor(piece, axes, step):
    size = lax.axis_size(axes)
    return lax.ppermute(piece, axes, [(rank, rank ^ step) for rank in range(size)])


def pick(stack, index):
    return lax.dynamic_index_in_dim(stack, index, 0, keepdims=False)


def exchange(stack, axes):
    size = lax.axis_size(axes)
    me = lax.axis_index(axes)
    got = [pick(stack, me)]
    for step in range(1, size):
        got.append(send_xor(pick(stack, jnp.bitwise_xor(me, step)), axes, step))
    return got


def give_back(pieces, axes):
    me = lax.axis_index(axes)
    out = jnp.zeros((len(pieces),) + pieces[0].shape, pieces[0].dtype)
    for step, piece in enumerate(pieces):
        arrived = send_xor(piece, axes, step) if step else piece
        out = lax.dynamic_update_index_in_dim(out, arrived, jnp.bitwise_xor(me, step), 0)
    return out


def plane_sum(values, dtype):
    step = 1
    while step < lax.axis_size(PLANE):
        sent = values.astype(dtype)
        values = sent.astype(f32) + send_xor(sent, PLANE, step).astype(f32)
        step *= 2
    return values


def over_latents(values):
    return give_back([values] * lax.axis_size("lat"), "lat")


def attend_kernel(heads, q_ref, kv_ref, low_ref, att_ref, lse_ref, keys, vals, column):
    edge = heads * HEAD_DIM

    @pl.when(pl.program_id(0) == 0)
    def _():
        for head in range(heads):
            low = head * HEAD_DIM
            keys[head] = kv_ref[:, edge + low : edge + low + HEAD_DIM]
            vals[head] = kv_ref[:, 2 * edge + low : 2 * edge + low + HEAD_DIM]

    column[...] = jnp.zeros_like(column)
    for head in range(heads):
        low = head * HEAD_DIM
        scores = dot(q_ref[:, low : low + HEAD_DIM], keys[head], NT)
        top = jnp.max(scores, axis=1, keepdims=True)
        weights = jnp.exp2(scores * FACTOR2 - top * FACTOR2)
        total = jnp.sum(weights, axis=1, keepdims=True)
        out = dot(weights.astype(bf16), vals[head]) / total
        att_ref[:, low : low + HEAD_DIM] = out
        low_ref[:, low : low + HEAD_DIM] = out.astype(bf16)
        column[:, head : head + 1] = top * FACTOR2 + jnp.log2(total)
    lse_ref[...] = column[...].T[: lse_ref.shape[0]]


def attend(queries, keys_vals, heads):
    rows, width = queries.shape
    count = keys_vals.shape[0]
    block = min(256, rows)
    edge = heads * HEAD_DIM
    slots = -(-heads // 8) * 8
    return pl.pallas_call(
        partial(attend_kernel, heads),
        grid=(rows // block,),
        in_specs=[
            pl.BlockSpec((block, width), lambda i: (i, 0)),
            pl.BlockSpec((count, width), lambda i: (0, 0)),
        ],
        out_specs=[
            pl.BlockSpec((block, edge), lambda i: (i, 0)),
            pl.BlockSpec((block, edge), lambda i: (i, 0)),
            pl.BlockSpec((slots, block), lambda i: (0, i)),
        ],
        out_shape=[
            jax.ShapeDtypeStruct((rows, edge), bf16),
            jax.ShapeDtypeStruct((rows, edge), f32),
            jax.ShapeDtypeStruct((slots, rows), f32),
        ],
        scratch_shapes=[
            pltpu.VMEM((heads, count, HEAD_DIM), bf16),
            pltpu.VMEM((heads, count, HEAD_DIM), bf16),
            pltpu.VMEM((block, LANES), f32),
        ],
        compiler_params=pltpu.CompilerParams(vmem_limit_bytes=VMEM_LIMIT),
    )(queries, keys_vals)


def attend_back_kernel(
    heads, chunk, q_ref, kv_ref, att_ref, grad_ref, lse_ref, out_ref, keys, vals, turned, dk, dv, column
):
    edge = heads * HEAD_DIM
    index = pl.program_id(0)
    block = q_ref.shape[0]
    count = kv_ref.shape[0]

    @pl.when(index == 0)
    def _():
        turned[...] = jnp.zeros_like(turned)
        for head in range(heads):
            low = head * HEAD_DIM
            piece = kv_ref[:, edge + low : edge + low + HEAD_DIM]
            keys[head] = piece
            turned[head, :HEAD_DIM, :] = piece.astype(f32).T.astype(bf16)
            vals[head] = kv_ref[:, 2 * edge + low : 2 * edge + low + HEAD_DIM]
        dk[...] = jnp.zeros_like(dk)
        dv[...] = jnp.zeros_like(dv)
        out_ref[...] = jnp.zeros_like(out_ref)

    column[...] = jnp.zeros_like(column)
    product = att_ref[...] * grad_ref[...].astype(f32)
    for head in range(heads):
        low = head * HEAD_DIM
        column[:, head : head + 1] = jnp.sum(
            product[:, low : low + HEAD_DIM], axis=1, keepdims=True
        )
    deltas = column[...].T
    rows = pl.ds(pl.multiple_of(index * block, block), block)
    for head in range(heads):
        low = head * HEAD_DIM
        query = q_ref[:, low : low + HEAD_DIM]
        grad = grad_ref[:, low : low + HEAD_DIM]
        lse = lse_ref[head : head + 1, :]
        delta = deltas[head : head + 1, :]
        total = jnp.zeros((turned.shape[1], block), f32)
        for start in range(0, count, chunk):
            part = slice(start, start + chunk)
            scores = dot(keys[head, part, :], query, NT)
            probs = jnp.exp2(scores * FACTOR2 - lse)
            grad_probs = dot(vals[head, part, :], grad, NT)
            grad_scores = (probs * (grad_probs - delta)).astype(bf16)
            dv[head, part, :] += dot(probs.astype(bf16), grad)
            dk[head, part, :] += dot(grad_scores, query)
            total += dot(turned[head, :, part], grad_scores)
        out_ref[rows, low : low + HEAD_DIM] = (total.T[:, :HEAD_DIM] * FACTOR).astype(bf16)

    @pl.when(index == pl.num_programs(0) - 1)
    def _():
        for head in range(heads):
            low = head * HEAD_DIM
            out_ref[:, edge + low : edge + low + HEAD_DIM] = (dk[head] * FACTOR).astype(bf16)
            out_ref[:, 2 * edge + low : 2 * edge + low + HEAD_DIM] = dv[head].astype(bf16)


def attend_back(queries, keys_vals, att, grad, lse, heads):
    rows, width = queries.shape
    count = keys_vals.shape[0]
    block = min(256, rows)
    edge = heads * HEAD_DIM
    slots = lse.shape[0]
    return pl.pallas_call(
        partial(attend_back_kernel, heads, min(512, count)),
        grid=(rows // block,),
        in_specs=[
            pl.BlockSpec((block, width), lambda i: (i, 0)),
            pl.BlockSpec((count, width), lambda i: (0, 0)),
            pl.BlockSpec((block, edge), lambda i: (i, 0)),
            pl.BlockSpec((block, edge), lambda i: (i, 0)),
            pl.BlockSpec((slots, block), lambda i: (0, i)),
        ],
        out_specs=pl.BlockSpec((count, width), lambda i: (0, 0)),
        out_shape=jax.ShapeDtypeStruct((count, width), bf16),
        scratch_shapes=[
            pltpu.VMEM((heads, count, HEAD_DIM), bf16),
            pltpu.VMEM((heads, count, HEAD_DIM), bf16),
            pltpu.VMEM((heads, LANES, count), bf16),
            pltpu.VMEM((heads, count, HEAD_DIM), f32),
            pltpu.VMEM((heads, count, HEAD_DIM), f32),
            pltpu.VMEM((block, LANES), f32),
        ],
        compiler_params=pltpu.CompilerParams(vmem_limit_bytes=VMEM_LIMIT),
    )(queries, keys_vals, att, grad, lse)


def cross_kernel(q_ref, k_ref, v_ref, out_ref):
    for low in range(0, q_ref.shape[1], HEAD_DIM):
        part = slice(low, low + HEAD_DIM)
        scores = dot(q_ref[:, part], k_ref[:, part], NT) * FACTOR
        weights = jnp.exp(scores - jnp.max(scores, axis=1, keepdims=True))
        probs = weights / jnp.sum(weights, axis=1, keepdims=True)
        out_ref[:, part] = dot(probs.astype(bf16), v_ref[:, part]).astype(bf16)


def cross(queries, keys, values):
    rows, width = queries.shape
    texts = keys.shape[0]
    block = min(256, rows)
    return pl.pallas_call(
        cross_kernel,
        grid=(rows // block,),
        in_specs=[
            pl.BlockSpec((block, width), lambda i: (i, 0)),
            pl.BlockSpec((texts, width), lambda i: (0, 0)),
            pl.BlockSpec((texts, width), lambda i: (0, 0)),
        ],
        out_specs=pl.BlockSpec((block, width), lambda i: (i, 0)),
        out_shape=jax.ShapeDtypeStruct((rows, width), bf16),
        compiler_params=pltpu.CompilerParams(vmem_limit_bytes=VMEM_LIMIT),
    )(queries, keys, values)


def cross_back_kernel(q_ref, k_ref, v_ref, grad_ref, dq_ref, dk_ref, dv_ref, dk, dv):
    @pl.when(pl.program_id(0) == 0)
    def _():
        dk[...] = jnp.zeros_like(dk)
        dv[...] = jnp.zeros_like(dv)

    for low in range(0, q_ref.shape[1], HEAD_DIM):
        part = slice(low, low + HEAD_DIM)
        query = q_ref[:, part]
        key = k_ref[:, part]
        grad = grad_ref[:, part]
        scores = dot(query, key, NT) * FACTOR
        weights = jnp.exp(scores - jnp.max(scores, axis=1, keepdims=True))
        probs = weights / jnp.sum(weights, axis=1, keepdims=True)
        grad_probs = dot(grad, v_ref[:, part], NT)
        delta = jnp.sum(probs * grad_probs, axis=1, keepdims=True)
        grad_scores = (probs * (grad_probs - delta)).astype(bf16)
        dq_ref[:, part] = (dot(grad_scores, key) * FACTOR).astype(bf16)
        dk[:, part] += dot(grad_scores, query, TN)
        dv[:, part] += dot(probs.astype(bf16), grad, TN)

    @pl.when(pl.program_id(0) == pl.num_programs(0) - 1)
    def _():
        dk_ref[...] = (dk[...] * FACTOR).astype(bf16)
        dv_ref[...] = dv[...].astype(bf16)


def cross_back(queries, keys, values, grad):
    rows, width = queries.shape
    texts = keys.shape[0]
    block = min(256, rows)
    whole = pl.BlockSpec((texts, width), lambda i: (0, 0))
    split = pl.BlockSpec((block, width), lambda i: (i, 0))
    return pl.pallas_call(
        cross_back_kernel,
        grid=(rows // block,),
        in_specs=[split, whole, whole, split],
        out_specs=[split, whole, whole],
        out_shape=[
            jax.ShapeDtypeStruct((rows, width), bf16),
            jax.ShapeDtypeStruct((texts, width), bf16),
            jax.ShapeDtypeStruct((texts, width), bf16),
        ],
        scratch_shapes=[pltpu.VMEM((texts, width), f32), pltpu.VMEM((texts, width), f32)],
        compiler_params=pltpu.CompilerParams(vmem_limit_bytes=VMEM_LIMIT),
    )(queries, keys, values, grad)


def gather(stack):
    return lax.all_gather(stack, EVERY, axis=1, tiled=True)


def scatter(stack):
    return lax.psum_scatter(stack, EVERY, scatter_dimension=0, tiled=True).astype(f32)


def local(
    latents, text, time_vector, table, w_qkv, w_out, w_cq, w_ckv, w_co, w_up, w_down, cotangent
):
    width = latents.shape[2]
    share = w_cq.shape[0]
    part = w_cq.shape[1]
    inner_part = w_up.shape[1]
    splits = lax.axis_size("tensor")
    ranks = lax.axis_size("hr")
    halves = lax.axis_size("sr")
    edge = part // ranks
    heads = edge // HEAD_DIM
    piece_width = -(-(3 * edge + 6) // LANES) * LANES
    texts = text.shape[1]
    slot = lax.axis_index("lat")

    shard_qkv = jnp.transpose(w_qkv.reshape(share, 3, ranks, edge), (2, 0, 1, 3)).reshape(
        ranks, share, 3 * edge
    )
    table_part = jnp.zeros((ranks, share, piece_width - 3 * edge), bf16).at[:, :, :6].set(table.T)
    full_one = gather(jnp.concatenate((shard_qkv, table_part), axis=2))
    full_mid = gather(jnp.stack((w_ckv[:, 0], w_ckv[:, 1], w_cq, w_co.T, w_out.T)))
    full_two = gather(jnp.stack((w_up, w_down.T)))
    full_one = full_one.reshape(ranks, splits, width, piece_width)
    full_mid = full_mid.reshape(5, splits, width, part)
    full_two = full_two.reshape(2, splits, width, inner_part)
    up_full, down_full = (full_two[0], full_two[1])
    key_full, val_full, cq_full, co_full, out_full = (full_mid[row] for row in range(5))

    residual = jnp.concatenate(exchange(latents, "lat"), axis=0).astype(f32)
    grad_three = jnp.concatenate(exchange(cotangent, "lat"), axis=0).astype(f32)
    rows = residual.shape[0]
    caption = pick(text, slot)

    modulate = full_one[0, 0, :, 3 * edge : 3 * edge + 6].T.astype(f32) + pick(
        time_vector, slot
    ).astype(f32).reshape(6, width)
    shift_one, scale_one, gate_one, shift_two, scale_two, gate_two = (
        modulate[row : row + 1] for row in range(6)
    )

    normed_one, inverse_one = norm_parts(residual)
    hidden_one = (normed_one * (1.0 + scale_one) + shift_one).astype(bf16)
    projected = jnp.stack(
        [
            dot(hidden_one, full_one[rank, split]).astype(bf16)
            for rank in range(ranks)
            for split in range(splits)
        ]
    )
    mixed = jnp.concatenate(exchange(projected, HEAD_GROUP), axis=0)
    if halves > 1:
        keys_vals = lax.all_gather(mixed, "sr", axis=0, tiled=True)
    else:
        keys_vals = mixed
    att_low, att_wide, logsum = attend(mixed, keys_vals, heads)
    groups = ranks * splits
    att_back = give_back(list(att_low.reshape(groups, rows, edge)), HEAD_GROUP)
    att_back = att_back.reshape(ranks, splits, rows, edge)
    att = jnp.transpose(att_back, (2, 1, 0, 3)).reshape(rows, splits, part)

    out_one = jnp.einsum("ste,tde->sd", att, out_full, preferred_element_type=f32)
    after_one = residual + gate_one * out_one
    mid_low = after_one.astype(bf16)
    cross_q = (
        jnp.einsum("sd,tde->ste", mid_low, cq_full, preferred_element_type=f32)
        .astype(bf16)
        .reshape(rows, width)
    )
    cross_k = (
        jnp.einsum("sd,tde->ste", caption, key_full, preferred_element_type=f32)
        .astype(bf16)
        .reshape(texts, width)
    )
    cross_v = (
        jnp.einsum("sd,tde->ste", caption, val_full, preferred_element_type=f32)
        .astype(bf16)
        .reshape(texts, width)
    )
    cross_low = cross(cross_q, cross_k, cross_v)
    cross_split = cross_low.reshape(rows, splits, part)
    out_two = jnp.einsum("ste,tde->sd", cross_split, co_full, preferred_element_type=f32)
    after_two = after_one + out_two
    normed_two, inverse_two = norm_parts(after_two)
    hidden_two = (normed_two * (1.0 + scale_two) + shift_two).astype(bf16)
    inner = [dot(hidden_two, up_full[split]) for split in range(splits)]
    active = [jax.nn.gelu(values, approximate=True).astype(bf16) for values in inner]
    out_three = sum(dot(active[split], down_full[split], NT) for split in range(splits))
    result = (after_two + gate_two * out_three).astype(bf16)
    result_back = give_back(list(result.reshape(latents.shape)), "lat")

    grad_gate_two = jnp.sum(grad_three * out_three, axis=0)
    grad_z = (gate_two * grad_three).astype(bf16)
    grad_inner = []
    for split in range(splits):
        grad_active = dot(grad_z, down_full[split])
        _, pull = jax.vjp(partial(jax.nn.gelu, approximate=True), inner[split])
        grad_inner.append(pull(grad_active)[0].astype(bf16))
    grad_two_pack = jnp.concatenate(
        [
            jnp.concatenate([dot(hidden_two, piece, TN).astype(bf16) for piece in grad_inner]),
            jnp.concatenate([dot(grad_z, piece, TN).astype(bf16) for piece in active]),
        ],
        axis=1,
    )
    sum_two = scatter(grad_two_pack)
    grad_hidden_two = sum(dot(grad_inner[split], up_full[split], NT) for split in range(splits))
    grad_shift_two = jnp.sum(grad_hidden_two, axis=0)
    grad_scale_two = jnp.sum(grad_hidden_two * normed_two, axis=0)
    grad_two = grad_three + norm_back(grad_hidden_two * (1.0 + scale_two), normed_two, inverse_two)

    grad_out_two = grad_two.astype(bf16)
    grad_cross = (
        jnp.einsum("sd,tde->ste", grad_out_two, co_full, preferred_element_type=f32)
        .astype(bf16)
        .reshape(rows, width)
    )
    grad_cq, grad_ck, grad_cv = cross_back(cross_q, cross_k, cross_v, grad_cross)
    grad_cq = grad_cq.reshape(rows, splits, part)
    grad_ck = grad_ck.reshape(texts, splits, part)
    grad_cv = grad_cv.reshape(texts, splits, part)
    grad_one = grad_two + jnp.einsum("ste,tde->sd", grad_cq, cq_full, preferred_element_type=f32)
    text_terms = jnp.einsum(
        "ste,tde->sd", grad_ck, key_full, preferred_element_type=f32
    ) + jnp.einsum("ste,tde->sd", grad_cv, val_full, preferred_element_type=f32)

    grad_gate_one = jnp.sum(grad_one * out_one, axis=0)
    grad_out_one = (gate_one * grad_one).astype(bf16)
    grad_att = jnp.einsum("sd,tde->ste", grad_out_one, out_full, preferred_element_type=f32)
    grad_att = jnp.transpose(
        grad_att.astype(bf16).reshape(rows, splits, ranks, edge), (2, 1, 0, 3)
    ).reshape(groups, rows, edge)
    grad_heads = jnp.concatenate(exchange(grad_att, HEAD_GROUP), axis=0)
    grad_mix = attend_back(mixed, keys_vals, att_wide, grad_heads, logsum, heads)
    if halves > 1:
        grad_kv = lax.psum_scatter(grad_mix, "sr", scatter_dimension=0, tiled=True)
        grad_mix = jnp.concatenate((grad_mix[: mixed.shape[0], :edge], grad_kv[:, edge:]), axis=1)
    grad_proj = give_back(list(grad_mix.reshape(groups, rows, piece_width)), HEAD_GROUP)
    grad_proj = grad_proj.reshape(ranks, splits, rows, piece_width)
    grad_hidden_one = sum(
        dot(grad_proj[rank, split], full_one[rank, split], NT)
        for rank in range(ranks)
        for split in range(splits)
    )
    grad_shift_one = jnp.sum(grad_hidden_one, axis=0)
    grad_scale_one = jnp.sum(grad_hidden_one * normed_one, axis=0)
    grad_latents = grad_one + norm_back(
        grad_hidden_one * (1.0 + scale_one), normed_one, inverse_one
    )
    grad_latents = give_back(list(grad_latents.astype(bf16).reshape(latents.shape)), "lat")

    mid_pack = [
        jnp.einsum("kd,kte->tde", caption, grad_ck, preferred_element_type=f32),
        jnp.einsum("kd,kte->tde", caption, grad_cv, preferred_element_type=f32),
        jnp.einsum("kd,kte->tde", mid_low, grad_cq, preferred_element_type=f32),
        jnp.einsum("kd,kte->tde", grad_out_two, cross_split, preferred_element_type=f32),
        jnp.einsum("kd,kte->tde", grad_out_one, att, preferred_element_type=f32),
    ]
    mid_pack = [values.astype(bf16).reshape(splits * width, part) for values in mid_pack]
    mid_fill = jnp.zeros((splits * width, -5 * part % LANES), bf16)
    sum_mid = scatter(jnp.concatenate(mid_pack + [mid_fill], axis=1))
    sum_mid = [sum_mid[:, place * part : (place + 1) * part] for place in range(5)]
    time_terms = jnp.stack(
        (
            grad_shift_one,
            grad_scale_one,
            grad_gate_one,
            grad_shift_two,
            grad_scale_two,
            grad_gate_two,
        )
    )
    table_terms = jnp.pad(time_terms.T, ((0, 0), (3 * edge, piece_width - 3 * edge - 6)))
    sum_one = scatter(
        jnp.concatenate(
            [
                jnp.concatenate(
                    [
                        (dot(hidden_one, grad_proj[rank, split], TN) + table_terms).astype(bf16)
                        for split in range(splits)
                    ]
                )
                for rank in range(ranks)
            ],
            axis=1,
        )
    ).reshape(share, ranks, piece_width)
    grad_time = over_latents(plane_sum(time_terms, f32)).reshape(-1, 6 * width)
    grad_text = over_latents(plane_sum(text_terms, bf16).astype(bf16)).astype(f32)
    grad_qkv = jnp.transpose(
        sum_one[:, :, : 3 * edge].reshape(share, ranks, 3, edge), (0, 2, 1, 3)
    ).reshape(share, 3, part)
    return (
        result_back,
        grad_latents.astype(f32),
        grad_text,
        grad_time,
        sum_one[:, 0, 3 * edge : 3 * edge + 6].T,
        grad_qkv,
        sum_mid[4].T,
        sum_mid[2],
        jnp.stack((sum_mid[0], sum_mid[1]), axis=1),
        sum_mid[3].T,
        sum_two[:, :inner_part],
        sum_two[:, inner_part:].T,
    )


def solution(mesh):
    def run(latents, text, time_vector, table, w_qkv, *others):
        fsdp, context, tensor = (mesh.shape[name] for name in ("fsdp", "context", "tensor"))
        lat = latents.shape[0] // fsdp
        group = context // lat
        ranks = math.gcd(group, w_qkv.shape[2] // (tensor * HEAD_DIM))
        sizes = (fsdp, lat, group // ranks, ranks, tensor)
        finer = Mesh(mesh.devices.reshape(sizes), ("fsdp", "lat", "sr", "hr", "tensor"))
        line = ("lat", "sr", "hr")
        shard = ("fsdp",) + line
        tokens = P("fsdp", line + ("tensor",), None)
        by_row = P(shard, "tensor")
        by_row3 = P(shard, None, "tensor")
        by_column = P("tensor", shard)
        weights = (by_row3, by_column, by_row, by_row3, by_column, by_row, by_column)
        return jax.shard_map(
            local,
            mesh=finer,
            in_specs=(tokens, P("fsdp", None, None), P("fsdp", None), P(None, shard))
            + weights
            + (tokens,),
            out_specs=(tokens, tokens, P("fsdp", None, None), P("fsdp", None), P(None, shard))
            + weights,
            check_vma=False,
        )(latents, text, time_vector, table, w_qkv, *others)

    return run
```

```python
import math
from functools import partial

import jax
import jax.numpy as jnp
from jax import lax
from jax.experimental import pallas as pl
from jax.experimental.pallas import tpu as pltpu
from jax.sharding import Mesh
from jax.sharding import PartitionSpec as P

HEAD_DIM = 72
EPSILON = 1e-06
LANES = 128
FACTOR = HEAD_DIM ** (-0.5)
FACTOR2 = FACTOR * math.log2(math.e)
VMEM_LIMIT = 56 * 1024 * 1024

f32 = jnp.float32
bf16 = jnp.bfloat16

NT = (((1,), (1,)), ((), ()))
NN = (((1,), (0,)), ((), ()))
TN = (((0,), (0,)), ((), ()))

CHIPS = ("tensor", "lat", "sr", "hr")
PLANE = ("sr", "hr", "tensor")
HEAD_GROUP = ("hr", "tensor")


def dot(left, right, dims=NN):
    return lax.dot_general(left, right, dims, preferred_element_type=f32)


def norm_parts(values):
    center = values - jnp.mean(values, axis=-1, keepdims=True)
    inverse = lax.rsqrt(jnp.mean(center * center, axis=-1, keepdims=True) + EPSILON)
    return (center * inverse, inverse)


def norm_back(grad_hat, normed, inverse):
    first = jnp.mean(grad_hat, axis=-1, keepdims=True)
    second = jnp.mean(grad_hat * normed, axis=-1, keepdims=True)
    return inverse * (grad_hat - first - normed * second)


def send_xor(piece, axes, step):
    size = lax.axis_size(axes)
    return lax.ppermute(piece, axes, [(rank, rank ^ step) for rank in range(size)])


def pick(stack, index):
    return lax.dynamic_index_in_dim(stack, index, 0, keepdims=False)


def exchange(piece_for, axes):
    me = lax.axis_index(axes)
    got = [piece_for(me)]
    for step in range(1, lax.axis_size(axes)):
        got.append(send_xor(piece_for(jnp.bitwise_xor(me, step)), axes, step))
    return got


def give_back(pieces, axes):
    return [send_xor(piece, axes, step) if step else piece for step, piece in enumerate(pieces)]


def in_order(pieces, axes):
    me = lax.axis_index(axes)
    out = jnp.zeros((len(pieces),) + pieces[0].shape, pieces[0].dtype)
    for step, piece in enumerate(pieces):
        out = lax.dynamic_update_index_in_dim(out, piece, jnp.bitwise_xor(me, step), 0)
    return out


def plane_sum(values, dtype):
    sent = values.astype(dtype)
    total = sent.astype(f32)
    for step in range(1, lax.axis_size(PLANE)):
        total += send_xor(sent, PLANE, step).astype(f32)
    return total


def over_latents(values):
    return in_order(give_back([values] * lax.axis_size("lat"), "lat"), "lat")


def tie(first, second):
    return lax.optimization_barrier((first, second))


def attend_kernel(heads, chunks, own, *refs):
    pieces = refs[:chunks]
    low_refs = refs[chunks : chunks + own]
    att_ref, lse_ref, queries, keys, vals, lows, column = refs[chunks + own :]
    edge = heads * HEAD_DIM
    index = pl.program_id(0)
    block = att_ref.shape[1]

    @pl.when(index == 0)
    def _():
        lane = lax.broadcasted_iota(jnp.int32, vals.shape[1:], 1)
        column[...] = jnp.zeros_like(column)
        for head in range(heads):
            vals[head] = jnp.where(lane == HEAD_DIM, 1.0, 0.0).astype(bf16)
            low = head * HEAD_DIM
            for number, piece in enumerate(pieces):
                count = piece.shape[0]
                rows = slice(number * count, (number + 1) * count)
                if number < own:
                    queries[head, rows] = piece[:, low : low + HEAD_DIM]
                keys[head, rows] = piece[:, edge + low : edge + low + HEAD_DIM]
                vals[head, rows, :HEAD_DIM] = piece[:, 2 * edge + low : 2 * edge + low + HEAD_DIM]

    mine = pl.ds(pl.multiple_of(index * block, block), block)

    def score(head):
        return dot(queries[head, mine, :], keys[head], NT)

    ahead = score(0)
    for head in range(heads):
        scores = ahead
        if head + 1 < heads:
            ahead = score(head + 1)
        top = jnp.max(scores, axis=1, keepdims=True) * FACTOR2
        weights = jnp.exp2(scores * FACTOR2 - top).astype(bf16)
        out = dot(weights, vals[head])
        total = out[:, HEAD_DIM : HEAD_DIM + 1]
        out = out[:, :HEAD_DIM] / total
        att_ref[head] = out
        lows[head, mine, :] = out.astype(bf16)
        column[:, head : head + 1] = top + jnp.log2(total)
    lse_ref[...] = column[...].T[: lse_ref.shape[0]]

    @pl.when(index == pl.num_programs(0) - 1)
    def _():
        for head in range(heads):
            low = head * HEAD_DIM
            for number, ref in enumerate(low_refs):
                count = ref.shape[0]
                ref[:, low : low + HEAD_DIM] = lows[head, number * count : (number + 1) * count, :]


def whole_block(shape):
    return pl.BlockSpec(shape, lambda i: (0,) * len(shape))


def attend(pieces, own, heads):
    count, width = pieces[0].shape
    rows, total = own * count, len(pieces) * count
    block = min(256, rows)
    edge = heads * HEAD_DIM
    slots = -(-heads // 8) * 8
    out = pl.pallas_call(
        partial(attend_kernel, heads, len(pieces), own),
        grid=(rows // block,),
        in_specs=[whole_block((count, width))] * len(pieces),
        out_specs=[whole_block((count, edge))] * own
        + [
            pl.BlockSpec((heads, block, HEAD_DIM), lambda i: (0, i, 0)),
            pl.BlockSpec((slots, block), lambda i: (0, i)),
        ],
        out_shape=[jax.ShapeDtypeStruct((count, edge), bf16)] * own
        + [
            jax.ShapeDtypeStruct((heads, rows, HEAD_DIM), f32),
            jax.ShapeDtypeStruct((slots, rows), f32),
        ],
        scratch_shapes=[
            pltpu.VMEM((heads, rows, HEAD_DIM), bf16),
            pltpu.VMEM((heads, total, HEAD_DIM), bf16),
            pltpu.VMEM((heads, total, LANES), bf16),
            pltpu.VMEM((heads, rows, HEAD_DIM), bf16),
            pltpu.VMEM((block, LANES), f32),
        ],
        compiler_params=pltpu.CompilerParams(vmem_limit_bytes=VMEM_LIMIT),
    )(*pieces)
    return (out[:own], out[own], out[own + 1])


def attend_back_kernel(heads, chunk, chunks, own, *refs):
    pieces = refs[:chunks]
    grad_refs = refs[chunks : chunks + own]
    att_ref, lse_ref = refs[chunks + own : chunks + own + 2]
    outs = refs[chunks + own + 2 : 2 * chunks + own + 2]
    queries, keys, vals, grads, turned, dq, dk, dv, column = refs[2 * chunks + own + 2 :]
    edge = heads * HEAD_DIM
    index = pl.program_id(0)
    block = att_ref.shape[1]
    total = keys.shape[1]

    @pl.when(index == 0)
    def _():
        turned[...] = jnp.zeros_like(turned)
        column[...] = jnp.zeros_like(column)
        dk[...] = jnp.zeros_like(dk)
        dv[...] = jnp.zeros_like(dv)
        for head in range(heads):
            low = head * HEAD_DIM
            for number, piece in enumerate(pieces):
                count = piece.shape[0]
                rows = slice(number * count, (number + 1) * count)
                if number < own:
                    queries[head, rows] = piece[:, low : low + HEAD_DIM]
                    grads[head, rows] = grad_refs[number][:, low : low + HEAD_DIM]
                key = piece[:, edge + low : edge + low + HEAD_DIM]
                keys[head, rows] = key
                turned[head, :HEAD_DIM, rows] = key.astype(f32).T.astype(bf16)
                vals[head, rows] = piece[:, 2 * edge + low : 2 * edge + low + HEAD_DIM]

    mine = pl.ds(pl.multiple_of(index * block, block), block)
    for head in range(heads):
        column[:, head : head + 1] = jnp.sum(
            att_ref[head] * grads[head, mine, :].astype(f32), axis=1, keepdims=True
        )
    deltas = column[...].T
    for head in range(heads):
        query = queries[head, mine, :]
        grad = grads[head, mine, :]
        lse = lse_ref[head : head + 1, :]
        delta = deltas[head : head + 1, :]
        turned_grad = jnp.zeros((turned.shape[1], block), f32)
        for start in range(0, total, chunk):
            part = slice(start, start + chunk)
            scores = dot(keys[head, part, :], query, NT)
            grad_probs = dot(vals[head, part, :], grad, NT)
            probs = jnp.exp2(scores * FACTOR2 - lse)
            grad_scores = (probs * (grad_probs - delta)).astype(bf16)
            dv[head, part, :] += dot(probs.astype(bf16), grad)
            dk[head, part, :] += dot(grad_scores, query)
            turned_grad += dot(turned[head, :, part], grad_scores)
        dq[head, mine, :] = (turned_grad.T[:, :HEAD_DIM] * FACTOR).astype(bf16)

    @pl.when(index == pl.num_programs(0) - 1)
    def _():
        for number, ref in enumerate(outs):
            count = ref.shape[0]
            rows = slice(number * count, (number + 1) * count)
            ref[...] = jnp.zeros_like(ref)
            for head in range(heads):
                low = head * HEAD_DIM
                if number < own:
                    ref[:, low : low + HEAD_DIM] = dq[head, rows]
                ref[:, edge + low : edge + low + HEAD_DIM] = (dk[head, rows] * FACTOR).astype(bf16)
                ref[:, 2 * edge + low : 2 * edge + low + HEAD_DIM] = dv[head, rows].astype(bf16)


def attend_back(pieces, own, grads, att, lse, heads):
    count, width = pieces[0].shape
    rows, total = own * count, len(pieces) * count
    block = min(256, rows)
    edge = heads * HEAD_DIM
    slots = lse.shape[0]
    return pl.pallas_call(
        partial(attend_back_kernel, heads, min(512, total), len(pieces), own),
        grid=(rows // block,),
        in_specs=[whole_block((count, width))] * len(pieces)
        + [whole_block((count, edge))] * own
        + [
            pl.BlockSpec((heads, block, HEAD_DIM), lambda i: (0, i, 0)),
            pl.BlockSpec((slots, block), lambda i: (0, i)),
        ],
        out_specs=[whole_block((count, width))] * len(pieces),
        out_shape=[jax.ShapeDtypeStruct((count, width), bf16)] * len(pieces),
        scratch_shapes=[
            pltpu.VMEM((heads, rows, HEAD_DIM), bf16),
            pltpu.VMEM((heads, total, HEAD_DIM), bf16),
            pltpu.VMEM((heads, total, HEAD_DIM), bf16),
            pltpu.VMEM((heads, rows, HEAD_DIM), bf16),
            pltpu.VMEM((heads, LANES, total), bf16),
            pltpu.VMEM((heads, rows, HEAD_DIM), bf16),
            pltpu.VMEM((heads, total, HEAD_DIM), f32),
            pltpu.VMEM((heads, total, HEAD_DIM), f32),
            pltpu.VMEM((block, LANES), f32),
        ],
        compiler_params=pltpu.CompilerParams(vmem_limit_bytes=VMEM_LIMIT),
    )(*pieces, *grads, att, lse)


def cross_kernel(q_ref, k_ref, v_ref, out_ref):
    for low in range(0, q_ref.shape[1], HEAD_DIM):
        part = slice(low, low + HEAD_DIM)
        scores = dot(q_ref[:, part], k_ref[:, part], NT) * FACTOR
        weights = jnp.exp(scores - jnp.max(scores, axis=1, keepdims=True))
        probs = weights / jnp.sum(weights, axis=1, keepdims=True)
        out_ref[:, part] = dot(probs.astype(bf16), v_ref[:, part]).astype(bf16)


def cross(queries, keys, values):
    rows, width = queries.shape
    texts = keys.shape[0]
    block = min(512, rows)
    return pl.pallas_call(
        cross_kernel,
        grid=(rows // block,),
        in_specs=[
            pl.BlockSpec((block, width), lambda i: (i, 0)),
            pl.BlockSpec((texts, width), lambda i: (0, 0)),
            pl.BlockSpec((texts, width), lambda i: (0, 0)),
        ],
        out_specs=pl.BlockSpec((block, width), lambda i: (i, 0)),
        out_shape=jax.ShapeDtypeStruct((rows, width), bf16),
        compiler_params=pltpu.CompilerParams(vmem_limit_bytes=VMEM_LIMIT),
    )(queries, keys, values)


def cross_back_kernel(q_ref, k_ref, v_ref, grad_ref, dq_ref, dk_ref, dv_ref, dk, dv):
    @pl.when(pl.program_id(0) == 0)
    def _():
        dk[...] = jnp.zeros_like(dk)
        dv[...] = jnp.zeros_like(dv)

    for low in range(0, q_ref.shape[1], HEAD_DIM):
        part = slice(low, low + HEAD_DIM)
        query = q_ref[:, part]
        key = k_ref[:, part]
        grad = grad_ref[:, part]
        scores = dot(query, key, NT) * FACTOR
        weights = jnp.exp(scores - jnp.max(scores, axis=1, keepdims=True))
        probs = weights / jnp.sum(weights, axis=1, keepdims=True)
        grad_probs = dot(grad, v_ref[:, part], NT)
        delta = jnp.sum(probs * grad_probs, axis=1, keepdims=True)
        grad_scores = (probs * (grad_probs - delta)).astype(bf16)
        dq_ref[:, part] = (dot(grad_scores, key) * FACTOR).astype(bf16)
        dk[:, part] += dot(grad_scores, query, TN)
        dv[:, part] += dot(probs.astype(bf16), grad, TN)

    @pl.when(pl.program_id(0) == pl.num_programs(0) - 1)
    def _():
        dk_ref[...] = (dk[...] * FACTOR).astype(bf16)
        dv_ref[...] = dv[...].astype(bf16)


def cross_back(queries, keys, values, grad):
    rows, width = queries.shape
    texts = keys.shape[0]
    block = min(512, rows)
    whole = pl.BlockSpec((texts, width), lambda i: (0, 0))
    split = pl.BlockSpec((block, width), lambda i: (i, 0))
    return pl.pallas_call(
        cross_back_kernel,
        grid=(rows // block,),
        in_specs=[split, whole, whole, split],
        out_specs=[split, whole, whole],
        out_shape=[
            jax.ShapeDtypeStruct((rows, width), bf16),
            jax.ShapeDtypeStruct((texts, width), bf16),
            jax.ShapeDtypeStruct((texts, width), bf16),
        ],
        scratch_shapes=[pltpu.VMEM((texts, width), f32), pltpu.VMEM((texts, width), f32)],
        compiler_params=pltpu.CompilerParams(vmem_limit_bytes=VMEM_LIMIT),
    )(queries, keys, values, grad)


def gather(stack):
    pieces, _, columns = stack.shape
    own = lax.all_gather(stack, CHIPS, axis=1, tiled=True)
    own = own.reshape(pieces, lax.axis_size("tensor"), -1, columns)
    return own, send_xor(own, "fsdp", 1)


def join(own, other):
    core = lax.axis_index("fsdp")
    place = own.ndim - 2
    shape = own.shape[:place] + (2,) + own.shape[place:]
    both = jnp.zeros(shape, own.dtype)
    both = lax.dynamic_update_index_in_dim(both, own, core, place)
    both = lax.dynamic_update_index_in_dim(both, other, 1 - core, place)
    return both.reshape(own.shape[:place] + (2 * own.shape[place],) + own.shape[place + 1 :])


def core_halves(values):
    half = values.shape[1] // 2
    first = lax.axis_index("fsdp") == 0
    left, right = values[:, :half], values[:, half:]
    return jnp.where(first, left, right), jnp.where(first, right, left)


def weight_grad(halves, right):
    own, other = halves
    sent = jnp.einsum("sd,ste->tde", other, right, preferred_element_type=f32).astype(bf16)
    arrived = send_xor(sent, "fsdp", 1)
    kept = jnp.einsum("sd,ste->tde", own, right, preferred_element_type=f32)
    return (kept + arrived.astype(f32)).astype(bf16)


def scatter(pieces, offsets, columns):
    splits, half, _ = pieces[0].shape
    pack = jnp.zeros((splits * half, columns), bf16)
    for piece, offset in zip(pieces, offsets):
        pack = lax.dynamic_update_slice(pack, piece.reshape(splits * half, -1), (0, offset))
    return pack


def chip_sum(pack):
    return lax.psum_scatter(pack, CHIPS, scatter_dimension=0, tiled=True).astype(f32)


def local(
    latents, text, time_vector, table, w_qkv, w_out, w_cq, w_ckv, w_co, w_up, w_down, cotangent
):
    width = latents.shape[2]
    share = w_cq.shape[0]
    part = w_cq.shape[1]
    inner_part = w_up.shape[1]
    splits = lax.axis_size("tensor")
    ranks = lax.axis_size("hr")
    halves = lax.axis_size("sr")
    edge = part // ranks
    heads = edge // HEAD_DIM
    groups = ranks * splits
    piece_width = -(-(3 * edge + 6) // LANES) * LANES
    texts = text.shape[1]
    slot = lax.axis_index("lat")
    member = lax.axis_index(HEAD_GROUP)

    shard_qkv = jnp.transpose(w_qkv.reshape(share, 3, ranks, edge), (2, 0, 1, 3)).reshape(
        ranks, share, 3 * edge
    )
    table_part = jnp.zeros((ranks, share, piece_width - 3 * edge), bf16).at[:, :, :6].set(table.T)
    halves_one = gather(jnp.concatenate((shard_qkv, table_part), axis=2))
    residual = jnp.concatenate(exchange(partial(pick, latents), "lat"), axis=0).astype(f32)
    halves_mid = gather(jnp.stack((w_ckv[:, 0], w_ckv[:, 1], w_cq, w_co.T, w_out.T)))
    halves_two = gather(jnp.stack((w_up, w_down.T)))
    table_full = join(*(half[0, 0, :, 3 * edge : 3 * edge + 6] for half in halves_one))
    halves_one = [half.reshape(groups, width // 2, piece_width) for half in halves_one]
    qkv_full = [
        join(*(pick(half, jnp.bitwise_xor(member, step)) for half in halves_one))
        for step in range(groups)
    ]
    key_full, val_full, cq_full, co_full, out_full = (
        join(*(half[row] for half in halves_mid)) for row in range(5)
    )
    up_full, down_full = (join(*(half[row] for half in halves_two)) for row in range(2))

    grad_three = jnp.concatenate(exchange(partial(pick, cotangent), "lat"), axis=0).astype(f32)
    rows = residual.shape[0]
    caption = pick(text, slot)

    modulate = table_full.T.astype(f32) + pick(time_vector, slot).astype(f32).reshape(6, width)
    shift_one, scale_one, gate_one, shift_two, scale_two, gate_two = (
        modulate[row : row + 1] for row in range(6)
    )

    normed_one, inverse_one = norm_parts(residual)
    hidden_one = (normed_one * (1.0 + scale_one) + shift_one).astype(bf16)
    mixed = []
    for step in range(groups):
        piece = dot(hidden_one, qkv_full[step]).astype(bf16)
        mixed.append(send_xor(piece, HEAD_GROUP, step) if step else piece)
    for step in range(1, halves):
        mixed += [send_xor(piece, "sr", step) for piece in mixed[:groups]]
    att_low, att_wide, logsum = attend(mixed, groups, heads)
    att_back = in_order(give_back(att_low, HEAD_GROUP), HEAD_GROUP)
    att = jnp.transpose(att_back.reshape(ranks, splits, rows, edge), (2, 1, 0, 3)).reshape(
        rows, splits, part
    )

    out_one = jnp.einsum("ste,tde->sd", att, out_full, preferred_element_type=f32)
    after_one = residual + gate_one * out_one
    mid_low = after_one.astype(bf16)
    cross_q = (
        jnp.einsum("sd,tde->ste", mid_low, cq_full, preferred_element_type=f32)
        .astype(bf16)
        .reshape(rows, width)
    )
    cross_k = (
        jnp.einsum("sd,tde->ste", caption, key_full, preferred_element_type=f32)
        .astype(bf16)
        .reshape(texts, width)
    )
    cross_v = (
        jnp.einsum("sd,tde->ste", caption, val_full, preferred_element_type=f32)
        .astype(bf16)
        .reshape(texts, width)
    )
    cross_low = cross(cross_q, cross_k, cross_v)
    cross_split = cross_low.reshape(rows, splits, part)
    out_two = jnp.einsum("ste,tde->sd", cross_split, co_full, preferred_element_type=f32)
    after_two = after_one + out_two
    normed_two, inverse_two = norm_parts(after_two)
    hidden_two = (normed_two * (1.0 + scale_two) + shift_two).astype(bf16)
    inner = [dot(hidden_two, up_full[split]) for split in range(splits)]
    active = [jax.nn.gelu(values, approximate=True).astype(bf16) for values in inner]
    out_three = sum(dot(active[split], down_full[split], NT) for split in range(splits))
    result = (after_two + gate_two * out_three).astype(bf16)
    result_back = in_order(give_back(list(result.reshape(latents.shape)), "lat"), "lat")

    grad_gate_two = jnp.sum(grad_three * out_three, axis=0)
    grad_z = (gate_two * grad_three).astype(bf16)
    grad_inner = []
    for split in range(splits):
        grad_active = dot(grad_z, down_full[split])
        _, pull = jax.vjp(partial(jax.nn.gelu, approximate=True), inner[split])
        grad_inner.append(pull(grad_active)[0].astype(bf16))
    down_grad = weight_grad(core_halves(grad_z), jnp.stack(active, axis=1))
    up_grad = weight_grad(core_halves(hidden_two), jnp.stack(grad_inner, axis=1))
    pack_two = scatter((up_grad, down_grad), (0, inner_part), 2 * inner_part)
    grad_hidden_two = sum(dot(grad_inner[split], up_full[split], NT) for split in range(splits))
    grad_shift_two = jnp.sum(grad_hidden_two, axis=0)
    grad_scale_two = jnp.sum(grad_hidden_two * normed_two, axis=0)
    grad_two = grad_three + norm_back(grad_hidden_two * (1.0 + scale_two), normed_two, inverse_two)

    grad_out_two = grad_two.astype(bf16)
    grad_cross = (
        jnp.einsum("sd,tde->ste", grad_out_two, co_full, preferred_element_type=f32)
        .astype(bf16)
        .reshape(rows, width)
    )
    grad_cross, pack_two = tie(grad_cross, pack_two)
    sum_two = chip_sum(pack_two)
    grad_cq, grad_ck, grad_cv = cross_back(cross_q, cross_k, cross_v, grad_cross)
    grad_cq = grad_cq.reshape(rows, splits, part)
    grad_ck = grad_ck.reshape(texts, splits, part)
    grad_cv = grad_cv.reshape(texts, splits, part)
    grad_one = grad_two + jnp.einsum("ste,tde->sd", grad_cq, cq_full, preferred_element_type=f32)
    text_terms = jnp.einsum(
        "ste,tde->sd", grad_ck, key_full, preferred_element_type=f32
    ) + jnp.einsum("ste,tde->sd", grad_cv, val_full, preferred_element_type=f32)

    grad_gate_one = jnp.sum(grad_one * out_one, axis=0)
    grad_out_one = (gate_one * grad_one).astype(bf16)
    grad_att = jnp.einsum("sd,tde->ste", grad_out_one, out_full, preferred_element_type=f32)
    grad_att = jnp.transpose(
        grad_att.astype(bf16).reshape(rows, splits, ranks, edge), (2, 1, 0, 3)
    ).reshape(groups, rows, edge)
    grad_heads = exchange(partial(pick, grad_att), HEAD_GROUP)
    caption_halves = core_halves(caption)
    mid_grads = (
        weight_grad(caption_halves, jnp.concatenate((grad_ck, grad_cv), axis=2)),
        weight_grad(core_halves(mid_low), grad_cq),
        weight_grad(core_halves(grad_out_two), cross_split),
        weight_grad(core_halves(grad_out_one), att),
    )
    step_mid = -(-part // LANES) * LANES
    step_pair = -(-2 * part // LANES) * LANES
    offsets_mid = [step_pair * (place > 0) + step_mid * max(place - 1, 0) for place in range(4)]
    columns_mid = -(-(step_pair + 3 * step_mid) // (2 * LANES)) * 2 * LANES
    pack_mid = scatter(mid_grads, offsets_mid, columns_mid)
    grad_heads[0], pack_mid = tie(grad_heads[0], pack_mid)
    sum_mid = chip_sum(pack_mid)
    grad_mix = attend_back(mixed, groups, grad_heads, att_wide, logsum, heads)
    for step in range(1, halves):
        for place in range(groups):
            more = send_xor(grad_mix[step * groups + place], "sr", step)
            grad_mix[place] = (grad_mix[place].astype(f32) + more.astype(f32)).astype(bf16)
    grad_proj = give_back(grad_mix[:groups], HEAD_GROUP)
    grad_hidden_one = sum(dot(grad_proj[step], qkv_full[step], NT) for step in range(groups))
    grad_shift_one = jnp.sum(grad_hidden_one, axis=0)
    grad_scale_one = jnp.sum(grad_hidden_one * normed_one, axis=0)
    grad_latents = grad_one + norm_back(
        grad_hidden_one * (1.0 + scale_one), normed_one, inverse_one
    )
    grad_latents = grad_latents.astype(bf16).reshape(latents.shape)
    grad_latents = in_order(give_back(list(grad_latents), "lat"), "lat")

    time_terms = jnp.stack(
        (
            grad_shift_one,
            grad_scale_one,
            grad_gate_one,
            grad_shift_two,
            grad_scale_two,
            grad_gate_two,
        )
    )
    table_own, table_other = core_halves(time_terms)
    table_own += send_xor(table_other, "fsdp", 1)
    one_grads = [
        weight_grad(core_halves(hidden_one), piece[:, None, :])[0] for piece in grad_proj
    ]
    pack_one = jnp.zeros((splits, width // 2, ranks, piece_width), bf16)
    for step, piece in enumerate(one_grads):
        owner = jnp.bitwise_xor(member, step)
        pack_one = lax.dynamic_update_slice(
            pack_one,
            piece[None, :, None],
            (lax.rem(owner, splits), 0, lax.div(owner, splits), 0),
        )
    table_terms = jnp.broadcast_to(table_own.T.astype(bf16), (splits, width // 2, 6))
    pack_one = lax.dynamic_update_slice(pack_one, table_terms[:, :, None], (0, 0, 0, 3 * edge))
    sum_one = chip_sum(pack_one.reshape(splits * width // 2, ranks * piece_width))
    sum_one = sum_one.reshape(share, ranks, piece_width)
    grad_time = over_latents(plane_sum(time_terms, f32)).reshape(-1, 6 * width)
    grad_text = over_latents(plane_sum(text_terms, bf16).astype(bf16)).astype(f32)
    grad_qkv = jnp.transpose(
        sum_one[:, :, : 3 * edge].reshape(share, ranks, 3, edge), (0, 2, 1, 3)
    ).reshape(share, 3, part)
    pair, cq_sum, co_sum, out_sum = (
        sum_mid[:, offset : offset + (part if place else 2 * part)]
        for place, offset in enumerate(offsets_mid)
    )
    return (
        result_back,
        grad_latents.astype(f32),
        grad_text,
        grad_time,
        sum_one[:, 0, 3 * edge : 3 * edge + 6].T,
        grad_qkv,
        out_sum.T,
        cq_sum,
        pair.reshape(share, 2, part),
        co_sum.T,
        sum_two[:, :inner_part],
        sum_two[:, inner_part:].T,
    )


def solution(mesh):
    def run(latents, text, time_vector, table, w_qkv, *others):
        fsdp, context, tensor = (mesh.shape[name] for name in ("fsdp", "context", "tensor"))
        lat = latents.shape[0] // fsdp
        group = context // lat
        ranks = math.gcd(group, w_qkv.shape[2] // (tensor * HEAD_DIM))
        sizes = (fsdp, lat, group // ranks, ranks, tensor)
        finer = Mesh(mesh.devices.reshape(sizes), ("fsdp", "lat", "sr", "hr", "tensor"))
        line = ("lat", "sr", "hr")
        shard = ("fsdp",) + line
        tokens = P("fsdp", line + ("tensor",), None)
        by_row = P(shard, "tensor")
        by_row3 = P(shard, None, "tensor")
        by_column = P("tensor", shard)
        weights = (by_row3, by_column, by_row, by_row3, by_column, by_row, by_column)
        return jax.shard_map(
            local,
            mesh=finer,
            in_specs=(tokens, P("fsdp", None, None), P("fsdp", None), P(None, shard))
            + weights
            + (tokens,),
            out_specs=(tokens, tokens, P("fsdp", None, None), P("fsdp", None), P(None, shard))
            + weights,
            check_vma=False,
        )(latents, text, time_vector, table, w_qkv, *others)

    return run
```

```python
import math
from functools import partial

import jax
import jax.numpy as jnp
from jax import lax
from jax.experimental import pallas as pl
from jax.experimental.pallas import tpu as pltpu
from jax.sharding import Mesh
from jax.sharding import PartitionSpec as P

HEAD_DIM = 72
EPSILON = 1e-06
LANES = 128
FACTOR = HEAD_DIM ** (-0.5)
FACTOR2 = FACTOR * math.log2(math.e)
VMEM_LIMIT = 56 * 1024 * 1024

f32 = jnp.float32
bf16 = jnp.bfloat16

NT = (((1,), (1,)), ((), ()))
NN = (((1,), (0,)), ((), ()))
TN = (((0,), (0,)), ((), ()))

ROW = ("sr", "hr")
PLANE = ("sr", "hr", "tensor")
HEAD_GROUP = ("hr", "tensor")


def dot(left, right, dims=NN):
    return lax.dot_general(left, right, dims, preferred_element_type=f32)


def norm_parts(values):
    center = values - jnp.mean(values, axis=-1, keepdims=True)
    inverse = lax.rsqrt(jnp.mean(center * center, axis=-1, keepdims=True) + EPSILON)
    return (center * inverse, inverse)


def norm_back(grad_hat, normed, inverse):
    first = jnp.mean(grad_hat, axis=-1, keepdims=True)
    second = jnp.mean(grad_hat * normed, axis=-1, keepdims=True)
    return inverse * (grad_hat - first - normed * second)


def send_xor(piece, axes, step):
    size = lax.axis_size(axes)
    return lax.ppermute(piece, axes, [(rank, rank ^ step) for rank in range(size)])


def pick(stack, index):
    return lax.dynamic_index_in_dim(stack, index, 0, keepdims=False)


def exchange(piece_for, axes):
    me = lax.axis_index(axes)
    got = [piece_for(me)]
    for step in range(1, lax.axis_size(axes)):
        got.append(send_xor(piece_for(jnp.bitwise_xor(me, step)), axes, step))
    return got


def give_back(pieces, axes):
    return [send_xor(piece, axes, step) if step else piece for step, piece in enumerate(pieces)]


def in_order(pieces, axes):
    me = lax.axis_index(axes)
    places = range(len(pieces))
    return jnp.stack([choose(pieces, jnp.bitwise_xor(me, place)) for place in places])


def choose(pieces, index):
    out = pieces[0]
    for place in range(1, len(pieces)):
        out = jnp.where(index == place, pieces[place], out)
    return out


def plane_sum(values, dtype):
    sent = values.astype(dtype)
    total = sent.astype(f32)
    for step in range(1, lax.axis_size(PLANE)):
        total += send_xor(sent, PLANE, step).astype(f32)
    return total


def over_latents(values):
    return in_order(give_back([values] * lax.axis_size("lat"), "lat"), "lat")


def tie(first, second):
    return lax.optimization_barrier((first, second))


def attend_kernel(heads, chunks, own, *refs):
    pieces = refs[:chunks]
    low_refs = refs[chunks : chunks + own]
    att_ref, lse_ref, queries, keys, vals, lows, column = refs[chunks + own :]
    edge = heads * HEAD_DIM
    index = pl.program_id(0)
    block = att_ref.shape[1]

    @pl.when(index == 0)
    def _():
        lane = lax.broadcasted_iota(jnp.int32, vals.shape[1:], 1)
        column[...] = jnp.zeros_like(column)
        for head in range(heads):
            vals[head] = jnp.where(lane == HEAD_DIM, 1.0, 0.0).astype(bf16)
            low = head * HEAD_DIM
            for number, piece in enumerate(pieces):
                count = piece.shape[0]
                rows = slice(number * count, (number + 1) * count)
                if number < own:
                    queries[head, rows] = piece[:, low : low + HEAD_DIM]
                keys[head, rows] = piece[:, edge + low : edge + low + HEAD_DIM]
                vals[head, rows, :HEAD_DIM] = piece[:, 2 * edge + low : 2 * edge + low + HEAD_DIM]

    mine = pl.ds(pl.multiple_of(index * block, block), block)

    def score(head):
        return dot(queries[head, mine, :], keys[head], NT)

    ahead = score(0)
    for head in range(heads):
        scores = ahead
        if head + 1 < heads:
            ahead = score(head + 1)
        top = jnp.max(scores, axis=1, keepdims=True) * FACTOR2
        weights = jnp.exp2(scores * FACTOR2 - top).astype(bf16)
        out = dot(weights, vals[head])
        total = out[:, HEAD_DIM : HEAD_DIM + 1]
        out = out[:, :HEAD_DIM] / total
        att_ref[head] = out
        lows[head, mine, :] = out.astype(bf16)
        column[:, head : head + 1] = top + jnp.log2(total)
    lse_ref[...] = column[...].T[: lse_ref.shape[0]]

    @pl.when(index == pl.num_programs(0) - 1)
    def _():
        for head in range(heads):
            low = head * HEAD_DIM
            for number, ref in enumerate(low_refs):
                count = ref.shape[0]
                ref[:, low : low + HEAD_DIM] = lows[head, number * count : (number + 1) * count, :]


def whole_block(shape):
    return pl.BlockSpec(shape, lambda i: (0,) * len(shape))


def attend(pieces, own, heads):
    count, width = pieces[0].shape
    rows, total = own * count, len(pieces) * count
    block = min(256, rows)
    edge = heads * HEAD_DIM
    slots = -(-heads // 8) * 8
    out = pl.pallas_call(
        partial(attend_kernel, heads, len(pieces), own),
        grid=(rows // block,),
        in_specs=[whole_block((count, width))] * len(pieces),
        out_specs=[whole_block((count, edge))] * own
        + [
            pl.BlockSpec((heads, block, HEAD_DIM), lambda i: (0, i, 0)),
            pl.BlockSpec((slots, block), lambda i: (0, i)),
        ],
        out_shape=[jax.ShapeDtypeStruct((count, edge), bf16)] * own
        + [
            jax.ShapeDtypeStruct((heads, rows, HEAD_DIM), f32),
            jax.ShapeDtypeStruct((slots, rows), f32),
        ],
        scratch_shapes=[
            pltpu.VMEM((heads, rows, HEAD_DIM), bf16),
            pltpu.VMEM((heads, total, HEAD_DIM), bf16),
            pltpu.VMEM((heads, total, LANES), bf16),
            pltpu.VMEM((heads, rows, HEAD_DIM), bf16),
            pltpu.VMEM((block, LANES), f32),
        ],
        cost_estimate=pl.CostEstimate(
            flops=8 * heads * rows * total * LANES,
            transcendentals=heads * rows * total,
            bytes_accessed=4 * total * width,
        ),
        compiler_params=pltpu.CompilerParams(vmem_limit_bytes=VMEM_LIMIT),
    )(*pieces)
    return (out[:own], out[own], out[own + 1])


def attend_back_kernel(heads, chunk, chunks, own, *refs):
    pieces = refs[:chunks]
    grad_refs = refs[chunks : chunks + own]
    att_ref, lse_ref = refs[chunks + own : chunks + own + 2]
    outs = refs[chunks + own + 2 : 2 * chunks + own + 2]
    queries, keys, vals, grads, turned, dq, dk, dv, column = refs[2 * chunks + own + 2 :]
    edge = heads * HEAD_DIM
    index = pl.program_id(0)
    block = att_ref.shape[1]
    total = keys.shape[1]

    @pl.when(index == 0)
    def _():
        turned[...] = jnp.zeros_like(turned)
        column[...] = jnp.zeros_like(column)
        dk[...] = jnp.zeros_like(dk)
        dv[...] = jnp.zeros_like(dv)
        for head in range(heads):
            low = head * HEAD_DIM
            for number, piece in enumerate(pieces):
                count = piece.shape[0]
                rows = slice(number * count, (number + 1) * count)
                if number < own:
                    queries[head, rows] = piece[:, low : low + HEAD_DIM]
                    grads[head, rows] = grad_refs[number][:, low : low + HEAD_DIM]
                key = piece[:, edge + low : edge + low + HEAD_DIM]
                keys[head, rows] = key
                turned[head, :HEAD_DIM, rows] = key.astype(f32).T.astype(bf16)
                vals[head, rows] = piece[:, 2 * edge + low : 2 * edge + low + HEAD_DIM]

    mine = pl.ds(pl.multiple_of(index * block, block), block)
    for head in range(heads):
        column[:, head : head + 1] = jnp.sum(
            att_ref[head] * grads[head, mine, :].astype(f32), axis=1, keepdims=True
        )
    deltas = column[...].T
    for head in range(heads):
        query = queries[head, mine, :]
        grad = grads[head, mine, :]
        lse = lse_ref[head : head + 1, :]
        delta = deltas[head : head + 1, :]
        turned_grad = jnp.zeros((turned.shape[1], block), f32)
        for start in range(0, total, chunk):
            part = slice(start, start + chunk)
            scores = dot(keys[head, part, :], query, NT)
            grad_probs = dot(vals[head, part, :], grad, NT)
            probs = jnp.exp2(scores * FACTOR2 - lse)
            grad_scores = (probs * (grad_probs - delta)).astype(bf16)
            dv[head, part, :] += dot(probs.astype(bf16), grad)
            dk[head, part, :] += dot(grad_scores, query)
            turned_grad += dot(turned[head, :, part], grad_scores)
        dq[head, mine, :] = (turned_grad.T[:, :HEAD_DIM] * FACTOR).astype(bf16)

    @pl.when(index == pl.num_programs(0) - 1)
    def _():
        for number, ref in enumerate(outs):
            count = ref.shape[0]
            rows = slice(number * count, (number + 1) * count)
            ref[...] = jnp.zeros_like(ref)
            for head in range(heads):
                low = head * HEAD_DIM
                if number < own:
                    ref[:, low : low + HEAD_DIM] = dq[head, rows]
                ref[:, edge + low : edge + low + HEAD_DIM] = (dk[head, rows] * FACTOR).astype(bf16)
                ref[:, 2 * edge + low : 2 * edge + low + HEAD_DIM] = dv[head, rows].astype(bf16)


def attend_back(pieces, own, grads, att, lse, heads):
    count, width = pieces[0].shape
    rows, total = own * count, len(pieces) * count
    block = min(256, rows)
    edge = heads * HEAD_DIM
    slots = lse.shape[0]
    return pl.pallas_call(
        partial(attend_back_kernel, heads, min(512, total), len(pieces), own),
        grid=(rows // block,),
        in_specs=[whole_block((count, width))] * len(pieces)
        + [whole_block((count, edge))] * own
        + [
            pl.BlockSpec((heads, block, HEAD_DIM), lambda i: (0, i, 0)),
            pl.BlockSpec((slots, block), lambda i: (0, i)),
        ],
        out_specs=[whole_block((count, width))] * len(pieces),
        out_shape=[jax.ShapeDtypeStruct((count, width), bf16)] * len(pieces),
        scratch_shapes=[
            pltpu.VMEM((heads, rows, HEAD_DIM), bf16),
            pltpu.VMEM((heads, total, HEAD_DIM), bf16),
            pltpu.VMEM((heads, total, HEAD_DIM), bf16),
            pltpu.VMEM((heads, rows, HEAD_DIM), bf16),
            pltpu.VMEM((heads, LANES, total), bf16),
            pltpu.VMEM((heads, rows, HEAD_DIM), bf16),
            pltpu.VMEM((heads, total, HEAD_DIM), f32),
            pltpu.VMEM((heads, total, HEAD_DIM), f32),
            pltpu.VMEM((block, LANES), f32),
        ],
        cost_estimate=pl.CostEstimate(
            flops=20 * heads * rows * total * LANES,
            transcendentals=heads * rows * total,
            bytes_accessed=8 * total * width,
        ),
        compiler_params=pltpu.CompilerParams(vmem_limit_bytes=VMEM_LIMIT),
    )(*pieces, *grads, att, lse)


def head_lanes(part):
    return [slice(low, low + HEAD_DIM) for low in range(0, part, HEAD_DIM)]


def cross_kernel(part, splits, *refs):
    q_refs, k_refs, v_refs, out_refs = (refs[splits * i : splits * (i + 1)] for i in range(4))
    for q_ref, k_ref, v_ref, out_ref in zip(q_refs, k_refs, v_refs, out_refs):
        fill = out_ref.shape[1] - part
        if fill:
            out_ref[:, part:] = jnp.zeros((out_ref.shape[0], fill), bf16)
        for lanes in head_lanes(part):
            scores = dot(q_ref[:, lanes], k_ref[:, lanes], NT) * FACTOR
            weights = jnp.exp(scores - jnp.max(scores, axis=1, keepdims=True))
            probs = weights / jnp.sum(weights, axis=1, keepdims=True)
            out_ref[:, lanes] = dot(probs.astype(bf16), v_ref[:, lanes]).astype(bf16)


def cross(queries, keys, values, part):
    splits = len(queries)
    rows, width = queries[0].shape
    texts = keys[0].shape[0]
    block = min(512, rows)
    split = pl.BlockSpec((block, width), lambda i: (i, 0))
    return pl.pallas_call(
        partial(cross_kernel, part, splits),
        grid=(rows // block,),
        in_specs=[split] * splits + [whole_block((texts, width))] * (2 * splits),
        out_specs=[split] * splits,
        out_shape=[jax.ShapeDtypeStruct((rows, width), bf16)] * splits,
        compiler_params=pltpu.CompilerParams(vmem_limit_bytes=VMEM_LIMIT),
    )(*queries, *keys, *values)


def cross_back_kernel(part, splits, *refs):
    q_refs, k_refs, v_refs, grad_refs, dq_refs, dk_refs, dv_refs, dk_sums, dv_sums = (
        refs[splits * i : splits * (i + 1)] for i in range(9)
    )
    first = pl.program_id(0) == 0
    last = pl.program_id(0) == pl.num_programs(0) - 1
    for q_ref, k_ref, v_ref, grad_ref, dq_ref, dk, dv in zip(
        q_refs, k_refs, v_refs, grad_refs, dq_refs, dk_sums, dv_sums
    ):

        @pl.when(first)
        def _():
            dk[...] = jnp.zeros_like(dk)
            dv[...] = jnp.zeros_like(dv)

        fill = dq_ref.shape[1] - part
        if fill:
            dq_ref[:, part:] = jnp.zeros((dq_ref.shape[0], fill), bf16)
        for lanes in head_lanes(part):
            query = q_ref[:, lanes]
            key = k_ref[:, lanes]
            grad = grad_ref[:, lanes]
            scores = dot(query, key, NT) * FACTOR
            weights = jnp.exp(scores - jnp.max(scores, axis=1, keepdims=True))
            probs = weights / jnp.sum(weights, axis=1, keepdims=True)
            grad_probs = dot(grad, v_ref[:, lanes], NT)
            delta = jnp.sum(probs * grad_probs, axis=1, keepdims=True)
            grad_scores = (probs * (grad_probs - delta)).astype(bf16)
            dq_ref[:, lanes] = (dot(grad_scores, key) * FACTOR).astype(bf16)
            dk[:, lanes] += dot(grad_scores, query, TN)
            dv[:, lanes] += dot(probs.astype(bf16), grad, TN)

    @pl.when(last)
    def _():
        for dk_ref, dv_ref, dk, dv in zip(dk_refs, dv_refs, dk_sums, dv_sums):
            dk_ref[...] = (dk[...] * FACTOR).astype(bf16)
            dv_ref[...] = dv[...].astype(bf16)


def cross_back(queries, keys, values, grads, part):
    splits = len(queries)
    rows, width = queries[0].shape
    texts = keys[0].shape[0]
    block = min(512, rows)
    whole = whole_block((texts, width))
    split = pl.BlockSpec((block, width), lambda i: (i, 0))
    out = pl.pallas_call(
        partial(cross_back_kernel, part, splits),
        grid=(rows // block,),
        in_specs=[split] * splits + [whole] * (2 * splits) + [split] * splits,
        out_specs=[split] * splits + [whole] * (2 * splits),
        out_shape=[jax.ShapeDtypeStruct((rows, width), bf16)] * splits
        + [jax.ShapeDtypeStruct((texts, width), bf16)] * (2 * splits),
        scratch_shapes=[pltpu.VMEM((texts, width), f32)] * (2 * splits),
        compiler_params=pltpu.CompilerParams(vmem_limit_bytes=VMEM_LIMIT),
    )(*queries, *keys, *values, *grads)
    return (out[:splits], out[splits : 2 * splits], out[2 * splits :])


def assemble_kernel(plan, count, *refs):
    sources, (sems,) = refs[:count], refs[-1:]
    outs = refs[count:-1]
    copies = [
        pltpu.make_async_copy(
            sources[source].at[:, pl.ds(column, size)],
            outs[place].at[pl.ds(row, sources[source].shape[0]), :],
            sems.at[number],
        )
        for number, (source, column, size, place, row) in enumerate(plan)
    ]
    for copy in copies:
        copy.start()
    for copy in copies:
        copy.wait()


def assemble(stacks, columns):
    sources = [piece for stack in stacks for piece in stack]
    plan, shapes, base = [], [], 0
    for stack in stacks:
        offset = 0
        for size in columns:
            row = 0
            for number, piece in enumerate(stack):
                plan.append((base + number, offset, size, len(shapes), row))
                row += piece.shape[0]
            shapes.append(jax.ShapeDtypeStruct((row, size), piece.dtype))
            offset += size
        base += len(stack)
    anywhere = pl.BlockSpec(memory_space=pl.ANY)
    out = pl.pallas_call(
        partial(assemble_kernel, plan, len(sources)),
        in_specs=[anywhere] * len(sources),
        out_specs=[anywhere] * len(shapes),
        out_shape=shapes,
        scratch_shapes=[pltpu.SemaphoreType.DMA((len(plan),))],
    )(*sources)
    out = list(out)
    return [out[place : place + len(columns)] for place in range(0, len(out), len(columns))]


def with_others(piece, axes):
    return [piece] + [send_xor(piece, axes, step) for step in range(1, lax.axis_size(axes))]


def gather(shard, columns, tensor_first):
    start = jnp.concatenate(with_others(shard, "lat"))
    if tensor_first and lax.axis_size("tensor") * lax.axis_size(ROW) <= 8:
        stacks = [with_others(piece, ROW) for piece in with_others(start, "tensor")]
    else:
        half = assemble([with_others(start, ROW)], [start.shape[1]])[0][0]
        stacks = [[piece] for piece in with_others(half, "tensor")]
    stacks = [
        stack + [send_xor(piece, "fsdp", step) for step in range(1, lax.axis_size("fsdp")) for piece in stack]
        for stack in stacks
    ]
    return assemble(stacks, columns)


def kept_sums(left, rights, extra=None):
    cores = lax.axis_size("fsdp")
    half = left.shape[1] // cores
    out = []
    for right in rights:
        sums = []
        for core in range(cores):
            rows = slice(core * half, (core + 1) * half)
            total = dot(left[:, rows], right, TN)
            if extra is not None:
                total += extra[rows]
            sums.append(total)
        total = sums[0]
        for core in range(1, cores):
            total += send_xor(sums[core].astype(bf16), "fsdp", core).astype(f32)
        out.append(total.astype(bf16))
    return out


def sum_pieces(pieces, axes, dtype=bf16):
    total = pieces[0].astype(f32)
    for step in range(1, len(pieces)):
        total += send_xor(pieces[step], axes, step).astype(f32)
    return total.astype(dtype)


def row_blocks(piece, count):
    size = piece.shape[0] // count
    return [piece[place * size : (place + 1) * size] for place in range(count)]


def sum_tensor(parts):
    return [sum_pieces(parts, "tensor")]


def sum_row(parts):
    return [sum_pieces(row_blocks(part, lax.axis_size(ROW)), ROW) for part in parts]


def sum_lat(parts):
    return sum_pieces(row_blocks(parts[0], lax.axis_size("lat")), "lat", f32)


def own_order(share, width):
    cores, lats, rows = (lax.axis_size(axes) for axes in ("fsdp", "lat", ROW))
    place = lax.iota(jnp.int32, width)
    block, rest = place // share, place % share
    lat = jnp.bitwise_xor(block % lats, lax.axis_index("lat"))
    row = jnp.bitwise_xor(block // lats % rows, lax.axis_index(ROW))
    core = jnp.bitwise_xor(block // (lats * rows), lax.axis_index("fsdp"))
    natural = ((core * lats + lat) * rows + row) * share + rest
    return (lax.broadcasted_iota(jnp.int32, (width, width), 0) == natural[None, :]).astype(bf16)


def local(
    latents, text, time_vector, table, w_qkv, w_out, w_cq, w_ckv, w_co, w_up, w_down, cotangent
):
    width = latents.shape[2]
    share = w_cq.shape[0]
    part = w_cq.shape[1]
    inner_part = w_up.shape[1]
    splits = lax.axis_size("tensor")
    ranks = lax.axis_size("hr")
    halves = lax.axis_size("sr")
    edge = part // ranks
    heads = edge // HEAD_DIM
    groups = ranks * splits
    piece_width = -(-(3 * edge + 6) // LANES) * LANES
    wide = -(-part // LANES) * LANES
    slot = lax.axis_index("lat")
    rank = lax.axis_index("hr")

    def padded(values):
        return jnp.pad(values, ((0, 0), (0, wide - part)))

    latents_got = exchange(partial(pick, latents), "lat")
    shard_qkv = jnp.transpose(w_qkv.reshape(share, 3, ranks, edge), (2, 0, 1, 3)).reshape(
        ranks, share, 3 * edge
    )
    fill = jnp.pad(table.T, ((0, 0), (0, piece_width - 3 * edge - 6)))
    qkv_full = [
        gather(jnp.concatenate((shard_qkv[place], fill), axis=1), [piece_width], place % 2 == 0)
        for place in range(ranks)
    ]
    mid_shard = jnp.concatenate(
        [padded(piece) for piece in (w_out.T, w_ckv[:, 0], w_ckv[:, 1], w_cq, w_co.T)], axis=1
    )
    mid_shard, qkv_full[0][0][0] = tie(mid_shard, qkv_full[0][0][0])
    mid_full = gather(mid_shard, [wide] * 5, False)
    out_full, key_full, val_full, cq_full, co_full = (
        [full[place] for full in mid_full] for place in range(5)
    )
    up_shard, down_shard, out_full[0] = lax.optimization_barrier((w_up, w_down.T, out_full[0]))
    up_full = [full[0] for full in gather(up_shard, [inner_part], False)]
    down_full = [full[0] for full in gather(down_shard, [inner_part], True)]

    turn = own_order(share, width)
    residual = dot(jnp.concatenate(latents_got, axis=0), turn)
    grad_three = dot(jnp.concatenate(exchange(partial(pick, cotangent), "lat"), axis=0), turn)
    rows = residual.shape[0]
    caption = dot(pick(text, slot), turn).astype(bf16)
    table_full = qkv_full[0][0][0][:, 3 * edge : 3 * edge + 6]
    modulate = table_full.T.astype(f32) + dot(pick(time_vector, slot).reshape(6, width), turn)
    shift_one, scale_one, gate_one, shift_two, scale_two, gate_two = (
        modulate[row : row + 1] for row in range(6)
    )

    normed_one, inverse_one = norm_parts(residual)
    hidden_one = (normed_one * (1.0 + scale_one) + shift_one).astype(bf16)
    mixed = [None] * groups
    for split in range(splits):
        pieces = [dot(hidden_one, full[split][0]).astype(bf16) for full in qkv_full]
        for other in range(ranks):
            step = other * splits + split
            piece = choose(pieces, jnp.bitwise_xor(rank, other))
            mixed[step] = send_xor(piece, HEAD_GROUP, step) if step else piece
    for step in range(1, halves):
        mixed += [send_xor(piece, "sr", step) for piece in mixed[:groups]]
    att_low, att_wide, logsum = attend(mixed, groups, heads)

    def by_split(pieces, split):
        own = [pieces[other * splits + split] for other in range(ranks)]
        return [choose(own, jnp.bitwise_xor(rank, place)) for place in range(ranks)]

    att_back = give_back(att_low, HEAD_GROUP)
    att = [
        padded(jnp.concatenate(by_split(att_back, split), axis=1)) for split in range(splits)
    ]

    out_one = sum(dot(att[split], out_full[split], NT) for split in range(splits))
    after_one = residual + gate_one * out_one
    mid_low = after_one.astype(bf16)
    cross_q = [dot(mid_low, full).astype(bf16) for full in cq_full]
    cross_k = [dot(caption, full).astype(bf16) for full in key_full]
    cross_v = [dot(caption, full).astype(bf16) for full in val_full]
    cross_low = cross(cross_q, cross_k, cross_v, part)
    out_two = sum(dot(cross_low[split], co_full[split], NT) for split in range(splits))
    after_two = after_one + out_two
    normed_two, inverse_two = norm_parts(after_two)
    hidden_two = (normed_two * (1.0 + scale_two) + shift_two).astype(bf16)
    inner = [dot(hidden_two, up_full[split]) for split in range(splits)]
    active = [jax.nn.gelu(values, approximate=True).astype(bf16) for values in inner]
    out_three = sum(dot(active[split], down_full[split], NT) for split in range(splits))
    result = dot((after_two + gate_two * out_three).astype(bf16), turn, NT).astype(bf16)
    result_back = in_order(give_back(list(result.reshape(latents.shape)), "lat"), "lat")

    grad_gate_two = jnp.sum(grad_three * out_three, axis=0)
    grad_z = (gate_two * grad_three).astype(bf16)
    grad_inner = []
    for split in range(splits):
        grad_active = dot(grad_z, down_full[split])
        _, pull = jax.vjp(partial(jax.nn.gelu, approximate=True), inner[split])
        grad_inner.append(pull(grad_active)[0].astype(bf16))
    down_sums = kept_sums(grad_z, active)
    up_sums = kept_sums(hidden_two, grad_inner)
    grad_hidden_two = sum(dot(grad_inner[split], up_full[split], NT) for split in range(splits))
    grad_shift_two = jnp.sum(grad_hidden_two, axis=0)
    grad_scale_two = jnp.sum(grad_hidden_two * normed_two, axis=0)
    grad_two = grad_three + norm_back(grad_hidden_two * (1.0 + scale_two), normed_two, inverse_two)

    grad_out_two = grad_two.astype(bf16)
    grad_cross = [dot(grad_out_two, full).astype(bf16) for full in co_full]
    (grad_cross[0], down_sums, up_sums) = lax.optimization_barrier(
        (grad_cross[0], down_sums, up_sums)
    )
    down_sums, up_sums = sum_tensor(down_sums), sum_row(up_sums)
    grad_cq, grad_ck, grad_cv = cross_back(cross_q, cross_k, cross_v, grad_cross, part)
    grad_one = grad_two + sum(dot(grad_cq[split], cq_full[split], NT) for split in range(splits))
    text_terms = sum(
        dot(grad_ck[split], key_full[split], NT) + dot(grad_cv[split], val_full[split], NT)
        for split in range(splits)
    )

    grad_gate_one = jnp.sum(grad_one * out_one, axis=0)
    grad_out_one = (gate_one * grad_one).astype(bf16)
    grad_att = [dot(grad_out_one, full).astype(bf16) for full in out_full]
    grad_heads = [None] * groups
    for split in range(splits):
        cuts = [grad_att[split][:, place * edge : (place + 1) * edge] for place in range(ranks)]
        for other in range(ranks):
            step = other * splits + split
            piece = choose(cuts, jnp.bitwise_xor(rank, other))
            grad_heads[step] = send_xor(piece, HEAD_GROUP, step) if step else piece
    mid_sums = [
        kept_sums(left, rights)
        for left, rights in (
            (caption, grad_ck),
            (caption, grad_cv),
            (mid_low, grad_cq),
            (grad_out_two, cross_low),
            (grad_out_one, att),
        )
    ]
    (grad_heads[0], down_sums, up_sums, mid_sums) = lax.optimization_barrier(
        (grad_heads[0], down_sums, up_sums, mid_sums)
    )
    down_sums, up_sums = sum_row(down_sums), sum_tensor(up_sums)
    orders = [(sum_tensor, sum_row), (sum_row, sum_tensor)]
    mid_sums = [orders[place % 2][0](sums) for place, sums in enumerate(mid_sums)]
    grad_mix = list(attend_back(mixed, groups, grad_heads, att_wide, logsum, heads))
    (grad_mix[0], down_sums, up_sums, mid_sums) = lax.optimization_barrier(
        (grad_mix[0], down_sums, up_sums, mid_sums)
    )
    for step in range(1, halves):
        for place in range(groups):
            more = send_xor(grad_mix[step * groups + place], "sr", step)
            grad_mix[place] = (grad_mix[place].astype(f32) + more.astype(f32)).astype(bf16)
    grad_proj = give_back(grad_mix[:groups], HEAD_GROUP)
    grad_proj = [by_split(grad_proj, split) for split in range(splits)]
    mid_sums = [orders[place % 2][1](sums) for place, sums in enumerate(mid_sums)]
    grad_hidden_one = sum(
        dot(grad_proj[split][place], qkv_full[place][split][0], NT)
        for place in range(ranks)
        for split in range(splits)
    )
    grad_shift_one = jnp.sum(grad_hidden_one, axis=0)
    grad_scale_one = jnp.sum(grad_hidden_one * normed_one, axis=0)
    grad_latents = grad_one + norm_back(
        grad_hidden_one * (1.0 + scale_one), normed_one, inverse_one
    )
    grad_latents = dot(grad_latents.astype(bf16), turn, NT).astype(bf16).reshape(latents.shape)
    grad_latents = in_order(give_back(list(grad_latents), "lat"), "lat")

    time_terms = jnp.stack(
        (
            grad_shift_one,
            grad_scale_one,
            grad_gate_one,
            grad_shift_two,
            grad_scale_two,
            grad_gate_two,
        )
    )
    table_terms = jnp.pad(time_terms.T, ((0, 0), (3 * edge, piece_width - 3 * edge - 6)))
    one_sums = [
        kept_sums(
            hidden_one,
            [grad_proj[split][place] for split in range(splits)],
            table_terms if place == 0 else None,
        )
        for place in range(ranks)
    ]
    one_sums = [orders[place % 2][0](sums) for place, sums in enumerate(one_sums)]
    one_sums = [sum_lat(orders[place % 2][1](sums)) for place, sums in enumerate(one_sums)]
    key_sum, val_sum, cq_sum, co_sum, out_sum = (sum_lat(sums)[:, :part] for sums in mid_sums)
    time_natural = lax.dot_general(
        time_terms, turn.astype(f32), NT, precision=lax.Precision.HIGHEST
    )
    text_natural = dot(text_terms.astype(bf16), turn, NT)
    grad_time = over_latents(plane_sum(time_natural, f32)).reshape(-1, 6 * width)
    grad_text = over_latents(plane_sum(text_natural, bf16).astype(bf16)).astype(f32)
    grad_qkv = jnp.stack(
        [sums[:, : 3 * edge].reshape(share, 3, edge) for sums in one_sums], axis=2
    ).reshape(share, 3, part)
    return (
        result_back,
        grad_latents.astype(f32),
        grad_text,
        grad_time,
        one_sums[0][:, 3 * edge : 3 * edge + 6].T,
        grad_qkv,
        out_sum.T,
        cq_sum,
        jnp.stack((key_sum, val_sum), axis=1),
        co_sum.T,
        sum_lat(up_sums),
        sum_lat(down_sums).T,
    )


def solution(mesh):
    def run(latents, text, time_vector, table, w_qkv, *others):
        fsdp, context, tensor = (mesh.shape[name] for name in ("fsdp", "context", "tensor"))
        lat = latents.shape[0] // fsdp
        group = context // lat
        ranks = math.gcd(group, w_qkv.shape[2] // (tensor * HEAD_DIM))
        sizes = (fsdp, lat, group // ranks, ranks, tensor)
        finer = Mesh(mesh.devices.reshape(sizes), ("fsdp", "lat", "sr", "hr", "tensor"))
        line = ("lat", "sr", "hr")
        shard = ("fsdp",) + line
        tokens = P("fsdp", line + ("tensor",), None)
        by_row = P(shard, "tensor")
        by_row3 = P(shard, None, "tensor")
        by_column = P("tensor", shard)
        weights = (by_row3, by_column, by_row, by_row3, by_column, by_row, by_column)
        return jax.shard_map(
            local,
            mesh=finer,
            in_specs=(tokens, P("fsdp", None, None), P("fsdp", None), P(None, shard))
            + weights
            + (tokens,),
            out_specs=(tokens, tokens, P("fsdp", None, None), P("fsdp", None), P(None, shard))
            + weights,
            check_vma=False,
        )(latents, text, time_vector, table, w_qkv, *others)

    return run
```

```python
import math
from functools import partial

import jax
import jax.numpy as jnp
from jax import lax
from jax.experimental import pallas as pl
from jax.experimental.pallas import tpu as pltpu
from jax.sharding import Mesh
from jax.sharding import PartitionSpec as P

HEAD_DIM = 72
EPSILON = 1e-06
LANES = 128
FACTOR = HEAD_DIM ** (-0.5)
FACTOR2 = FACTOR * math.log2(math.e)
VMEM_LIMIT = 56 * 1024 * 1024

f32 = jnp.float32
bf16 = jnp.bfloat16

NT = (((1,), (1,)), ((), ()))
NN = (((1,), (0,)), ((), ()))
TN = (((0,), (0,)), ((), ()))

ROW = ("sr", "hr")
PLANE = ("sr", "hr", "tensor")
HEAD_GROUP = ("hr", "tensor")


def dot(left, right, dims=NN):
    return lax.dot_general(left, right, dims, preferred_element_type=f32)


def norm_parts(values):
    center = values - jnp.mean(values, axis=-1, keepdims=True)
    inverse = lax.rsqrt(jnp.mean(center * center, axis=-1, keepdims=True) + EPSILON)
    return (center * inverse, inverse)


def norm_back(grad_hat, normed, inverse):
    first = jnp.mean(grad_hat, axis=-1, keepdims=True)
    second = jnp.mean(grad_hat * normed, axis=-1, keepdims=True)
    return inverse * (grad_hat - first - normed * second)


def send_xor(piece, axes, step):
    size = lax.axis_size(axes)
    return lax.ppermute(piece, axes, [(rank, rank ^ step) for rank in range(size)])


def pick(stack, index):
    return lax.dynamic_index_in_dim(stack, index, 0, keepdims=False)


def exchange(piece_for, axes):
    me = lax.axis_index(axes)
    got = [piece_for(me)]
    for step in range(1, lax.axis_size(axes)):
        got.append(send_xor(piece_for(jnp.bitwise_xor(me, step)), axes, step))
    return got


def give_back(pieces, axes):
    return [send_xor(piece, axes, step) if step else piece for step, piece in enumerate(pieces)]


def in_order(pieces, axes):
    me = lax.axis_index(axes)
    places = range(len(pieces))
    return jnp.stack([choose(pieces, jnp.bitwise_xor(me, place)) for place in places])


def choose(pieces, index):
    out = pieces[0]
    for place in range(1, len(pieces)):
        out = jnp.where(index == place, pieces[place], out)
    return out


def plane_sum(values, dtype):
    sent = values.astype(dtype)
    total = sent.astype(f32)
    for step in range(1, lax.axis_size(PLANE)):
        total += send_xor(sent, PLANE, step).astype(f32)
    return total


def over_latents(values):
    return in_order(give_back([values] * lax.axis_size("lat"), "lat"), "lat")


def tie(first, second):
    return lax.optimization_barrier((first, second))


def attend_kernel(heads, chunks, own, *refs):
    pieces = refs[:chunks]
    low_refs = refs[chunks : chunks + own]
    att_ref, lse_ref, queries, keys, vals, lows, column = refs[chunks + own :]
    edge = heads * HEAD_DIM
    index = pl.program_id(0)
    block = att_ref.shape[1]

    @pl.when(index == 0)
    def _():
        lane = lax.broadcasted_iota(jnp.int32, vals.shape[1:], 1)
        column[...] = jnp.zeros_like(column)
        for head in range(heads):
            vals[head] = jnp.where(lane == HEAD_DIM, 1.0, 0.0).astype(bf16)
            low = head * HEAD_DIM
            for number, piece in enumerate(pieces):
                count = piece.shape[0]
                rows = slice(number * count, (number + 1) * count)
                if number < own:
                    queries[head, rows] = piece[:, low : low + HEAD_DIM]
                keys[head, rows] = piece[:, edge + low : edge + low + HEAD_DIM]
                vals[head, rows, :HEAD_DIM] = piece[:, 2 * edge + low : 2 * edge + low + HEAD_DIM]

    mine = pl.ds(pl.multiple_of(index * block, block), block)

    def score(head):
        return dot(queries[head, mine, :], keys[head], NT)

    ahead = score(0)
    for head in range(heads):
        scores = ahead
        if head + 1 < heads:
            ahead = score(head + 1)
        top = jnp.max(scores, axis=1, keepdims=True) * FACTOR2
        weights = jnp.exp2(scores * FACTOR2 - top).astype(bf16)
        out = dot(weights, vals[head])
        total = out[:, HEAD_DIM : HEAD_DIM + 1]
        out = out[:, :HEAD_DIM] / total
        att_ref[head] = out
        lows[head, mine, :] = out.astype(bf16)
        column[:, head : head + 1] = top + jnp.log2(total)
    lse_ref[...] = column[...].T[: lse_ref.shape[0]]

    @pl.when(index == pl.num_programs(0) - 1)
    def _():
        for head in range(heads):
            low = head * HEAD_DIM
            for number, ref in enumerate(low_refs):
                count = ref.shape[0]
                ref[:, low : low + HEAD_DIM] = lows[head, number * count : (number + 1) * count, :]


def whole_block(shape):
    return pl.BlockSpec(shape, lambda i: (0,) * len(shape))


def attend(pieces, own, heads):
    count, width = pieces[0].shape
    rows, total = own * count, len(pieces) * count
    block = min(256, rows)
    edge = heads * HEAD_DIM
    slots = -(-heads // 8) * 8
    out = pl.pallas_call(
        partial(attend_kernel, heads, len(pieces), own),
        grid=(rows // block,),
        in_specs=[whole_block((count, width))] * len(pieces),
        out_specs=[whole_block((count, edge))] * own
        + [
            pl.BlockSpec((heads, block, HEAD_DIM), lambda i: (0, i, 0)),
            pl.BlockSpec((slots, block), lambda i: (0, i)),
        ],
        out_shape=[jax.ShapeDtypeStruct((count, edge), bf16)] * own
        + [
            jax.ShapeDtypeStruct((heads, rows, HEAD_DIM), f32),
            jax.ShapeDtypeStruct((slots, rows), f32),
        ],
        scratch_shapes=[
            pltpu.VMEM((heads, rows, HEAD_DIM), bf16),
            pltpu.VMEM((heads, total, HEAD_DIM), bf16),
            pltpu.VMEM((heads, total, LANES), bf16),
            pltpu.VMEM((heads, rows, HEAD_DIM), bf16),
            pltpu.VMEM((block, LANES), f32),
        ],
        cost_estimate=pl.CostEstimate(
            flops=8 * heads * rows * total * LANES,
            transcendentals=heads * rows * total,
            bytes_accessed=4 * total * width,
        ),
        compiler_params=pltpu.CompilerParams(vmem_limit_bytes=VMEM_LIMIT),
    )(*pieces)
    return (out[:own], out[own], out[own + 1])


def attend_back_kernel(heads, chunk, chunks, own, *refs):
    pieces = refs[:chunks]
    grad_refs = refs[chunks : chunks + own]
    att_ref, lse_ref = refs[chunks + own : chunks + own + 2]
    outs = refs[chunks + own + 2 : 2 * chunks + own + 2]
    queries, keys, vals, grads, turned, dq, dk, dv, column = refs[2 * chunks + own + 2 :]
    edge = heads * HEAD_DIM
    index = pl.program_id(0)
    block = att_ref.shape[1]
    total = keys.shape[1]

    @pl.when(index == 0)
    def _():
        turned[...] = jnp.zeros_like(turned)
        column[...] = jnp.zeros_like(column)
        dk[...] = jnp.zeros_like(dk)
        dv[...] = jnp.zeros_like(dv)
        for head in range(heads):
            low = head * HEAD_DIM
            for number, piece in enumerate(pieces):
                count = piece.shape[0]
                rows = slice(number * count, (number + 1) * count)
                if number < own:
                    queries[head, rows] = piece[:, low : low + HEAD_DIM]
                    grads[head, rows] = grad_refs[number][:, low : low + HEAD_DIM]
                key = piece[:, edge + low : edge + low + HEAD_DIM]
                keys[head, rows] = key
                turned[head, :HEAD_DIM, rows] = key.astype(f32).T.astype(bf16)
                vals[head, rows] = piece[:, 2 * edge + low : 2 * edge + low + HEAD_DIM]

    mine = pl.ds(pl.multiple_of(index * block, block), block)
    for head in range(heads):
        column[:, head : head + 1] = jnp.sum(
            att_ref[head] * grads[head, mine, :].astype(f32), axis=1, keepdims=True
        )
    deltas = column[...].T
    for head in range(heads):
        query = queries[head, mine, :]
        grad = grads[head, mine, :]
        lse = lse_ref[head : head + 1, :]
        delta = deltas[head : head + 1, :]
        turned_grad = jnp.zeros((turned.shape[1], block), f32)
        for start in range(0, total, chunk):
            part = slice(start, start + chunk)
            scores = dot(keys[head, part, :], query, NT)
            grad_probs = dot(vals[head, part, :], grad, NT)
            probs = jnp.exp2(scores * FACTOR2 - lse)
            grad_scores = (probs * (grad_probs - delta)).astype(bf16)
            dv[head, part, :] += dot(probs.astype(bf16), grad)
            dk[head, part, :] += dot(grad_scores, query)
            turned_grad += dot(turned[head, :, part], grad_scores)
        dq[head, mine, :] = (turned_grad.T[:, :HEAD_DIM] * FACTOR).astype(bf16)

    @pl.when(index == pl.num_programs(0) - 1)
    def _():
        for number, ref in enumerate(outs):
            count = ref.shape[0]
            rows = slice(number * count, (number + 1) * count)
            ref[...] = jnp.zeros_like(ref)
            for head in range(heads):
                low = head * HEAD_DIM
                if number < own:
                    ref[:, low : low + HEAD_DIM] = dq[head, rows]
                ref[:, edge + low : edge + low + HEAD_DIM] = (dk[head, rows] * FACTOR).astype(bf16)
                ref[:, 2 * edge + low : 2 * edge + low + HEAD_DIM] = dv[head, rows].astype(bf16)


def attend_back(pieces, own, grads, att, lse, heads):
    count, width = pieces[0].shape
    rows, total = own * count, len(pieces) * count
    block = min(256, rows)
    edge = heads * HEAD_DIM
    slots = lse.shape[0]
    return pl.pallas_call(
        partial(attend_back_kernel, heads, min(512, total), len(pieces), own),
        grid=(rows // block,),
        in_specs=[whole_block((count, width))] * len(pieces)
        + [whole_block((count, edge))] * own
        + [
            pl.BlockSpec((heads, block, HEAD_DIM), lambda i: (0, i, 0)),
            pl.BlockSpec((slots, block), lambda i: (0, i)),
        ],
        out_specs=[whole_block((count, width))] * len(pieces),
        out_shape=[jax.ShapeDtypeStruct((count, width), bf16)] * len(pieces),
        scratch_shapes=[
            pltpu.VMEM((heads, rows, HEAD_DIM), bf16),
            pltpu.VMEM((heads, total, HEAD_DIM), bf16),
            pltpu.VMEM((heads, total, HEAD_DIM), bf16),
            pltpu.VMEM((heads, rows, HEAD_DIM), bf16),
            pltpu.VMEM((heads, LANES, total), bf16),
            pltpu.VMEM((heads, rows, HEAD_DIM), bf16),
            pltpu.VMEM((heads, total, HEAD_DIM), f32),
            pltpu.VMEM((heads, total, HEAD_DIM), f32),
            pltpu.VMEM((block, LANES), f32),
        ],
        cost_estimate=pl.CostEstimate(
            flops=20 * heads * rows * total * LANES,
            transcendentals=heads * rows * total,
            bytes_accessed=8 * total * width,
        ),
        compiler_params=pltpu.CompilerParams(vmem_limit_bytes=VMEM_LIMIT),
    )(*pieces, *grads, att, lse)


def head_lanes(part):
    return [slice(low, low + HEAD_DIM) for low in range(0, part, HEAD_DIM)]


def cross_kernel(part, splits, *refs):
    q_refs, k_refs, v_refs, out_refs = (refs[splits * i : splits * (i + 1)] for i in range(4))
    for q_ref, k_ref, v_ref, out_ref in zip(q_refs, k_refs, v_refs, out_refs):
        fill = out_ref.shape[1] - part
        if fill:
            out_ref[:, part:] = jnp.zeros((out_ref.shape[0], fill), bf16)
        for lanes in head_lanes(part):
            scores = dot(q_ref[:, lanes], k_ref[:, lanes], NT) * FACTOR
            weights = jnp.exp(scores - jnp.max(scores, axis=1, keepdims=True))
            probs = weights / jnp.sum(weights, axis=1, keepdims=True)
            out_ref[:, lanes] = dot(probs.astype(bf16), v_ref[:, lanes]).astype(bf16)


def cross(queries, keys, values, part):
    splits = len(queries)
    rows, width = queries[0].shape
    texts = keys[0].shape[0]
    block = min(512, rows)
    split = pl.BlockSpec((block, width), lambda i: (i, 0))
    return pl.pallas_call(
        partial(cross_kernel, part, splits),
        grid=(rows // block,),
        in_specs=[split] * splits + [whole_block((texts, width))] * (2 * splits),
        out_specs=[split] * splits,
        out_shape=[jax.ShapeDtypeStruct((rows, width), bf16)] * splits,
        compiler_params=pltpu.CompilerParams(vmem_limit_bytes=VMEM_LIMIT),
    )(*queries, *keys, *values)


def cross_back_kernel(part, splits, *refs):
    q_refs, k_refs, v_refs, grad_refs, dq_refs, dk_refs, dv_refs, dk_sums, dv_sums = (
        refs[splits * i : splits * (i + 1)] for i in range(9)
    )
    first = pl.program_id(0) == 0
    last = pl.program_id(0) == pl.num_programs(0) - 1
    for q_ref, k_ref, v_ref, grad_ref, dq_ref, dk, dv in zip(
        q_refs, k_refs, v_refs, grad_refs, dq_refs, dk_sums, dv_sums
    ):

        @pl.when(first)
        def _():
            dk[...] = jnp.zeros_like(dk)
            dv[...] = jnp.zeros_like(dv)

        fill = dq_ref.shape[1] - part
        if fill:
            dq_ref[:, part:] = jnp.zeros((dq_ref.shape[0], fill), bf16)
        for lanes in head_lanes(part):
            query = q_ref[:, lanes]
            key = k_ref[:, lanes]
            grad = grad_ref[:, lanes]
            scores = dot(query, key, NT) * FACTOR
            weights = jnp.exp(scores - jnp.max(scores, axis=1, keepdims=True))
            probs = weights / jnp.sum(weights, axis=1, keepdims=True)
            grad_probs = dot(grad, v_ref[:, lanes], NT)
            delta = jnp.sum(probs * grad_probs, axis=1, keepdims=True)
            grad_scores = (probs * (grad_probs - delta)).astype(bf16)
            dq_ref[:, lanes] = (dot(grad_scores, key) * FACTOR).astype(bf16)
            dk[:, lanes] += dot(grad_scores, query, TN)
            dv[:, lanes] += dot(probs.astype(bf16), grad, TN)

    @pl.when(last)
    def _():
        for dk_ref, dv_ref, dk, dv in zip(dk_refs, dv_refs, dk_sums, dv_sums):
            dk_ref[...] = (dk[...] * FACTOR).astype(bf16)
            dv_ref[...] = dv[...].astype(bf16)


def cross_back(queries, keys, values, grads, part):
    splits = len(queries)
    rows, width = queries[0].shape
    texts = keys[0].shape[0]
    block = min(512, rows)
    whole = whole_block((texts, width))
    split = pl.BlockSpec((block, width), lambda i: (i, 0))
    out = pl.pallas_call(
        partial(cross_back_kernel, part, splits),
        grid=(rows // block,),
        in_specs=[split] * splits + [whole] * (2 * splits) + [split] * splits,
        out_specs=[split] * splits + [whole] * (2 * splits),
        out_shape=[jax.ShapeDtypeStruct((rows, width), bf16)] * splits
        + [jax.ShapeDtypeStruct((texts, width), bf16)] * (2 * splits),
        scratch_shapes=[pltpu.VMEM((texts, width), f32)] * (2 * splits),
        compiler_params=pltpu.CompilerParams(vmem_limit_bytes=VMEM_LIMIT),
    )(*queries, *keys, *values, *grads)
    return (out[:splits], out[splits : 2 * splits], out[2 * splits :])


def assemble_kernel(plan, count, *refs):
    sources, (sems,) = refs[:count], refs[-1:]
    outs = refs[count:-1]
    copies = [
        pltpu.make_async_copy(
            sources[source].at[:, pl.ds(column, size)],
            outs[place].at[pl.ds(row, sources[source].shape[0]), :],
            sems.at[number],
        )
        for number, (source, column, size, place, row) in enumerate(plan)
    ]
    for copy in copies:
        copy.start()
    for copy in copies:
        copy.wait()


def assemble(stacks, columns):
    sources = [piece for stack in stacks for piece in stack]
    plan, shapes, base = [], [], 0
    for stack in stacks:
        offset = 0
        for size in columns:
            row = 0
            for number, piece in enumerate(stack):
                plan.append((base + number, offset, size, len(shapes), row))
                row += piece.shape[0]
            shapes.append(jax.ShapeDtypeStruct((row, size), piece.dtype))
            offset += size
        base += len(stack)
    anywhere = pl.BlockSpec(memory_space=pl.ANY)
    out = pl.pallas_call(
        partial(assemble_kernel, plan, len(sources)),
        in_specs=[anywhere] * len(sources),
        out_specs=[pl.BlockSpec(memory_space=pltpu.VMEM)] * len(shapes),
        out_shape=shapes,
        scratch_shapes=[pltpu.SemaphoreType.DMA((len(plan),))],
        compiler_params=pltpu.CompilerParams(vmem_limit_bytes=VMEM_LIMIT),
    )(*sources)
    out = list(out)
    return [out[place : place + len(columns)] for place in range(0, len(out), len(columns))]


def with_others(piece, axes):
    return [piece] + [send_xor(piece, axes, step) for step in range(1, lax.axis_size(axes))]


def gather(shard, columns, tensor_first):
    start = jnp.concatenate(with_others(shard, "lat"))
    if tensor_first and lax.axis_size("tensor") * lax.axis_size(ROW) <= 8:
        stacks = [with_others(piece, ROW) for piece in with_others(start, "tensor")]
    else:
        half = assemble([with_others(start, ROW)], [start.shape[1]])[0][0]
        stacks = [[piece] for piece in with_others(half, "tensor")]
    token = stacks[0][-1]
    stacks = [
        stack + [send_xor(piece, "fsdp", step) for step in range(1, lax.axis_size("fsdp")) for piece in stack]
        for stack in stacks
    ]
    return assemble(stacks, columns), token


def kept_sums(left, rights, extra=None):
    cores = lax.axis_size("fsdp")
    half = left.shape[1] // cores
    out = []
    for right in rights:
        sums = []
        for core in range(cores):
            rows = slice(core * half, (core + 1) * half)
            total = dot(left[:, rows], right, TN)
            if extra is not None:
                total += extra[rows]
            sums.append(total)
        total = sums[0]
        for core in range(1, cores):
            total += send_xor(sums[core].astype(bf16), "fsdp", core).astype(f32)
        out.append(total.astype(bf16))
    return out


def sum_pieces(pieces, axes, dtype=bf16):
    total = pieces[0].astype(f32)
    for step in range(1, len(pieces)):
        total += send_xor(pieces[step], axes, step).astype(f32)
    return total.astype(dtype)


def row_blocks(piece, count):
    size = piece.shape[0] // count
    return [piece[place * size : (place + 1) * size] for place in range(count)]


def sum_tensor(parts):
    return [sum_pieces(parts, "tensor")]


def sum_row(parts):
    return [sum_pieces(row_blocks(part, lax.axis_size(ROW)), ROW) for part in parts]


def sum_lat(parts):
    return sum_pieces(row_blocks(parts[0], lax.axis_size("lat")), "lat", f32)


def own_order(share, width):
    cores, lats, rows = (lax.axis_size(axes) for axes in ("fsdp", "lat", ROW))
    place = lax.iota(jnp.int32, width)
    block, rest = place // share, place % share
    lat = jnp.bitwise_xor(block % lats, lax.axis_index("lat"))
    row = jnp.bitwise_xor(block // lats % rows, lax.axis_index(ROW))
    core = jnp.bitwise_xor(block // (lats * rows), lax.axis_index("fsdp"))
    natural = ((core * lats + lat) * rows + row) * share + rest
    return (lax.broadcasted_iota(jnp.int32, (width, width), 0) == natural[None, :]).astype(bf16)


def local(
    latents, text, time_vector, table, w_qkv, w_out, w_cq, w_ckv, w_co, w_up, w_down, cotangent
):
    width = latents.shape[2]
    share = w_cq.shape[0]
    part = w_cq.shape[1]
    inner_part = w_up.shape[1]
    splits = lax.axis_size("tensor")
    ranks = lax.axis_size("hr")
    halves = lax.axis_size("sr")
    edge = part // ranks
    heads = edge // HEAD_DIM
    groups = ranks * splits
    piece_width = -(-(3 * edge + 6) // LANES) * LANES
    wide = -(-part // LANES) * LANES
    slot = lax.axis_index("lat")
    rank = lax.axis_index("hr")

    def padded(values):
        return jnp.pad(values, ((0, 0), (0, wide - part)))

    latents_got = exchange(partial(pick, latents), "lat")
    shard_qkv = jnp.transpose(w_qkv.reshape(share, 3, ranks, edge), (2, 0, 1, 3)).reshape(
        ranks, share, 3 * edge
    )
    fill = jnp.pad(table.T, ((0, 0), (0, piece_width - 3 * edge - 6)))
    qkv_got = [
        gather(jnp.concatenate((shard_qkv[place], fill), axis=1), [piece_width], place % 2 == 0)
        for place in range(ranks)
    ]
    mid_shard = jnp.concatenate(
        [padded(piece) for piece in (w_out.T, w_ckv[:, 0], w_ckv[:, 1], w_cq, w_co.T)], axis=1
    )
    qkv_full = [full for full, _ in qkv_got]
    mid_shard = lax.optimization_barrier([mid_shard] + [token for _, token in qkv_got])[0]
    mid_full, token = gather(mid_shard, [wide] * 5, False)
    out_full, key_full, val_full, cq_full, co_full = (
        [full[place] for full in mid_full] for place in range(5)
    )
    up_shard, down_shard, _ = lax.optimization_barrier((w_up, w_down.T, token))
    up_got, token = gather(up_shard, [inner_part], False)
    down_got, other_token = gather(down_shard, [inner_part], True)
    up_full, down_full = ([full[0] for full in got] for got in (up_got, down_got))
    cotangent, _, _ = lax.optimization_barrier((cotangent, token, other_token))

    turn = own_order(share, width)
    residual = dot(jnp.concatenate(latents_got, axis=0), turn)
    grad_three = dot(jnp.concatenate(exchange(partial(pick, cotangent), "lat"), axis=0), turn)
    rows = residual.shape[0]
    caption = dot(pick(text, slot), turn).astype(bf16)
    table_full = qkv_full[0][0][0][:, 3 * edge : 3 * edge + 6]
    modulate = table_full.T.astype(f32) + dot(pick(time_vector, slot).reshape(6, width), turn)
    shift_one, scale_one, gate_one, shift_two, scale_two, gate_two = (
        modulate[row : row + 1] for row in range(6)
    )

    normed_one, inverse_one = norm_parts(residual)
    hidden_one = (normed_one * (1.0 + scale_one) + shift_one).astype(bf16)
    mixed = [None] * groups
    for split in range(splits):
        pieces = [dot(hidden_one, full[split][0]).astype(bf16) for full in qkv_full]
        for other in range(ranks):
            step = other * splits + split
            piece = choose(pieces, jnp.bitwise_xor(rank, other))
            mixed[step] = send_xor(piece, HEAD_GROUP, step) if step else piece
    for step in range(1, halves):
        mixed += [send_xor(piece, "sr", step) for piece in mixed[:groups]]
    att_low, att_wide, logsum = attend(mixed, groups, heads)

    def by_split(pieces, split):
        own = [pieces[other * splits + split] for other in range(ranks)]
        return [choose(own, jnp.bitwise_xor(rank, place)) for place in range(ranks)]

    att_back = give_back(att_low, HEAD_GROUP)
    att = [
        padded(jnp.concatenate(by_split(att_back, split), axis=1)) for split in range(splits)
    ]

    out_one = sum(dot(att[split], out_full[split], NT) for split in range(splits))
    after_one = residual + gate_one * out_one
    mid_low = after_one.astype(bf16)
    cross_q = [dot(mid_low, full).astype(bf16) for full in cq_full]
    cross_k = [dot(caption, full).astype(bf16) for full in key_full]
    cross_v = [dot(caption, full).astype(bf16) for full in val_full]
    cross_low = cross(cross_q, cross_k, cross_v, part)
    out_two = sum(dot(cross_low[split], co_full[split], NT) for split in range(splits))
    after_two = after_one + out_two
    normed_two, inverse_two = norm_parts(after_two)
    hidden_two = (normed_two * (1.0 + scale_two) + shift_two).astype(bf16)
    inner = [dot(hidden_two, up_full[split]) for split in range(splits)]
    active = [jax.nn.gelu(values, approximate=True).astype(bf16) for values in inner]
    out_three = sum(dot(active[split], down_full[split], NT) for split in range(splits))
    result = dot((after_two + gate_two * out_three).astype(bf16), turn, NT).astype(bf16)
    result_back = in_order(give_back(list(result.reshape(latents.shape)), "lat"), "lat")

    grad_gate_two = jnp.sum(grad_three * out_three, axis=0)
    grad_z = (gate_two * grad_three).astype(bf16)
    grad_inner = []
    for split in range(splits):
        grad_active = dot(grad_z, down_full[split])
        _, pull = jax.vjp(partial(jax.nn.gelu, approximate=True), inner[split])
        grad_inner.append(pull(grad_active)[0].astype(bf16))
    down_sums = kept_sums(grad_z, active)
    up_sums = kept_sums(hidden_two, grad_inner)
    grad_hidden_two = sum(dot(grad_inner[split], up_full[split], NT) for split in range(splits))
    grad_shift_two = jnp.sum(grad_hidden_two, axis=0)
    grad_scale_two = jnp.sum(grad_hidden_two * normed_two, axis=0)
    grad_two = grad_three + norm_back(grad_hidden_two * (1.0 + scale_two), normed_two, inverse_two)

    grad_out_two = grad_two.astype(bf16)
    grad_cross = [dot(grad_out_two, full).astype(bf16) for full in co_full]
    (grad_cross[0], down_sums, up_sums) = lax.optimization_barrier(
        (grad_cross[0], down_sums, up_sums)
    )
    down_sums, up_sums = sum_tensor(down_sums), sum_row(up_sums)
    grad_cq, grad_ck, grad_cv = cross_back(cross_q, cross_k, cross_v, grad_cross, part)
    grad_one = grad_two + sum(dot(grad_cq[split], cq_full[split], NT) for split in range(splits))
    text_terms = sum(
        dot(grad_ck[split], key_full[split], NT) + dot(grad_cv[split], val_full[split], NT)
        for split in range(splits)
    )

    grad_gate_one = jnp.sum(grad_one * out_one, axis=0)
    grad_out_one = (gate_one * grad_one).astype(bf16)
    grad_att = [dot(grad_out_one, full).astype(bf16) for full in out_full]
    grad_heads = [None] * groups
    for split in range(splits):
        cuts = [grad_att[split][:, place * edge : (place + 1) * edge] for place in range(ranks)]
        for other in range(ranks):
            step = other * splits + split
            piece = choose(cuts, jnp.bitwise_xor(rank, other))
            grad_heads[step] = send_xor(piece, HEAD_GROUP, step) if step else piece
    mid_sums = [
        kept_sums(left, rights)
        for left, rights in (
            (caption, grad_ck),
            (caption, grad_cv),
            (mid_low, grad_cq),
            (grad_out_two, cross_low),
            (grad_out_one, att),
        )
    ]
    (grad_heads[0], down_sums, up_sums, mid_sums, result_back) = lax.optimization_barrier(
        (grad_heads[0], down_sums, up_sums, mid_sums, result_back)
    )
    down_sums, up_sums = sum_row(down_sums), sum_tensor(up_sums)
    orders = [(sum_tensor, sum_row), (sum_row, sum_tensor)]
    mid_sums = [orders[place % 2][0](sums) for place, sums in enumerate(mid_sums)]
    grad_mix = list(attend_back(mixed, groups, grad_heads, att_wide, logsum, heads))
    (grad_mix[0], down_sums, up_sums, mid_sums) = lax.optimization_barrier(
        (grad_mix[0], down_sums, up_sums, mid_sums)
    )
    for step in range(1, halves):
        for place in range(groups):
            more = send_xor(grad_mix[step * groups + place], "sr", step)
            grad_mix[place] = (grad_mix[place].astype(f32) + more.astype(f32)).astype(bf16)
    grad_proj = give_back(grad_mix[:groups], HEAD_GROUP)
    grad_proj = [by_split(grad_proj, split) for split in range(splits)]
    mid_sums = [orders[place % 2][1](sums) for place, sums in enumerate(mid_sums)]
    up_sum, down_sum = sum_lat(up_sums), sum_lat(down_sums)
    (grad_proj, mid_sums, up_sum, down_sum) = lax.optimization_barrier(
        (grad_proj, mid_sums, up_sum, down_sum)
    )
    grad_hidden_one = sum(
        dot(grad_proj[split][place], qkv_full[place][split][0], NT)
        for place in range(ranks)
        for split in range(splits)
    )
    grad_shift_one = jnp.sum(grad_hidden_one, axis=0)
    grad_scale_one = jnp.sum(grad_hidden_one * normed_one, axis=0)
    grad_latents = grad_one + norm_back(
        grad_hidden_one * (1.0 + scale_one), normed_one, inverse_one
    )
    grad_latents = dot(grad_latents.astype(bf16), turn, NT).astype(bf16).reshape(latents.shape)
    grad_latents = in_order(give_back(list(grad_latents), "lat"), "lat")

    time_terms = jnp.stack(
        (
            grad_shift_one,
            grad_scale_one,
            grad_gate_one,
            grad_shift_two,
            grad_scale_two,
            grad_gate_two,
        )
    )
    table_terms = jnp.pad(time_terms.T, ((0, 0), (3 * edge, piece_width - 3 * edge - 6)))
    one_sums = [
        kept_sums(
            hidden_one,
            [grad_proj[split][place] for split in range(splits)],
            table_terms if place == 0 else None,
        )
        for place in range(ranks)
    ]
    one_sums = [orders[place % 2][0](sums) for place, sums in enumerate(one_sums)]
    one_sums = [sum_lat(orders[place % 2][1](sums)) for place, sums in enumerate(one_sums)]
    key_sum, val_sum, cq_sum, co_sum, out_sum = (sum_lat(sums)[:, :part] for sums in mid_sums)
    time_natural = lax.dot_general(
        time_terms, turn.astype(f32), NT, precision=lax.Precision.HIGHEST
    )
    text_natural = dot(text_terms.astype(bf16), turn, NT)
    grad_time = over_latents(plane_sum(time_natural, f32)).reshape(-1, 6 * width)
    grad_text = over_latents(plane_sum(text_natural, bf16).astype(bf16)).astype(f32)
    grad_qkv = jnp.stack(
        [sums[:, : 3 * edge].reshape(share, 3, edge) for sums in one_sums], axis=2
    ).reshape(share, 3, part)
    return (
        result_back,
        grad_latents.astype(f32),
        grad_text,
        grad_time,
        one_sums[0][:, 3 * edge : 3 * edge + 6].T,
        grad_qkv,
        out_sum.T,
        cq_sum,
        jnp.stack((key_sum, val_sum), axis=1),
        co_sum.T,
        up_sum,
        down_sum.T,
    )


def solution(mesh):
    def run(latents, text, time_vector, table, w_qkv, *others):
        fsdp, context, tensor = (mesh.shape[name] for name in ("fsdp", "context", "tensor"))
        lat = latents.shape[0] // fsdp
        group = context // lat
        ranks = math.gcd(group, w_qkv.shape[2] // (tensor * HEAD_DIM))
        sizes = (fsdp, lat, group // ranks, ranks, tensor)
        finer = Mesh(mesh.devices.reshape(sizes), ("fsdp", "lat", "sr", "hr", "tensor"))
        line = ("lat", "sr", "hr")
        shard = ("fsdp",) + line
        tokens = P("fsdp", line + ("tensor",), None)
        by_row = P(shard, "tensor")
        by_row3 = P(shard, None, "tensor")
        by_column = P("tensor", shard)
        weights = (by_row3, by_column, by_row, by_row3, by_column, by_row, by_column)
        return jax.shard_map(
            local,
            mesh=finer,
            in_specs=(tokens, P("fsdp", None, None), P("fsdp", None), P(None, shard))
            + weights
            + (tokens,),
            out_specs=(tokens, tokens, P("fsdp", None, None), P("fsdp", None), P(None, shard))
            + weights,
            check_vma=False,
        )(latents, text, time_vector, table, w_qkv, *others)

    return run
```

```python
import math
from functools import partial

import jax
import jax.numpy as jnp
from jax import lax
from jax.experimental import pallas as pl
from jax.experimental.pallas import tpu as pltpu
from jax.sharding import Mesh
from jax.sharding import PartitionSpec as P

HEAD_DIM = 72
EPSILON = 1e-06
LANES = 128
FACTOR = HEAD_DIM ** (-0.5)
FACTOR2 = FACTOR * math.log2(math.e)
VMEM_LIMIT = 56 * 1024 * 1024

f32 = jnp.float32
bf16 = jnp.bfloat16

NT = (((1,), (1,)), ((), ()))
NN = (((1,), (0,)), ((), ()))
TN = (((0,), (0,)), ((), ()))

ROW = ("sr", "hr")
EVERY = ("tensor", "fsdp", "lat", "sr", "hr")
PLANE = ("sr", "hr", "tensor")
HEAD_GROUP = ("hr", "tensor")


def dot(left, right, dims=NN):
    return lax.dot_general(left, right, dims, preferred_element_type=f32)


def norm_parts(values):
    center = values - jnp.mean(values, axis=-1, keepdims=True)
    inverse = lax.rsqrt(jnp.mean(center * center, axis=-1, keepdims=True) + EPSILON)
    return (center * inverse, inverse)


def norm_back(grad_hat, normed, inverse):
    first = jnp.mean(grad_hat, axis=-1, keepdims=True)
    second = jnp.mean(grad_hat * normed, axis=-1, keepdims=True)
    return inverse * (grad_hat - first - normed * second)


def send_xor(piece, axes, step):
    size = lax.axis_size(axes)
    return lax.ppermute(piece, axes, [(rank, rank ^ step) for rank in range(size)])


def pick(stack, index):
    return lax.dynamic_index_in_dim(stack, index, 0, keepdims=False)


def exchange(piece_for, axes):
    me = lax.axis_index(axes)
    got = [piece_for(me)]
    for step in range(1, lax.axis_size(axes)):
        got.append(send_xor(piece_for(jnp.bitwise_xor(me, step)), axes, step))
    return got


def give_back(pieces, axes):
    return [send_xor(piece, axes, step) if step else piece for step, piece in enumerate(pieces)]


def in_order(pieces, axes):
    me = lax.axis_index(axes)
    places = range(len(pieces))
    return jnp.stack([choose(pieces, jnp.bitwise_xor(me, place)) for place in places])


def choose(pieces, index):
    out = pieces[0]
    for place in range(1, len(pieces)):
        out = jnp.where(index == place, pieces[place], out)
    return out


def plane_sum(values, dtype):
    sent = values.astype(dtype)
    total = sent.astype(f32)
    for step in range(1, lax.axis_size(PLANE)):
        total += send_xor(sent, PLANE, step).astype(f32)
    return total


def over_latents(values):
    return in_order(give_back([values] * lax.axis_size("lat"), "lat"), "lat")


def tie(first, second):
    return lax.optimization_barrier((first, second))


def attend_kernel(heads, chunks, own, *refs):
    pieces = refs[:chunks]
    low_refs = refs[chunks : chunks + own]
    att_ref, lse_ref, queries, keys, vals, lows, column = refs[chunks + own :]
    edge = heads * HEAD_DIM
    index = pl.program_id(0)
    block = att_ref.shape[1]

    @pl.when(index == 0)
    def _():
        lane = lax.broadcasted_iota(jnp.int32, vals.shape[1:], 1)
        column[...] = jnp.zeros_like(column)
        for head in range(heads):
            vals[head] = jnp.where(lane == HEAD_DIM, 1.0, 0.0).astype(bf16)
            low = head * HEAD_DIM
            for number, piece in enumerate(pieces):
                count = piece.shape[0]
                rows = slice(number * count, (number + 1) * count)
                if number < own:
                    queries[head, rows] = piece[:, low : low + HEAD_DIM]
                keys[head, rows] = piece[:, edge + low : edge + low + HEAD_DIM]
                vals[head, rows, :HEAD_DIM] = piece[:, 2 * edge + low : 2 * edge + low + HEAD_DIM]

    mine = pl.ds(pl.multiple_of(index * block, block), block)

    def score(head):
        return dot(queries[head, mine, :], keys[head], NT)

    ahead = score(0)
    for head in range(heads):
        scores = ahead
        if head + 1 < heads:
            ahead = score(head + 1)
        top = jnp.max(scores, axis=1, keepdims=True) * FACTOR2
        weights = jnp.exp2(scores * FACTOR2 - top).astype(bf16)
        out = dot(weights, vals[head])
        total = out[:, HEAD_DIM : HEAD_DIM + 1]
        out = out[:, :HEAD_DIM] / total
        att_ref[head] = out
        lows[head, mine, :] = out.astype(bf16)
        column[:, head : head + 1] = top + jnp.log2(total)
    lse_ref[...] = column[...].T[: lse_ref.shape[0]]

    @pl.when(index == pl.num_programs(0) - 1)
    def _():
        for head in range(heads):
            low = head * HEAD_DIM
            for number, ref in enumerate(low_refs):
                count = ref.shape[0]
                ref[:, low : low + HEAD_DIM] = lows[head, number * count : (number + 1) * count, :]


def whole_block(shape):
    return pl.BlockSpec(shape, lambda i: (0,) * len(shape))


def attend(pieces, own, heads):
    count, width = pieces[0].shape
    rows, total = own * count, len(pieces) * count
    block = min(256, rows)
    edge = heads * HEAD_DIM
    slots = -(-heads // 8) * 8
    out = pl.pallas_call(
        partial(attend_kernel, heads, len(pieces), own),
        grid=(rows // block,),
        in_specs=[whole_block((count, width))] * len(pieces),
        out_specs=[whole_block((count, edge))] * own
        + [
            pl.BlockSpec((heads, block, HEAD_DIM), lambda i: (0, i, 0)),
            pl.BlockSpec((slots, block), lambda i: (0, i)),
        ],
        out_shape=[jax.ShapeDtypeStruct((count, edge), bf16)] * own
        + [
            jax.ShapeDtypeStruct((heads, rows, HEAD_DIM), f32),
            jax.ShapeDtypeStruct((slots, rows), f32),
        ],
        scratch_shapes=[
            pltpu.VMEM((heads, rows, HEAD_DIM), bf16),
            pltpu.VMEM((heads, total, HEAD_DIM), bf16),
            pltpu.VMEM((heads, total, LANES), bf16),
            pltpu.VMEM((heads, rows, HEAD_DIM), bf16),
            pltpu.VMEM((block, LANES), f32),
        ],
        cost_estimate=pl.CostEstimate(
            flops=8 * heads * rows * total * LANES,
            transcendentals=heads * rows * total,
            bytes_accessed=4 * total * width,
        ),
        compiler_params=pltpu.CompilerParams(vmem_limit_bytes=VMEM_LIMIT),
    )(*pieces)
    return (out[:own], out[own], out[own + 1])


def attend_back_kernel(heads, chunk, chunks, own, *refs):
    pieces = refs[:chunks]
    grad_refs = refs[chunks : chunks + own]
    att_ref, lse_ref = refs[chunks + own : chunks + own + 2]
    outs = refs[chunks + own + 2 : 2 * chunks + own + 2]
    queries, keys, vals, grads, turned, dq, dk, dv, column = refs[2 * chunks + own + 2 :]
    edge = heads * HEAD_DIM
    index = pl.program_id(0)
    block = att_ref.shape[1]
    total = keys.shape[1]

    @pl.when(index == 0)
    def _():
        turned[...] = jnp.zeros_like(turned)
        column[...] = jnp.zeros_like(column)
        dk[...] = jnp.zeros_like(dk)
        dv[...] = jnp.zeros_like(dv)
        for head in range(heads):
            low = head * HEAD_DIM
            for number, piece in enumerate(pieces):
                count = piece.shape[0]
                rows = slice(number * count, (number + 1) * count)
                if number < own:
                    queries[head, rows] = piece[:, low : low + HEAD_DIM]
                    grads[head, rows] = grad_refs[number][:, low : low + HEAD_DIM]
                key = piece[:, edge + low : edge + low + HEAD_DIM]
                keys[head, rows] = key
                turned[head, :HEAD_DIM, rows] = key.astype(f32).T.astype(bf16)
                vals[head, rows] = piece[:, 2 * edge + low : 2 * edge + low + HEAD_DIM]

    mine = pl.ds(pl.multiple_of(index * block, block), block)
    for head in range(heads):
        column[:, head : head + 1] = jnp.sum(
            att_ref[head] * grads[head, mine, :].astype(f32), axis=1, keepdims=True
        )
    deltas = column[...].T
    for head in range(heads):
        query = queries[head, mine, :]
        grad = grads[head, mine, :]
        lse = lse_ref[head : head + 1, :]
        delta = deltas[head : head + 1, :]
        turned_grad = jnp.zeros((turned.shape[1], block), f32)
        for start in range(0, total, chunk):
            part = slice(start, start + chunk)
            scores = dot(keys[head, part, :], query, NT)
            grad_probs = dot(vals[head, part, :], grad, NT)
            probs = jnp.exp2(scores * FACTOR2 - lse)
            grad_scores = (probs * (grad_probs - delta)).astype(bf16)
            dv[head, part, :] += dot(probs.astype(bf16), grad)
            dk[head, part, :] += dot(grad_scores, query)
            turned_grad += dot(turned[head, :, part], grad_scores)
        dq[head, mine, :] = (turned_grad.T[:, :HEAD_DIM] * FACTOR).astype(bf16)

    @pl.when(index == pl.num_programs(0) - 1)
    def _():
        for number, ref in enumerate(outs):
            count = ref.shape[0]
            rows = slice(number * count, (number + 1) * count)
            ref[...] = jnp.zeros_like(ref)
            for head in range(heads):
                low = head * HEAD_DIM
                if number < own:
                    ref[:, low : low + HEAD_DIM] = dq[head, rows]
                ref[:, edge + low : edge + low + HEAD_DIM] = (dk[head, rows] * FACTOR).astype(bf16)
                ref[:, 2 * edge + low : 2 * edge + low + HEAD_DIM] = dv[head, rows].astype(bf16)


def attend_back(pieces, own, grads, att, lse, heads):
    count, width = pieces[0].shape
    rows, total = own * count, len(pieces) * count
    block = min(256, rows)
    edge = heads * HEAD_DIM
    slots = lse.shape[0]
    return pl.pallas_call(
        partial(attend_back_kernel, heads, min(512, total), len(pieces), own),
        grid=(rows // block,),
        in_specs=[whole_block((count, width))] * len(pieces)
        + [whole_block((count, edge))] * own
        + [
            pl.BlockSpec((heads, block, HEAD_DIM), lambda i: (0, i, 0)),
            pl.BlockSpec((slots, block), lambda i: (0, i)),
        ],
        out_specs=[whole_block((count, width))] * len(pieces),
        out_shape=[jax.ShapeDtypeStruct((count, width), bf16)] * len(pieces),
        scratch_shapes=[
            pltpu.VMEM((heads, rows, HEAD_DIM), bf16),
            pltpu.VMEM((heads, total, HEAD_DIM), bf16),
            pltpu.VMEM((heads, total, HEAD_DIM), bf16),
            pltpu.VMEM((heads, rows, HEAD_DIM), bf16),
            pltpu.VMEM((heads, LANES, total), bf16),
            pltpu.VMEM((heads, rows, HEAD_DIM), bf16),
            pltpu.VMEM((heads, total, HEAD_DIM), f32),
            pltpu.VMEM((heads, total, HEAD_DIM), f32),
            pltpu.VMEM((block, LANES), f32),
        ],
        cost_estimate=pl.CostEstimate(
            flops=20 * heads * rows * total * LANES,
            transcendentals=heads * rows * total,
            bytes_accessed=8 * total * width,
        ),
        compiler_params=pltpu.CompilerParams(vmem_limit_bytes=VMEM_LIMIT),
    )(*pieces, *grads, att, lse)


def head_lanes(part):
    return [slice(low, low + HEAD_DIM) for low in range(0, part, HEAD_DIM)]


def cross_kernel(part, splits, *refs):
    q_refs, k_refs, v_refs, out_refs = (refs[splits * i : splits * (i + 1)] for i in range(4))
    for q_ref, k_ref, v_ref, out_ref in zip(q_refs, k_refs, v_refs, out_refs):
        fill = out_ref.shape[1] - part
        if fill:
            out_ref[:, part:] = jnp.zeros((out_ref.shape[0], fill), bf16)
        for lanes in head_lanes(part):
            scores = dot(q_ref[:, lanes], k_ref[:, lanes], NT) * FACTOR
            weights = jnp.exp(scores - jnp.max(scores, axis=1, keepdims=True))
            probs = weights / jnp.sum(weights, axis=1, keepdims=True)
            out_ref[:, lanes] = dot(probs.astype(bf16), v_ref[:, lanes]).astype(bf16)


def cross(queries, keys, values, part):
    splits = len(queries)
    rows, width = queries[0].shape
    texts = keys[0].shape[0]
    block = min(512, rows)
    split = pl.BlockSpec((block, width), lambda i: (i, 0))
    return pl.pallas_call(
        partial(cross_kernel, part, splits),
        grid=(rows // block,),
        in_specs=[split] * splits + [whole_block((texts, width))] * (2 * splits),
        out_specs=[split] * splits,
        out_shape=[jax.ShapeDtypeStruct((rows, width), bf16)] * splits,
        compiler_params=pltpu.CompilerParams(vmem_limit_bytes=VMEM_LIMIT),
    )(*queries, *keys, *values)


def cross_back_kernel(part, splits, *refs):
    q_refs, k_refs, v_refs, grad_refs, dq_refs, dk_refs, dv_refs, dk_sums, dv_sums = (
        refs[splits * i : splits * (i + 1)] for i in range(9)
    )
    first = pl.program_id(0) == 0
    last = pl.program_id(0) == pl.num_programs(0) - 1
    for q_ref, k_ref, v_ref, grad_ref, dq_ref, dk, dv in zip(
        q_refs, k_refs, v_refs, grad_refs, dq_refs, dk_sums, dv_sums
    ):

        @pl.when(first)
        def _():
            dk[...] = jnp.zeros_like(dk)
            dv[...] = jnp.zeros_like(dv)

        fill = dq_ref.shape[1] - part
        if fill:
            dq_ref[:, part:] = jnp.zeros((dq_ref.shape[0], fill), bf16)
        for lanes in head_lanes(part):
            query = q_ref[:, lanes]
            key = k_ref[:, lanes]
            grad = grad_ref[:, lanes]
            scores = dot(query, key, NT) * FACTOR
            weights = jnp.exp(scores - jnp.max(scores, axis=1, keepdims=True))
            probs = weights / jnp.sum(weights, axis=1, keepdims=True)
            grad_probs = dot(grad, v_ref[:, lanes], NT)
            delta = jnp.sum(probs * grad_probs, axis=1, keepdims=True)
            grad_scores = (probs * (grad_probs - delta)).astype(bf16)
            dq_ref[:, lanes] = (dot(grad_scores, key) * FACTOR).astype(bf16)
            dk[:, lanes] += dot(grad_scores, query, TN)
            dv[:, lanes] += dot(probs.astype(bf16), grad, TN)

    @pl.when(last)
    def _():
        for dk_ref, dv_ref, dk, dv in zip(dk_refs, dv_refs, dk_sums, dv_sums):
            dk_ref[...] = (dk[...] * FACTOR).astype(bf16)
            dv_ref[...] = dv[...].astype(bf16)


def cross_back(queries, keys, values, grads, part):
    splits = len(queries)
    rows, width = queries[0].shape
    texts = keys[0].shape[0]
    block = min(512, rows)
    whole = whole_block((texts, width))
    split = pl.BlockSpec((block, width), lambda i: (i, 0))
    out = pl.pallas_call(
        partial(cross_back_kernel, part, splits),
        grid=(rows // block,),
        in_specs=[split] * splits + [whole] * (2 * splits) + [split] * splits,
        out_specs=[split] * splits + [whole] * (2 * splits),
        out_shape=[jax.ShapeDtypeStruct((rows, width), bf16)] * splits
        + [jax.ShapeDtypeStruct((texts, width), bf16)] * (2 * splits),
        scratch_shapes=[pltpu.VMEM((texts, width), f32)] * (2 * splits),
        compiler_params=pltpu.CompilerParams(vmem_limit_bytes=VMEM_LIMIT),
    )(*queries, *keys, *values, *grads)
    return (out[:splits], out[splits : 2 * splits], out[2 * splits :])


def assemble_kernel(plan, count, *refs):
    sources, outs, sems = refs[:count], refs[count:-1], refs[-1]
    copies = []
    for number, (source, start, rows, column, size, place, row, shift) in enumerate(plan):
        copies.append(
            pltpu.make_async_copy(
                sources[source].at[pl.ds(start, rows), pl.ds(column, size)],
                outs[place].at[pl.ds(row, rows), pl.ds(shift, size)],
                sems.at[number],
            )
        )
    for copy in copies:
        copy.start()
    for copy in copies:
        copy.wait()


def lay(sources, plan, shapes):
    anywhere = pl.BlockSpec(memory_space=pl.ANY)
    return list(
        pl.pallas_call(
            partial(assemble_kernel, plan, len(sources)),
            in_specs=[anywhere] * len(sources),
            out_specs=[pl.BlockSpec(memory_space=pltpu.VMEM)] * len(shapes),
            out_shape=[jax.ShapeDtypeStruct(shape, bf16) for shape in shapes],
            scratch_shapes=[pltpu.SemaphoreType.DMA((len(plan),))],
            compiler_params=pltpu.CompilerParams(vmem_limit_bytes=VMEM_LIMIT),
        )(*sources)
    )


def assemble(stacks):
    sources = [piece for stack in stacks for piece in stack]
    plan, shapes = [], []
    for stack in stacks:
        row, width = 0, stack[0].shape[1]
        for piece in stack:
            plan.append((len(plan), 0, piece.shape[0], 0, width, len(shapes), row, 0))
            row += piece.shape[0]
        shapes.append((row, width))
    return lay(sources, plan, shapes)


def cut(source, rows, columns):
    grid = [
        (place, row) for place in range(source.shape[1] // columns) for row in range(source.shape[0] // rows)
    ]
    plan = [
        (0, row * rows, rows, place * columns, columns, number, 0, 0)
        for number, (place, row) in enumerate(grid)
    ]
    out = lay([source], plan, [(rows, columns)] * len(grid))
    count = source.shape[0] // rows
    return [out[place : place + count] for place in range(0, len(out), count)]


def with_others(piece, axes):
    return [piece] + [send_xor(piece, axes, step) for step in range(1, lax.axis_size(axes))]


def gather(shard, tensor_first):
    start = jnp.concatenate(with_others(shard, "lat"))
    if tensor_first and lax.axis_size("tensor") * lax.axis_size(ROW) <= 8:
        stacks = [with_others(piece, ROW) for piece in with_others(start, "tensor")]
    else:
        half = assemble([with_others(start, ROW)])[0]
        stacks = [[piece] for piece in with_others(half, "tensor")]
    cores = range(1, lax.axis_size("fsdp"))
    return assemble(
        [stack + [send_xor(piece, "fsdp", step) for step in cores for piece in stack] for stack in stacks]
    )


def gather_all(shard):
    return lax.all_gather(shard, EVERY, axis=shard.ndim - 2, tiled=True)


def scatter_all(pieces):
    pack = assemble([pieces])[0]
    return lax.psum_scatter(pack, EVERY, scatter_dimension=0, tiled=True).astype(f32)


def kept_sums(left, rights, extra=None):
    cores = lax.axis_size("fsdp")
    half = left.shape[1] // cores
    out = []
    for right in rights:
        sums = []
        for core in range(cores):
            rows = slice(core * half, (core + 1) * half)
            total = dot(left[:, rows], right, TN)
            if extra is not None:
                total += extra[rows]
            sums.append(total)
        total = sums[0]
        for core in range(1, cores):
            total += send_xor(sums[core].astype(bf16), "fsdp", core).astype(f32)
        out.append(total.astype(bf16))
    return out


def sum_pieces(pieces, axes, dtype=bf16):
    total = pieces[0].astype(f32)
    for step in range(1, len(pieces)):
        total += send_xor(pieces[step], axes, step).astype(f32)
    return total.astype(dtype)


def row_blocks(piece, count):
    size = piece.shape[0] // count
    return [piece[place * size : (place + 1) * size] for place in range(count)]


def sum_tensor(parts):
    return [sum_pieces(parts, "tensor")]


def sum_row(parts):
    return [sum_pieces(row_blocks(part, lax.axis_size(ROW)), ROW) for part in parts]


def sum_lat(parts):
    return sum_pieces(row_blocks(parts[0], lax.axis_size("lat")), "lat", f32)


def own_order(share, width):
    cores, lats, rows = (lax.axis_size(axes) for axes in ("fsdp", "lat", ROW))
    place = lax.iota(jnp.int32, width)
    block, rest = place // share, place % share
    lat = jnp.bitwise_xor(block % lats, lax.axis_index("lat"))
    row = jnp.bitwise_xor(block // lats % rows, lax.axis_index(ROW))
    core = jnp.bitwise_xor(block // (lats * rows), lax.axis_index("fsdp"))
    natural = ((core * lats + lat) * rows + row) * share + rest
    return (lax.broadcasted_iota(jnp.int32, (width, width), 0) == natural[None, :]).astype(bf16)


def local(
    latents, text, time_vector, table, w_qkv, w_out, w_cq, w_ckv, w_co, w_up, w_down, cotangent
):
    width = latents.shape[2]
    share = w_cq.shape[0]
    part = w_cq.shape[1]
    inner_part = w_up.shape[1]
    splits = lax.axis_size("tensor")
    ranks = lax.axis_size("hr")
    halves = lax.axis_size("sr")
    edge = part // ranks
    heads = edge // HEAD_DIM
    groups = ranks * splits
    piece_width = -(-(3 * edge + 6) // LANES) * LANES
    wide = -(-part // LANES) * LANES
    slot = lax.axis_index("lat")
    rank = lax.axis_index("hr")

    def padded(values):
        return jnp.pad(values, ((0, 0), (0, wide - part)))

    latents_got = exchange(partial(pick, latents), "lat")
    mid_shard = jnp.concatenate(
        [padded(piece) for piece in (w_out.T, w_ckv[:, 0], w_ckv[:, 1], w_cq, w_co.T)], axis=1
    )
    mid_full = gather_all(mid_shard)
    two_full = gather_all(jnp.stack((w_up, w_down.T)))
    shard_qkv = jnp.transpose(w_qkv.reshape(share, 3, ranks, edge), (2, 0, 1, 3)).reshape(
        ranks, share, 3 * edge
    )
    fill = jnp.pad(table.T, ((0, 0), (0, piece_width - 3 * edge - 6)))
    qkv_full = [
        gather(jnp.concatenate((shard_qkv[place], fill), axis=1), place % 2 == 0)
        for place in range(ranks)
    ]

    turn = own_order(share, width)
    residual = jnp.concatenate(latents_got, axis=0).astype(f32)
    cotangent, _ = tie(cotangent, qkv_full[0][0])
    grad_three = jnp.concatenate(exchange(partial(pick, cotangent), "lat"), axis=0).astype(f32)
    rows = residual.shape[0]
    caption = pick(text, slot)
    table_full = dot(qkv_full[0][0][:, 3 * edge : 3 * edge + 6].T, turn, NT)
    modulate = table_full + pick(time_vector, slot).astype(f32).reshape(6, width)
    shift_one, scale_one, gate_one, shift_two, scale_two, gate_two = (
        modulate[row : row + 1] for row in range(6)
    )

    normed_one, inverse_one = norm_parts(residual)
    hidden_one = (normed_one * (1.0 + scale_one) + shift_one).astype(bf16)
    hidden_one = dot(hidden_one, turn).astype(bf16)
    mixed = [None] * groups
    for split in range(splits):
        pieces = [dot(hidden_one, full[split]).astype(bf16) for full in qkv_full]
        for other in range(ranks):
            step = other * splits + split
            piece = choose(pieces, jnp.bitwise_xor(rank, other))
            mixed[step] = send_xor(piece, HEAD_GROUP, step) if step else piece
    for step in range(1, halves):
        mixed += [send_xor(piece, "sr", step) for piece in mixed[:groups]]
    att_low, att_wide, logsum = attend(mixed, groups, heads)

    def by_split(pieces, split):
        own = [pieces[other * splits + split] for other in range(ranks)]
        return [choose(own, jnp.bitwise_xor(rank, place)) for place in range(ranks)]

    att_back = give_back(att_low, HEAD_GROUP)
    att_own = [
        padded(jnp.concatenate(by_split(att_back, split), axis=1)) for split in range(splits)
    ]
    col = lax.axis_index("tensor")

    def from_own(pieces):
        return [choose(pieces, jnp.bitwise_xor(col, place)) for place in range(splits)]

    att = from_own(att_own)
    out_full, key_full, val_full, cq_full, co_full = cut(mid_full, width, wide)
    up_full, down_full = (
        [two_full[place, split * width : (split + 1) * width] for split in range(splits)]
        for place in range(2)
    )

    out_one = sum(dot(att[split], out_full[split], NT) for split in range(splits))
    after_one = residual + gate_one * out_one
    mid_low = after_one.astype(bf16)
    cross_q = [dot(mid_low, full).astype(bf16) for full in cq_full]
    cross_k = [dot(caption, full).astype(bf16) for full in key_full]
    cross_v = [dot(caption, full).astype(bf16) for full in val_full]
    cross_low = cross(cross_q, cross_k, cross_v, part)
    out_two = sum(dot(cross_low[split], co_full[split], NT) for split in range(splits))
    after_two = after_one + out_two
    normed_two, inverse_two = norm_parts(after_two)
    hidden_two = (normed_two * (1.0 + scale_two) + shift_two).astype(bf16)
    inner = [dot(hidden_two, up_full[split]) for split in range(splits)]
    active = [jax.nn.gelu(values, approximate=True).astype(bf16) for values in inner]
    out_three = sum(dot(active[split], down_full[split], NT) for split in range(splits))
    result = (after_two + gate_two * out_three).astype(bf16)
    result_back = in_order(give_back(list(result.reshape(latents.shape)), "lat"), "lat")

    grad_gate_two = jnp.sum(grad_three * out_three, axis=0)
    grad_z = (gate_two * grad_three).astype(bf16)
    grad_inner = []
    for split in range(splits):
        grad_active = dot(grad_z, down_full[split])
        _, pull = jax.vjp(partial(jax.nn.gelu, approximate=True), inner[split])
        grad_inner.append(pull(grad_active)[0].astype(bf16))
    down_sum = scatter_all([dot(grad_z, piece, TN).astype(bf16) for piece in active])
    up_sum = scatter_all([dot(hidden_two, piece, TN).astype(bf16) for piece in grad_inner])
    grad_hidden_two = sum(dot(grad_inner[split], up_full[split], NT) for split in range(splits))
    grad_shift_two = jnp.sum(grad_hidden_two, axis=0)
    grad_scale_two = jnp.sum(grad_hidden_two * normed_two, axis=0)
    grad_two = grad_three + norm_back(grad_hidden_two * (1.0 + scale_two), normed_two, inverse_two)

    grad_out_two = grad_two.astype(bf16)
    grad_cross = [dot(grad_out_two, full).astype(bf16) for full in co_full]
    grad_cq, grad_ck, grad_cv = cross_back(cross_q, cross_k, cross_v, grad_cross, part)
    grad_one = grad_two + sum(dot(grad_cq[split], cq_full[split], NT) for split in range(splits))
    text_terms = sum(
        dot(grad_ck[split], key_full[split], NT) + dot(grad_cv[split], val_full[split], NT)
        for split in range(splits)
    )

    grad_gate_one = jnp.sum(grad_one * out_one, axis=0)
    grad_out_one = (gate_one * grad_one).astype(bf16)
    grad_att = from_own([dot(grad_out_one, full).astype(bf16) for full in out_full])
    grad_heads = [None] * groups
    for split in range(splits):
        cuts = [grad_att[split][:, place * edge : (place + 1) * edge] for place in range(ranks)]
        for other in range(ranks):
            step = other * splits + split
            piece = choose(cuts, jnp.bitwise_xor(rank, other))
            grad_heads[step] = send_xor(piece, HEAD_GROUP, step) if step else piece
    caption_turn = dot(caption, turn).astype(bf16)
    mid_sums = [
        kept_sums(left, rights)
        for left, rights in (
            (caption_turn, from_own(grad_ck)),
            (caption_turn, from_own(grad_cv)),
            (dot(mid_low, turn).astype(bf16), from_own(grad_cq)),
            (dot(grad_out_two, turn).astype(bf16), from_own(cross_low)),
            (dot(grad_out_one, turn).astype(bf16), att_own),
        )
    ]
    (grad_heads[0], mid_sums, result_back, down_sum) = lax.optimization_barrier(
        (grad_heads[0], mid_sums, result_back, down_sum)
    )
    orders = [(sum_tensor, sum_row), (sum_row, sum_tensor)]
    mid_sums = [orders[place % 2][0](sums) for place, sums in enumerate(mid_sums)]
    grad_mix = list(attend_back(mixed, groups, grad_heads, att_wide, logsum, heads))
    (grad_mix[0], mid_sums) = tie(grad_mix[0], mid_sums)
    for step in range(1, halves):
        for place in range(groups):
            more = send_xor(grad_mix[step * groups + place], "sr", step)
            grad_mix[place] = (grad_mix[place].astype(f32) + more.astype(f32)).astype(bf16)
    grad_proj = give_back(grad_mix[:groups], HEAD_GROUP)
    grad_proj = [by_split(grad_proj, split) for split in range(splits)]
    mid_sums = [orders[place % 2][1](sums) for place, sums in enumerate(mid_sums)]
    text_sum = plane_sum(text_terms, bf16)
    (grad_proj, mid_sums, text_sum) = lax.optimization_barrier((grad_proj, mid_sums, text_sum))
    grad_hidden_one = sum(
        dot(grad_proj[split][place], qkv_full[place][split], NT)
        for place in range(ranks)
        for split in range(splits)
    )
    grad_hidden_one = dot(grad_hidden_one.astype(bf16), turn, NT)
    grad_shift_one = jnp.sum(grad_hidden_one, axis=0)
    grad_scale_one = jnp.sum(grad_hidden_one * normed_one, axis=0)
    grad_latents = grad_one + norm_back(
        grad_hidden_one * (1.0 + scale_one), normed_one, inverse_one
    )
    grad_latents = grad_latents.astype(bf16).reshape(latents.shape)
    grad_latents, up_sum = tie(grad_latents, up_sum)
    grad_latents = in_order(give_back(list(grad_latents), "lat"), "lat")

    time_terms = jnp.stack(
        (
            grad_shift_one,
            grad_scale_one,
            grad_gate_one,
            grad_shift_two,
            grad_scale_two,
            grad_gate_two,
        )
    )
    time_turn = lax.dot_general(
        time_terms, turn.astype(f32), NN, precision=lax.Precision.HIGHEST
    )
    table_terms = jnp.pad(time_turn.T, ((0, 0), (3 * edge, piece_width - 3 * edge - 6)))
    one_sums = [
        kept_sums(
            hidden_one,
            [grad_proj[split][place] for split in range(splits)],
            table_terms if place == 0 else None,
        )
        for place in range(ranks)
    ]
    one_sums = [orders[place % 2][0](sums) for place, sums in enumerate(one_sums)]
    one_sums = [sum_lat(orders[place % 2][1](sums)) for place, sums in enumerate(one_sums)]
    key_sum, val_sum, cq_sum, co_sum, out_sum = (sum_lat(sums)[:, :part] for sums in mid_sums)
    grad_time = over_latents(plane_sum(time_terms, f32)).reshape(-1, 6 * width)
    grad_text = over_latents(text_sum.astype(bf16)).astype(f32)
    grad_qkv = jnp.stack(
        [sums[:, : 3 * edge].reshape(share, 3, edge) for sums in one_sums], axis=2
    ).reshape(share, 3, part)
    return (
        result_back,
        grad_latents.astype(f32),
        grad_text,
        grad_time,
        one_sums[0][:, 3 * edge : 3 * edge + 6].T,
        grad_qkv,
        out_sum.T,
        cq_sum,
        jnp.stack((key_sum, val_sum), axis=1),
        co_sum.T,
        up_sum,
        down_sum.T,
    )


def solution(mesh):
    def run(latents, text, time_vector, table, w_qkv, *others):
        fsdp, context, tensor = (mesh.shape[name] for name in ("fsdp", "context", "tensor"))
        lat = latents.shape[0] // fsdp
        group = context // lat
        ranks = math.gcd(group, w_qkv.shape[2] // (tensor * HEAD_DIM))
        sizes = (fsdp, lat, group // ranks, ranks, tensor)
        finer = Mesh(mesh.devices.reshape(sizes), ("fsdp", "lat", "sr", "hr", "tensor"))
        line = ("lat", "sr", "hr")
        shard = ("fsdp",) + line
        tokens = P("fsdp", line + ("tensor",), None)
        by_row = P(shard, "tensor")
        by_row3 = P(shard, None, "tensor")
        by_column = P("tensor", shard)
        weights = (by_row3, by_column, by_row, by_row3, by_column, by_row, by_column)
        return jax.shard_map(
            local,
            mesh=finer,
            in_specs=(tokens, P("fsdp", None, None), P("fsdp", None), P(None, shard))
            + weights
            + (tokens,),
            out_specs=(tokens, tokens, P("fsdp", None, None), P("fsdp", None), P(None, shard))
            + weights,
            check_vma=False,
        )(latents, text, time_vector, table, w_qkv, *others)

    return run
```

```python
import math
from functools import partial

import jax
import jax.numpy as jnp
from jax import lax
from jax.experimental import pallas as pl
from jax.experimental.pallas import tpu as pltpu
from jax.sharding import Mesh
from jax.sharding import PartitionSpec as P

HEAD_DIM = 72
EPSILON = 1e-06
LANES = 128
FACTOR = HEAD_DIM ** (-0.5)
FACTOR2 = FACTOR * math.log2(math.e)
VMEM_LIMIT = 56 * 1024 * 1024

f32 = jnp.float32
bf16 = jnp.bfloat16

NT = (((1,), (1,)), ((), ()))
NN = (((1,), (0,)), ((), ()))
TN = (((0,), (0,)), ((), ()))

ROW = ("sr", "hr")
EVERY = ("tensor", "fsdp", "lat", "sr", "hr")
PLANE = ("sr", "hr", "tensor")
HEAD_GROUP = ("hr", "tensor")


def dot(left, right, dims=NN):
    return lax.dot_general(left, right, dims, preferred_element_type=f32)


def norm_parts(values):
    center = values - jnp.mean(values, axis=-1, keepdims=True)
    inverse = lax.rsqrt(jnp.mean(center * center, axis=-1, keepdims=True) + EPSILON)
    return (center * inverse, inverse)


def norm_back(grad_hat, normed, inverse):
    first = jnp.mean(grad_hat, axis=-1, keepdims=True)
    second = jnp.mean(grad_hat * normed, axis=-1, keepdims=True)
    return inverse * (grad_hat - first - normed * second)


def send_xor(piece, axes, step):
    size = lax.axis_size(axes)
    return lax.ppermute(piece, axes, [(rank, rank ^ step) for rank in range(size)])


def pick(stack, index):
    return lax.dynamic_index_in_dim(stack, index, 0, keepdims=False)


def exchange(piece_for, axes):
    me = lax.axis_index(axes)
    got = [piece_for(me)]
    for step in range(1, lax.axis_size(axes)):
        got.append(send_xor(piece_for(jnp.bitwise_xor(me, step)), axes, step))
    return got


def give_back(pieces, axes):
    return [send_xor(piece, axes, step) if step else piece for step, piece in enumerate(pieces)]


def in_order(pieces, axes):
    me = lax.axis_index(axes)
    places = range(len(pieces))
    return jnp.stack([choose(pieces, jnp.bitwise_xor(me, place)) for place in places])


def choose(pieces, index):
    out = pieces[0]
    for place in range(1, len(pieces)):
        out = jnp.where(index == place, pieces[place], out)
    return out


def plane_sum(values, dtype):
    sent = values.astype(dtype)
    total = sent.astype(f32)
    for step in range(1, lax.axis_size(PLANE)):
        total += send_xor(sent, PLANE, step).astype(f32)
    return total


def over_latents(values):
    return in_order(give_back([values] * lax.axis_size("lat"), "lat"), "lat")


def tie(first, second):
    return lax.optimization_barrier((first, second))


def attend_kernel(heads, chunks, own, *refs):
    pieces = refs[:chunks]
    low_refs = refs[chunks : chunks + own]
    att_ref, lse_ref, queries, keys, vals, lows, column = refs[chunks + own :]
    edge = heads * HEAD_DIM
    index = pl.program_id(0)
    block = att_ref.shape[1]

    @pl.when(index == 0)
    def _():
        lane = lax.broadcasted_iota(jnp.int32, vals.shape[1:], 1)
        column[...] = jnp.zeros_like(column)
        for head in range(heads):
            vals[head] = jnp.where(lane == HEAD_DIM, 1.0, 0.0).astype(bf16)
            low = head * HEAD_DIM
            for number, piece in enumerate(pieces):
                count = piece.shape[0]
                rows = slice(number * count, (number + 1) * count)
                if number < own:
                    queries[head, rows] = piece[:, low : low + HEAD_DIM]
                keys[head, rows] = piece[:, edge + low : edge + low + HEAD_DIM]
                vals[head, rows, :HEAD_DIM] = piece[:, 2 * edge + low : 2 * edge + low + HEAD_DIM]

    mine = pl.ds(pl.multiple_of(index * block, block), block)

    def score(head):
        return dot(queries[head, mine, :], keys[head], NT)

    ahead = score(0)
    for head in range(heads):
        scores = ahead
        if head + 1 < heads:
            ahead = score(head + 1)
        top = jnp.max(scores, axis=1, keepdims=True) * FACTOR2
        weights = jnp.exp2(scores * FACTOR2 - top).astype(bf16)
        out = dot(weights, vals[head])
        total = out[:, HEAD_DIM : HEAD_DIM + 1]
        out = out[:, :HEAD_DIM] / total
        att_ref[head] = out
        lows[head, mine, :] = out.astype(bf16)
        column[:, head : head + 1] = top + jnp.log2(total)
    lse_ref[...] = column[...].T[: lse_ref.shape[0]]

    @pl.when(index == pl.num_programs(0) - 1)
    def _():
        for head in range(heads):
            low = head * HEAD_DIM
            for number, ref in enumerate(low_refs):
                count = ref.shape[0]
                ref[:, low : low + HEAD_DIM] = lows[head, number * count : (number + 1) * count, :]


def whole_block(shape):
    return pl.BlockSpec(shape, lambda i: (0,) * len(shape))


def attend(pieces, own, heads):
    count, width = pieces[0].shape
    rows, total = own * count, len(pieces) * count
    block = min(256, rows)
    edge = heads * HEAD_DIM
    slots = -(-heads // 8) * 8
    out = pl.pallas_call(
        partial(attend_kernel, heads, len(pieces), own),
        grid=(rows // block,),
        in_specs=[whole_block((count, width))] * len(pieces),
        out_specs=[whole_block((count, edge))] * own
        + [
            pl.BlockSpec((heads, block, HEAD_DIM), lambda i: (0, i, 0)),
            pl.BlockSpec((slots, block), lambda i: (0, i)),
        ],
        out_shape=[jax.ShapeDtypeStruct((count, edge), bf16)] * own
        + [
            jax.ShapeDtypeStruct((heads, rows, HEAD_DIM), f32),
            jax.ShapeDtypeStruct((slots, rows), f32),
        ],
        scratch_shapes=[
            pltpu.VMEM((heads, rows, HEAD_DIM), bf16),
            pltpu.VMEM((heads, total, HEAD_DIM), bf16),
            pltpu.VMEM((heads, total, LANES), bf16),
            pltpu.VMEM((heads, rows, HEAD_DIM), bf16),
            pltpu.VMEM((block, LANES), f32),
        ],
        cost_estimate=pl.CostEstimate(
            flops=8 * heads * rows * total * LANES,
            transcendentals=heads * rows * total,
            bytes_accessed=4 * total * width,
        ),
        compiler_params=pltpu.CompilerParams(vmem_limit_bytes=VMEM_LIMIT),
    )(*pieces)
    return (out[:own], out[own], out[own + 1])


def attend_back_kernel(heads, chunk, chunks, own, *refs):
    pieces = refs[:chunks]
    grad_refs = refs[chunks : chunks + own]
    att_ref, lse_ref = refs[chunks + own : chunks + own + 2]
    outs = refs[chunks + own + 2 : 2 * chunks + own + 2]
    queries, keys, vals, grads, turned, dq, dk, dv, column = refs[2 * chunks + own + 2 :]
    edge = heads * HEAD_DIM
    index = pl.program_id(0)
    block = att_ref.shape[1]
    total = keys.shape[1]

    @pl.when(index == 0)
    def _():
        turned[...] = jnp.zeros_like(turned)
        column[...] = jnp.zeros_like(column)
        dk[...] = jnp.zeros_like(dk)
        dv[...] = jnp.zeros_like(dv)
        for head in range(heads):
            low = head * HEAD_DIM
            for number, piece in enumerate(pieces):
                count = piece.shape[0]
                rows = slice(number * count, (number + 1) * count)
                if number < own:
                    queries[head, rows] = piece[:, low : low + HEAD_DIM]
                    grads[head, rows] = grad_refs[number][:, low : low + HEAD_DIM]
                key = piece[:, edge + low : edge + low + HEAD_DIM]
                keys[head, rows] = key
                turned[head, :HEAD_DIM, rows] = key.astype(f32).T.astype(bf16)
                vals[head, rows] = piece[:, 2 * edge + low : 2 * edge + low + HEAD_DIM]

    mine = pl.ds(pl.multiple_of(index * block, block), block)
    for head in range(heads):
        column[:, head : head + 1] = jnp.sum(
            att_ref[head] * grads[head, mine, :].astype(f32), axis=1, keepdims=True
        )
    deltas = column[...].T
    for head in range(heads):
        query = queries[head, mine, :]
        grad = grads[head, mine, :]
        lse = lse_ref[head : head + 1, :]
        delta = deltas[head : head + 1, :]
        turned_grad = jnp.zeros((turned.shape[1], block), f32)
        for start in range(0, total, chunk):
            part = slice(start, start + chunk)
            scores = dot(keys[head, part, :], query, NT)
            grad_probs = dot(vals[head, part, :], grad, NT)
            probs = jnp.exp2(scores * FACTOR2 - lse)
            grad_scores = (probs * (grad_probs - delta)).astype(bf16)
            dv[head, part, :] += dot(probs.astype(bf16), grad)
            dk[head, part, :] += dot(grad_scores, query)
            turned_grad += dot(turned[head, :, part], grad_scores)
        dq[head, mine, :] = (turned_grad.T[:, :HEAD_DIM] * FACTOR).astype(bf16)

    @pl.when(index == pl.num_programs(0) - 1)
    def _():
        for number, ref in enumerate(outs):
            count = ref.shape[0]
            rows = slice(number * count, (number + 1) * count)
            ref[...] = jnp.zeros_like(ref)
            for head in range(heads):
                low = head * HEAD_DIM
                if number < own:
                    ref[:, low : low + HEAD_DIM] = dq[head, rows]
                ref[:, edge + low : edge + low + HEAD_DIM] = (dk[head, rows] * FACTOR).astype(bf16)
                ref[:, 2 * edge + low : 2 * edge + low + HEAD_DIM] = dv[head, rows].astype(bf16)


def attend_back(pieces, own, grads, att, lse, heads):
    count, width = pieces[0].shape
    rows, total = own * count, len(pieces) * count
    block = min(256, rows)
    edge = heads * HEAD_DIM
    slots = lse.shape[0]
    return pl.pallas_call(
        partial(attend_back_kernel, heads, min(512, total), len(pieces), own),
        grid=(rows // block,),
        in_specs=[whole_block((count, width))] * len(pieces)
        + [whole_block((count, edge))] * own
        + [
            pl.BlockSpec((heads, block, HEAD_DIM), lambda i: (0, i, 0)),
            pl.BlockSpec((slots, block), lambda i: (0, i)),
        ],
        out_specs=[whole_block((count, width))] * len(pieces),
        out_shape=[jax.ShapeDtypeStruct((count, width), bf16)] * len(pieces),
        scratch_shapes=[
            pltpu.VMEM((heads, rows, HEAD_DIM), bf16),
            pltpu.VMEM((heads, total, HEAD_DIM), bf16),
            pltpu.VMEM((heads, total, HEAD_DIM), bf16),
            pltpu.VMEM((heads, rows, HEAD_DIM), bf16),
            pltpu.VMEM((heads, LANES, total), bf16),
            pltpu.VMEM((heads, rows, HEAD_DIM), bf16),
            pltpu.VMEM((heads, total, HEAD_DIM), f32),
            pltpu.VMEM((heads, total, HEAD_DIM), f32),
            pltpu.VMEM((block, LANES), f32),
        ],
        cost_estimate=pl.CostEstimate(
            flops=20 * heads * rows * total * LANES,
            transcendentals=heads * rows * total,
            bytes_accessed=8 * total * width,
        ),
        compiler_params=pltpu.CompilerParams(vmem_limit_bytes=VMEM_LIMIT),
    )(*pieces, *grads, att, lse)


def head_lanes(part):
    return [slice(low, low + HEAD_DIM) for low in range(0, part, HEAD_DIM)]


def cross_kernel(part, splits, *refs):
    q_refs, k_refs, v_refs, out_refs = (refs[splits * i : splits * (i + 1)] for i in range(4))
    for q_ref, k_ref, v_ref, out_ref in zip(q_refs, k_refs, v_refs, out_refs):
        fill = out_ref.shape[1] - part
        if fill:
            out_ref[:, part:] = jnp.zeros((out_ref.shape[0], fill), bf16)
        for lanes in head_lanes(part):
            scores = dot(q_ref[:, lanes], k_ref[:, lanes], NT) * FACTOR
            weights = jnp.exp(scores - jnp.max(scores, axis=1, keepdims=True))
            probs = weights / jnp.sum(weights, axis=1, keepdims=True)
            out_ref[:, lanes] = dot(probs.astype(bf16), v_ref[:, lanes]).astype(bf16)


def cross(queries, keys, values, part):
    splits = len(queries)
    rows, width = queries[0].shape
    texts = keys[0].shape[0]
    block = min(512, rows)
    split = pl.BlockSpec((block, width), lambda i: (i, 0))
    return pl.pallas_call(
        partial(cross_kernel, part, splits),
        grid=(rows // block,),
        in_specs=[split] * splits + [whole_block((texts, width))] * (2 * splits),
        out_specs=[split] * splits,
        out_shape=[jax.ShapeDtypeStruct((rows, width), bf16)] * splits,
        compiler_params=pltpu.CompilerParams(vmem_limit_bytes=VMEM_LIMIT),
    )(*queries, *keys, *values)


def cross_back_kernel(part, splits, *refs):
    q_refs, k_refs, v_refs, grad_refs, dq_refs, dk_refs, dv_refs, dk_sums, dv_sums = (
        refs[splits * i : splits * (i + 1)] for i in range(9)
    )
    first = pl.program_id(0) == 0
    last = pl.program_id(0) == pl.num_programs(0) - 1
    for q_ref, k_ref, v_ref, grad_ref, dq_ref, dk, dv in zip(
        q_refs, k_refs, v_refs, grad_refs, dq_refs, dk_sums, dv_sums
    ):

        @pl.when(first)
        def _():
            dk[...] = jnp.zeros_like(dk)
            dv[...] = jnp.zeros_like(dv)

        fill = dq_ref.shape[1] - part
        if fill:
            dq_ref[:, part:] = jnp.zeros((dq_ref.shape[0], fill), bf16)
        for lanes in head_lanes(part):
            query = q_ref[:, lanes]
            key = k_ref[:, lanes]
            grad = grad_ref[:, lanes]
            scores = dot(query, key, NT) * FACTOR
            weights = jnp.exp(scores - jnp.max(scores, axis=1, keepdims=True))
            probs = weights / jnp.sum(weights, axis=1, keepdims=True)
            grad_probs = dot(grad, v_ref[:, lanes], NT)
            delta = jnp.sum(probs * grad_probs, axis=1, keepdims=True)
            grad_scores = (probs * (grad_probs - delta)).astype(bf16)
            dq_ref[:, lanes] = (dot(grad_scores, key) * FACTOR).astype(bf16)
            dk[:, lanes] += dot(grad_scores, query, TN)
            dv[:, lanes] += dot(probs.astype(bf16), grad, TN)

    @pl.when(last)
    def _():
        for dk_ref, dv_ref, dk, dv in zip(dk_refs, dv_refs, dk_sums, dv_sums):
            dk_ref[...] = (dk[...] * FACTOR).astype(bf16)
            dv_ref[...] = dv[...].astype(bf16)


def cross_back(queries, keys, values, grads, part):
    splits = len(queries)
    rows, width = queries[0].shape
    texts = keys[0].shape[0]
    block = min(512, rows)
    whole = whole_block((texts, width))
    split = pl.BlockSpec((block, width), lambda i: (i, 0))
    out = pl.pallas_call(
        partial(cross_back_kernel, part, splits),
        grid=(rows // block,),
        in_specs=[split] * splits + [whole] * (2 * splits) + [split] * splits,
        out_specs=[split] * splits + [whole] * (2 * splits),
        out_shape=[jax.ShapeDtypeStruct((rows, width), bf16)] * splits
        + [jax.ShapeDtypeStruct((texts, width), bf16)] * (2 * splits),
        scratch_shapes=[pltpu.VMEM((texts, width), f32)] * (2 * splits),
        compiler_params=pltpu.CompilerParams(vmem_limit_bytes=VMEM_LIMIT),
    )(*queries, *keys, *values, *grads)
    return (out[:splits], out[splits : 2 * splits], out[2 * splits :])


def assemble_kernel(plan, count, *refs):
    sources, outs, sems = refs[:count], refs[count:-1], refs[-1]
    copies = []
    for number, (source, start, rows, column, size, place, row, shift) in enumerate(plan):
        copies.append(
            pltpu.make_async_copy(
                sources[source].at[pl.ds(start, rows), pl.ds(column, size)],
                outs[place].at[pl.ds(row, rows), pl.ds(shift, size)],
                sems.at[number],
            )
        )
    for copy in copies:
        copy.start()
    for copy in copies:
        copy.wait()


def lay(sources, plan, shapes):
    anywhere = pl.BlockSpec(memory_space=pl.ANY)
    return list(
        pl.pallas_call(
            partial(assemble_kernel, plan, len(sources)),
            in_specs=[anywhere] * len(sources),
            out_specs=[pl.BlockSpec(memory_space=pltpu.VMEM)] * len(shapes),
            out_shape=[jax.ShapeDtypeStruct(shape, bf16) for shape in shapes],
            scratch_shapes=[pltpu.SemaphoreType.DMA((len(plan),))],
            compiler_params=pltpu.CompilerParams(vmem_limit_bytes=VMEM_LIMIT),
        )(*sources)
    )


def assemble(stacks):
    sources = [piece for stack in stacks for piece in stack]
    plan, shapes = [], []
    for stack in stacks:
        row, width = 0, stack[0].shape[1]
        for piece in stack:
            plan.append((len(plan), 0, piece.shape[0], 0, width, len(shapes), row, 0))
            row += piece.shape[0]
        shapes.append((row, width))
    return lay(sources, plan, shapes)


def cut(source, rows, columns):
    grid = [
        (place, row) for place in range(source.shape[1] // columns) for row in range(source.shape[0] // rows)
    ]
    plan = [
        (0, row * rows, rows, place * columns, columns, number, 0, 0)
        for number, (place, row) in enumerate(grid)
    ]
    out = lay([source], plan, [(rows, columns)] * len(grid))
    count = source.shape[0] // rows
    return [out[place : place + count] for place in range(0, len(out), count)]


def with_others(piece, axes):
    return [piece] + [send_xor(piece, axes, step) for step in range(1, lax.axis_size(axes))]


def gather(shard, tensor_first):
    start = jnp.concatenate(with_others(shard, "lat"))
    if tensor_first and lax.axis_size("tensor") * lax.axis_size(ROW) <= 8:
        stacks = [with_others(piece, ROW) for piece in with_others(start, "tensor")]
    else:
        half = assemble([with_others(start, ROW)])[0]
        stacks = [[piece] for piece in with_others(half, "tensor")]
    cores = range(1, lax.axis_size("fsdp"))
    stacks = [
        stack + [send_xor(piece, "fsdp", step) for step in cores for piece in stack] for stack in stacks
    ]
    return assemble(stacks), start


def gather_all(shard):
    return lax.all_gather(shard, EVERY, axis=shard.ndim - 2, tiled=True)


def scatter_all(pack):
    return lax.psum_scatter(pack, EVERY, scatter_dimension=0, tiled=True).astype(f32)


def sum_pieces(pieces, axes, dtype=bf16):
    total = pieces[0].astype(f32)
    for step in range(1, len(pieces)):
        total += send_xor(pieces[step], axes, step).astype(f32)
    return total.astype(dtype)


def sum_blocks(pack, axes, dtype=bf16):
    count = lax.axis_size(axes)
    size = pack.shape[0] // count
    blocks = [pack[place * size : (place + 1) * size] for place in range(count)]
    return sum_pieces(blocks, axes, dtype)


def pack_for(first, grads):
    splits, cores, ranks = (lax.axis_size(axes) for axes in ("tensor", "fsdp", ROW))
    rows, columns = grads[0][0].shape
    size = rows // cores // ranks
    plan = []
    for piece, row in enumerate(grads):
        for split in range(splits):
            for core in range(cores):
                for rank in range(ranks):
                    place = split * ranks + rank if first == "tensor" else rank * splits + split
                    source = (piece * splits + split, (core * ranks + rank) * size, size, 0, columns)
                    plan.append(source + (core, place * size, piece * columns))
    sources = [values for row in grads for values in row]
    return lay(sources, plan, [(splits * rows // cores, columns * len(grads))] * cores)


def pack_grid(grads):
    rows, columns = grads[0][0].shape
    count = len(grads[0])
    plan = [
        (place * count + row, 0, rows, 0, columns, 0, row * rows, place * columns)
        for place in range(len(grads))
        for row in range(count)
    ]
    return lay([values for row in grads for values in row], plan, [(rows * count, columns * len(grads))])[0]


def own_order(share, width):
    cores, lats, rows = (lax.axis_size(axes) for axes in ("fsdp", "lat", ROW))
    place = lax.iota(jnp.int32, width)
    block, rest = place // share, place % share
    lat = jnp.bitwise_xor(block % lats, lax.axis_index("lat"))
    row = jnp.bitwise_xor(block // lats % rows, lax.axis_index(ROW))
    core = jnp.bitwise_xor(block // (lats * rows), lax.axis_index("fsdp"))
    natural = ((core * lats + lat) * rows + row) * share + rest
    return (lax.broadcasted_iota(jnp.int32, (width, width), 0) == natural[None, :]).astype(bf16)


def local(
    latents, text, time_vector, table, w_qkv, w_out, w_cq, w_ckv, w_co, w_up, w_down, cotangent
):
    width = latents.shape[2]
    share = w_cq.shape[0]
    part = w_cq.shape[1]
    inner_part = w_up.shape[1]
    splits = lax.axis_size("tensor")
    ranks = lax.axis_size("hr")
    halves = lax.axis_size("sr")
    edge = part // ranks
    heads = edge // HEAD_DIM
    groups = ranks * splits
    piece_width = -(-(3 * edge + 6) // LANES) * LANES
    wide = -(-part // LANES) * LANES
    slot = lax.axis_index("lat")
    rank = lax.axis_index("hr")

    def padded(values):
        return jnp.pad(values, ((0, 0), (0, wide - part)))

    latents_got = exchange(partial(pick, latents), "lat")
    mid_shard = jnp.concatenate(
        [padded(piece) for piece in (w_out.T, w_ckv[:, 0], w_ckv[:, 1], w_cq, w_co.T)], axis=1
    )
    shard_qkv = jnp.transpose(w_qkv.reshape(share, 3, ranks, edge), (2, 0, 1, 3)).reshape(
        ranks, share, 3 * edge
    )
    fill = jnp.pad(table.T, ((0, 0), (0, piece_width - 3 * edge - 6)))
    qkv_got = [
        gather(jnp.concatenate((shard_qkv[place], fill), axis=1), place % 2 == 0)
        for place in range(ranks)
    ]
    qkv_full = [full for full, _ in qkv_got]
    mid_shard = lax.optimization_barrier([mid_shard] + [start for _, start in qkv_got])[0]
    mid_full = gather_all(mid_shard)
    two_full = gather_all(jnp.stack((w_up, w_down.T)))

    turn = own_order(share, width)
    residual = jnp.concatenate(latents_got, axis=0).astype(f32)
    cotangent, _ = tie(cotangent, qkv_full[0][0])
    grad_three = jnp.concatenate(exchange(partial(pick, cotangent), "lat"), axis=0).astype(f32)
    rows = residual.shape[0]
    caption = pick(text, slot)
    table_full = dot(qkv_full[0][0][:, 3 * edge : 3 * edge + 6].T, turn, NT)
    modulate = table_full + pick(time_vector, slot).astype(f32).reshape(6, width)
    shift_one, scale_one, gate_one, shift_two, scale_two, gate_two = (
        modulate[row : row + 1] for row in range(6)
    )

    normed_one, inverse_one = norm_parts(residual)
    hidden_one = (normed_one * (1.0 + scale_one) + shift_one).astype(bf16)
    hidden_turn = dot(hidden_one, turn).astype(bf16)
    mixed = [None] * groups
    for split in range(splits):
        pieces = [dot(hidden_turn, full[split]).astype(bf16) for full in qkv_full]
        for other in range(ranks):
            step = other * splits + split
            piece = choose(pieces, jnp.bitwise_xor(rank, other))
            mixed[step] = send_xor(piece, HEAD_GROUP, step) if step else piece
    for step in range(1, halves):
        mixed += [send_xor(piece, "sr", step) for piece in mixed[:groups]]
    att_low, att_wide, logsum = attend(mixed, groups, heads)

    def by_split(pieces, split):
        own = [pieces[other * splits + split] for other in range(ranks)]
        return [choose(own, jnp.bitwise_xor(rank, place)) for place in range(ranks)]

    att_back = give_back(att_low, HEAD_GROUP)
    att_own = [
        padded(jnp.concatenate(by_split(att_back, split), axis=1)) for split in range(splits)
    ]
    col = lax.axis_index("tensor")

    def from_own(pieces):
        return [choose(pieces, jnp.bitwise_xor(col, place)) for place in range(splits)]

    att = from_own(att_own)
    out_full, key_full, val_full, cq_full, co_full = cut(mid_full, width, wide)
    up_full, down_full = (
        [two_full[place, split * width : (split + 1) * width] for split in range(splits)]
        for place in range(2)
    )

    out_one = sum(dot(att[split], out_full[split], NT) for split in range(splits))
    after_one = residual + gate_one * out_one
    mid_low = after_one.astype(bf16)
    cross_q = [dot(mid_low, full).astype(bf16) for full in cq_full]
    cross_k = [dot(caption, full).astype(bf16) for full in key_full]
    cross_v = [dot(caption, full).astype(bf16) for full in val_full]
    cross_low = cross(cross_q, cross_k, cross_v, part)
    out_two = sum(dot(cross_low[split], co_full[split], NT) for split in range(splits))
    after_two = after_one + out_two
    normed_two, inverse_two = norm_parts(after_two)
    hidden_two = (normed_two * (1.0 + scale_two) + shift_two).astype(bf16)
    inner = [dot(hidden_two, up_full[split]) for split in range(splits)]
    active = [jax.nn.gelu(values, approximate=True).astype(bf16) for values in inner]
    out_three = sum(dot(active[split], down_full[split], NT) for split in range(splits))
    result = (after_two + gate_two * out_three).astype(bf16)
    result_back = in_order(give_back(list(result.reshape(latents.shape)), "lat"), "lat")

    grad_gate_two = jnp.sum(grad_three * out_three, axis=0)
    grad_z = (gate_two * grad_three).astype(bf16)
    grad_inner = []
    for split in range(splits):
        grad_active = dot(grad_z, down_full[split])
        _, pull = jax.vjp(partial(jax.nn.gelu, approximate=True), inner[split])
        grad_inner.append(pull(grad_active)[0].astype(bf16))
    down_sum = scatter_all(pack_grid([[dot(grad_z, piece, TN).astype(bf16) for piece in active]]))
    up_sum = scatter_all(
        pack_grid([[dot(hidden_two, piece, TN).astype(bf16) for piece in grad_inner]])
    )
    grad_hidden_two = sum(dot(grad_inner[split], up_full[split], NT) for split in range(splits))
    grad_shift_two = jnp.sum(grad_hidden_two, axis=0)
    grad_scale_two = jnp.sum(grad_hidden_two * normed_two, axis=0)
    grad_two = grad_three + norm_back(grad_hidden_two * (1.0 + scale_two), normed_two, inverse_two)

    grad_out_two = grad_two.astype(bf16)
    grad_cross = [dot(grad_out_two, full).astype(bf16) for full in co_full]
    grad_cq, grad_ck, grad_cv = cross_back(cross_q, cross_k, cross_v, grad_cross, part)
    grad_one = grad_two + sum(dot(grad_cq[split], cq_full[split], NT) for split in range(splits))
    text_terms = sum(
        dot(grad_ck[split], key_full[split], NT) + dot(grad_cv[split], val_full[split], NT)
        for split in range(splits)
    )

    grad_gate_one = jnp.sum(grad_one * out_one, axis=0)
    grad_out_one = (gate_one * grad_one).astype(bf16)
    grad_att = from_own([dot(grad_out_one, full).astype(bf16) for full in out_full])
    grad_heads = [None] * groups
    for split in range(splits):
        cuts = [grad_att[split][:, place * edge : (place + 1) * edge] for place in range(ranks)]
        for other in range(ranks):
            step = other * splits + split
            piece = choose(cuts, jnp.bitwise_xor(rank, other))
            grad_heads[step] = send_xor(piece, HEAD_GROUP, step) if step else piece
    caption_turn = dot(caption, turn).astype(bf16)
    mid_grads = [
        [dot(left, right, TN).astype(bf16) for right in rights]
        for left, rights in (
            (caption_turn, from_own(grad_ck)),
            (caption_turn, from_own(grad_cv)),
            (dot(mid_low, turn).astype(bf16), from_own(grad_cq)),
            (dot(grad_out_two, turn).astype(bf16), from_own(cross_low)),
            (dot(grad_out_one, turn).astype(bf16), att_own),
        )
    ]
    pack_a = sum_pieces(pack_for("tensor", mid_grads[:3]), "fsdp")
    pack_b = sum_pieces(pack_for(ROW, mid_grads[3:]), "fsdp")
    (grad_heads[0], pack_a, pack_b, result_back) = lax.optimization_barrier(
        (grad_heads[0], pack_a, pack_b, result_back)
    )
    pack_a, pack_b = sum_blocks(pack_a, "tensor"), sum_blocks(pack_b, ROW)
    grad_mix = list(attend_back(mixed, groups, grad_heads, att_wide, logsum, heads))
    (grad_mix[0], pack_a, pack_b, down_sum) = lax.optimization_barrier(
        (grad_mix[0], pack_a, pack_b, down_sum)
    )
    for step in range(1, halves):
        for place in range(groups):
            more = send_xor(grad_mix[step * groups + place], "sr", step)
            grad_mix[place] = (grad_mix[place].astype(f32) + more.astype(f32)).astype(bf16)
    grad_proj = give_back(grad_mix[:groups], HEAD_GROUP)
    grad_proj = [by_split(grad_proj, split) for split in range(splits)]
    pack_a, pack_b = sum_blocks(pack_a, ROW), sum_blocks(pack_b, "tensor")
    text_sum = plane_sum(text_terms, bf16)
    (grad_proj, pack_a, pack_b, text_sum) = lax.optimization_barrier(
        (grad_proj, pack_a, pack_b, text_sum)
    )
    grad_hidden_one = sum(
        dot(grad_proj[split][place], qkv_full[place][split], NT)
        for place in range(ranks)
        for split in range(splits)
    )
    grad_hidden_one = dot(grad_hidden_one.astype(bf16), turn, NT)
    grad_shift_one = jnp.sum(grad_hidden_one, axis=0)
    grad_scale_one = jnp.sum(grad_hidden_one * normed_one, axis=0)
    grad_latents = grad_one + norm_back(
        grad_hidden_one * (1.0 + scale_one), normed_one, inverse_one
    )
    grad_latents = grad_latents.astype(bf16).reshape(latents.shape)
    grad_latents = in_order(give_back(list(grad_latents), "lat"), "lat")

    time_terms = jnp.stack(
        (
            grad_shift_one,
            grad_scale_one,
            grad_gate_one,
            grad_shift_two,
            grad_scale_two,
            grad_gate_two,
        )
    )
    table_terms = jnp.pad(time_terms.T, ((0, 0), (3 * edge, piece_width - 3 * edge - 6)))
    one_grads = []
    for place in range(ranks):
        rights = from_own([grad_proj[split][place] for split in range(splits)])
        grads = [dot(hidden_one, right, TN) for right in rights]
        if place == 0:
            grads = [grad + table_terms for grad in grads]
        one_grads.append([grad.astype(bf16) for grad in grads])
    pack_one, up_sum = tie(pack_grid(one_grads), up_sum)
    one_sum = scatter_all(pack_one)
    one_sums = [
        one_sum[:, place * piece_width : (place + 1) * piece_width] for place in range(ranks)
    ]
    pack_a, pack_b = sum_blocks(pack_a, "lat", f32), sum_blocks(pack_b, "lat", f32)
    key_sum, val_sum, cq_sum, co_sum, out_sum = (
        pack[:, place * wide : place * wide + part]
        for pack, count in ((pack_a, 3), (pack_b, 2))
        for place in range(count)
    )
    grad_time = over_latents(plane_sum(time_terms, f32)).reshape(-1, 6 * width)
    grad_text = over_latents(text_sum.astype(bf16)).astype(f32)
    grad_qkv = jnp.stack(
        [sums[:, : 3 * edge].reshape(share, 3, edge) for sums in one_sums], axis=2
    ).reshape(share, 3, part)
    return (
        result_back,
        grad_latents.astype(f32),
        grad_text,
        grad_time,
        one_sums[0][:, 3 * edge : 3 * edge + 6].T,
        grad_qkv,
        out_sum.T,
        cq_sum,
        jnp.stack((key_sum, val_sum), axis=1),
        co_sum.T,
        up_sum,
        down_sum.T,
    )


def solution(mesh):
    def run(latents, text, time_vector, table, w_qkv, *others):
        fsdp, context, tensor = (mesh.shape[name] for name in ("fsdp", "context", "tensor"))
        lat = latents.shape[0] // fsdp
        group = context // lat
        ranks = math.gcd(group, w_qkv.shape[2] // (tensor * HEAD_DIM))
        sizes = (fsdp, lat, group // ranks, ranks, tensor)
        finer = Mesh(mesh.devices.reshape(sizes), ("fsdp", "lat", "sr", "hr", "tensor"))
        line = ("lat", "sr", "hr")
        shard = ("fsdp",) + line
        tokens = P("fsdp", line + ("tensor",), None)
        by_row = P(shard, "tensor")
        by_row3 = P(shard, None, "tensor")
        by_column = P("tensor", shard)
        weights = (by_row3, by_column, by_row, by_row3, by_column, by_row, by_column)
        return jax.shard_map(
            local,
            mesh=finer,
            in_specs=(tokens, P("fsdp", None, None), P("fsdp", None), P(None, shard))
            + weights
            + (tokens,),
            out_specs=(tokens, tokens, P("fsdp", None, None), P("fsdp", None), P(None, shard))
            + weights,
            check_vma=False,
        )(latents, text, time_vector, table, w_qkv, *others)

    return run
```

```python
import math
from functools import partial

import jax
import jax.numpy as jnp
from jax import lax
from jax.experimental import pallas as pl
from jax.experimental.pallas import tpu as pltpu
from jax.sharding import Mesh
from jax.sharding import PartitionSpec as P

HEAD_DIM = 72
EPSILON = 1e-06
LANES = 128
FACTOR = HEAD_DIM ** (-0.5)
FACTOR2 = FACTOR * math.log2(math.e)
VMEM_LIMIT = 56 * 1024 * 1024

f32 = jnp.float32
bf16 = jnp.bfloat16

NT = (((1,), (1,)), ((), ()))
NN = (((1,), (0,)), ((), ()))
TN = (((0,), (0,)), ((), ()))

ROW = ("sr", "hr")
EVERY = ("tensor", "fsdp", "lat", "sr", "hr")
PLANE = ("sr", "hr", "tensor")
HEAD_GROUP = ("hr", "tensor")


def dot(left, right, dims=NN):
    return lax.dot_general(left, right, dims, preferred_element_type=f32)


def norm_parts(values):
    center = values - jnp.mean(values, axis=-1, keepdims=True)
    inverse = lax.rsqrt(jnp.mean(center * center, axis=-1, keepdims=True) + EPSILON)
    return (center * inverse, inverse)


def norm_back(grad_hat, normed, inverse):
    first = jnp.mean(grad_hat, axis=-1, keepdims=True)
    second = jnp.mean(grad_hat * normed, axis=-1, keepdims=True)
    return inverse * (grad_hat - first - normed * second)


def send_xor(piece, axes, step):
    size = lax.axis_size(axes)
    return lax.ppermute(piece, axes, [(rank, rank ^ step) for rank in range(size)])


def pick(stack, index):
    return lax.dynamic_index_in_dim(stack, index, 0, keepdims=False)


def exchange(piece_for, axes):
    me = lax.axis_index(axes)
    got = [piece_for(me)]
    for step in range(1, lax.axis_size(axes)):
        got.append(send_xor(piece_for(jnp.bitwise_xor(me, step)), axes, step))
    return got


def give_back(pieces, axes):
    return [send_xor(piece, axes, step) if step else piece for step, piece in enumerate(pieces)]


def in_order(pieces, axes):
    me = lax.axis_index(axes)
    places = range(len(pieces))
    return jnp.stack([choose(pieces, jnp.bitwise_xor(me, place)) for place in places])


def choose(pieces, index):
    out = pieces[0]
    for place in range(1, len(pieces)):
        out = jnp.where(index == place, pieces[place], out)
    return out


def plane_sum(values, dtype):
    sent = values.astype(dtype)
    total = sent.astype(f32)
    for step in range(1, lax.axis_size(PLANE)):
        total += send_xor(sent, PLANE, step).astype(f32)
    return total


def over_latents(values):
    return in_order(give_back([values] * lax.axis_size("lat"), "lat"), "lat")


def tie(first, second):
    return lax.optimization_barrier((first, second))


def attend_kernel(heads, chunks, own, *refs):
    pieces = refs[:chunks]
    low_refs = refs[chunks : chunks + own]
    att_ref, lse_ref, queries, keys, vals, lows, column = refs[chunks + own :]
    edge = heads * HEAD_DIM
    index = pl.program_id(0)
    block = att_ref.shape[1]

    @pl.when(index == 0)
    def _():
        lane = lax.broadcasted_iota(jnp.int32, vals.shape[1:], 1)
        column[...] = jnp.zeros_like(column)
        for head in range(heads):
            vals[head] = jnp.where(lane == HEAD_DIM, 1.0, 0.0).astype(bf16)
            low = head * HEAD_DIM
            for number, piece in enumerate(pieces):
                count = piece.shape[0]
                rows = slice(number * count, (number + 1) * count)
                if number < own:
                    queries[head, rows] = piece[:, low : low + HEAD_DIM]
                keys[head, rows] = piece[:, edge + low : edge + low + HEAD_DIM]
                vals[head, rows, :HEAD_DIM] = piece[:, 2 * edge + low : 2 * edge + low + HEAD_DIM]

    mine = pl.ds(pl.multiple_of(index * block, block), block)

    def score(head):
        return dot(queries[head, mine, :], keys[head], NT)

    ahead = score(0)
    for head in range(heads):
        scores = ahead
        if head + 1 < heads:
            ahead = score(head + 1)
        top = jnp.max(scores, axis=1, keepdims=True) * FACTOR2
        weights = jnp.exp2(scores * FACTOR2 - top).astype(bf16)
        out = dot(weights, vals[head])
        total = out[:, HEAD_DIM : HEAD_DIM + 1]
        out = out[:, :HEAD_DIM] / total
        att_ref[head] = out
        lows[head, mine, :] = out.astype(bf16)
        column[:, head : head + 1] = top + jnp.log2(total)
    lse_ref[...] = column[...].T[: lse_ref.shape[0]]

    @pl.when(index == pl.num_programs(0) - 1)
    def _():
        for head in range(heads):
            low = head * HEAD_DIM
            for number, ref in enumerate(low_refs):
                count = ref.shape[0]
                ref[:, low : low + HEAD_DIM] = lows[head, number * count : (number + 1) * count, :]


def whole_block(shape):
    return pl.BlockSpec(shape, lambda i: (0,) * len(shape))


def attend(pieces, own, heads):
    count, width = pieces[0].shape
    rows, total = own * count, len(pieces) * count
    block = min(256, rows)
    edge = heads * HEAD_DIM
    slots = -(-heads // 8) * 8
    out = pl.pallas_call(
        partial(attend_kernel, heads, len(pieces), own),
        grid=(rows // block,),
        in_specs=[whole_block((count, width))] * len(pieces),
        out_specs=[whole_block((count, edge))] * own
        + [
            pl.BlockSpec((heads, block, HEAD_DIM), lambda i: (0, i, 0)),
            pl.BlockSpec((slots, block), lambda i: (0, i)),
        ],
        out_shape=[jax.ShapeDtypeStruct((count, edge), bf16)] * own
        + [
            jax.ShapeDtypeStruct((heads, rows, HEAD_DIM), f32),
            jax.ShapeDtypeStruct((slots, rows), f32),
        ],
        scratch_shapes=[
            pltpu.VMEM((heads, rows, HEAD_DIM), bf16),
            pltpu.VMEM((heads, total, HEAD_DIM), bf16),
            pltpu.VMEM((heads, total, LANES), bf16),
            pltpu.VMEM((heads, rows, HEAD_DIM), bf16),
            pltpu.VMEM((block, LANES), f32),
        ],
        cost_estimate=pl.CostEstimate(
            flops=8 * heads * rows * total * LANES,
            transcendentals=heads * rows * total,
            bytes_accessed=4 * total * width,
        ),
        compiler_params=pltpu.CompilerParams(vmem_limit_bytes=VMEM_LIMIT),
    )(*pieces)
    return (out[:own], out[own], out[own + 1])


def attend_back_kernel(heads, chunk, chunks, own, *refs):
    pieces = refs[:chunks]
    grad_refs = refs[chunks : chunks + own]
    att_ref, lse_ref = refs[chunks + own : chunks + own + 2]
    outs = refs[chunks + own + 2 : 2 * chunks + own + 2]
    queries, keys, vals, grads, turned, dq, dk, dv, column = refs[2 * chunks + own + 2 :]
    edge = heads * HEAD_DIM
    index = pl.program_id(0)
    block = att_ref.shape[1]
    total = keys.shape[1]

    @pl.when(index == 0)
    def _():
        turned[...] = jnp.zeros_like(turned)
        column[...] = jnp.zeros_like(column)
        dk[...] = jnp.zeros_like(dk)
        dv[...] = jnp.zeros_like(dv)
        for head in range(heads):
            low = head * HEAD_DIM
            for number, piece in enumerate(pieces):
                count = piece.shape[0]
                rows = slice(number * count, (number + 1) * count)
                if number < own:
                    queries[head, rows] = piece[:, low : low + HEAD_DIM]
                    grads[head, rows] = grad_refs[number][:, low : low + HEAD_DIM]
                key = piece[:, edge + low : edge + low + HEAD_DIM]
                keys[head, rows] = key
                turned[head, :HEAD_DIM, rows] = key.astype(f32).T.astype(bf16)
                vals[head, rows] = piece[:, 2 * edge + low : 2 * edge + low + HEAD_DIM]

    mine = pl.ds(pl.multiple_of(index * block, block), block)
    for head in range(heads):
        column[:, head : head + 1] = jnp.sum(
            att_ref[head] * grads[head, mine, :].astype(f32), axis=1, keepdims=True
        )
    deltas = column[...].T
    for head in range(heads):
        query = queries[head, mine, :]
        grad = grads[head, mine, :]
        lse = lse_ref[head : head + 1, :]
        delta = deltas[head : head + 1, :]
        turned_grad = jnp.zeros((turned.shape[1], block), f32)
        for start in range(0, total, chunk):
            part = slice(start, start + chunk)
            scores = dot(keys[head, part, :], query, NT)
            grad_probs = dot(vals[head, part, :], grad, NT)
            probs = jnp.exp2(scores * FACTOR2 - lse)
            grad_scores = (probs * (grad_probs - delta)).astype(bf16)
            dv[head, part, :] += dot(probs.astype(bf16), grad)
            dk[head, part, :] += dot(grad_scores, query)
            turned_grad += dot(turned[head, :, part], grad_scores)
        dq[head, mine, :] = (turned_grad.T[:, :HEAD_DIM] * FACTOR).astype(bf16)

    @pl.when(index == pl.num_programs(0) - 1)
    def _():
        for number, ref in enumerate(outs):
            count = ref.shape[0]
            rows = slice(number * count, (number + 1) * count)
            ref[...] = jnp.zeros_like(ref)
            for head in range(heads):
                low = head * HEAD_DIM
                if number < own:
                    ref[:, low : low + HEAD_DIM] = dq[head, rows]
                ref[:, edge + low : edge + low + HEAD_DIM] = (dk[head, rows] * FACTOR).astype(bf16)
                ref[:, 2 * edge + low : 2 * edge + low + HEAD_DIM] = dv[head, rows].astype(bf16)


def attend_back(pieces, own, grads, att, lse, heads):
    count, width = pieces[0].shape
    rows, total = own * count, len(pieces) * count
    block = min(256, rows)
    edge = heads * HEAD_DIM
    slots = lse.shape[0]
    return pl.pallas_call(
        partial(attend_back_kernel, heads, min(512, total), len(pieces), own),
        grid=(rows // block,),
        in_specs=[whole_block((count, width))] * len(pieces)
        + [whole_block((count, edge))] * own
        + [
            pl.BlockSpec((heads, block, HEAD_DIM), lambda i: (0, i, 0)),
            pl.BlockSpec((slots, block), lambda i: (0, i)),
        ],
        out_specs=[whole_block((count, width))] * len(pieces),
        out_shape=[jax.ShapeDtypeStruct((count, width), bf16)] * len(pieces),
        scratch_shapes=[
            pltpu.VMEM((heads, rows, HEAD_DIM), bf16),
            pltpu.VMEM((heads, total, HEAD_DIM), bf16),
            pltpu.VMEM((heads, total, HEAD_DIM), bf16),
            pltpu.VMEM((heads, rows, HEAD_DIM), bf16),
            pltpu.VMEM((heads, LANES, total), bf16),
            pltpu.VMEM((heads, rows, HEAD_DIM), bf16),
            pltpu.VMEM((heads, total, HEAD_DIM), f32),
            pltpu.VMEM((heads, total, HEAD_DIM), f32),
            pltpu.VMEM((block, LANES), f32),
        ],
        cost_estimate=pl.CostEstimate(
            flops=20 * heads * rows * total * LANES,
            transcendentals=heads * rows * total,
            bytes_accessed=8 * total * width,
        ),
        compiler_params=pltpu.CompilerParams(vmem_limit_bytes=VMEM_LIMIT),
    )(*pieces, *grads, att, lse)


def head_lanes(part):
    return [slice(low, low + HEAD_DIM) for low in range(0, part, HEAD_DIM)]


def cross_kernel(part, splits, *refs):
    q_refs, k_refs, v_refs, out_refs = (refs[splits * i : splits * (i + 1)] for i in range(4))
    for q_ref, k_ref, v_ref, out_ref in zip(q_refs, k_refs, v_refs, out_refs):
        fill = out_ref.shape[1] - part
        if fill:
            out_ref[:, part:] = jnp.zeros((out_ref.shape[0], fill), bf16)
        for lanes in head_lanes(part):
            scores = dot(q_ref[:, lanes], k_ref[:, lanes], NT) * FACTOR
            weights = jnp.exp(scores - jnp.max(scores, axis=1, keepdims=True))
            probs = weights / jnp.sum(weights, axis=1, keepdims=True)
            out_ref[:, lanes] = dot(probs.astype(bf16), v_ref[:, lanes]).astype(bf16)


def cross(queries, keys, values, part):
    splits = len(queries)
    rows, width = queries[0].shape
    texts = keys[0].shape[0]
    block = min(512, rows)
    split = pl.BlockSpec((block, width), lambda i: (i, 0))
    return pl.pallas_call(
        partial(cross_kernel, part, splits),
        grid=(rows // block,),
        in_specs=[split] * splits + [whole_block((texts, width))] * (2 * splits),
        out_specs=[split] * splits,
        out_shape=[jax.ShapeDtypeStruct((rows, width), bf16)] * splits,
        compiler_params=pltpu.CompilerParams(vmem_limit_bytes=VMEM_LIMIT),
    )(*queries, *keys, *values)


def cross_back_kernel(part, splits, *refs):
    q_refs, k_refs, v_refs, grad_refs, dq_refs, dk_refs, dv_refs, dk_sums, dv_sums = (
        refs[splits * i : splits * (i + 1)] for i in range(9)
    )
    first = pl.program_id(0) == 0
    last = pl.program_id(0) == pl.num_programs(0) - 1
    for q_ref, k_ref, v_ref, grad_ref, dq_ref, dk, dv in zip(
        q_refs, k_refs, v_refs, grad_refs, dq_refs, dk_sums, dv_sums
    ):

        @pl.when(first)
        def _():
            dk[...] = jnp.zeros_like(dk)
            dv[...] = jnp.zeros_like(dv)

        fill = dq_ref.shape[1] - part
        if fill:
            dq_ref[:, part:] = jnp.zeros((dq_ref.shape[0], fill), bf16)
        for lanes in head_lanes(part):
            query = q_ref[:, lanes]
            key = k_ref[:, lanes]
            grad = grad_ref[:, lanes]
            scores = dot(query, key, NT) * FACTOR
            weights = jnp.exp(scores - jnp.max(scores, axis=1, keepdims=True))
            probs = weights / jnp.sum(weights, axis=1, keepdims=True)
            grad_probs = dot(grad, v_ref[:, lanes], NT)
            delta = jnp.sum(probs * grad_probs, axis=1, keepdims=True)
            grad_scores = (probs * (grad_probs - delta)).astype(bf16)
            dq_ref[:, lanes] = (dot(grad_scores, key) * FACTOR).astype(bf16)
            dk[:, lanes] += dot(grad_scores, query, TN)
            dv[:, lanes] += dot(probs.astype(bf16), grad, TN)

    @pl.when(last)
    def _():
        for dk_ref, dv_ref, dk, dv in zip(dk_refs, dv_refs, dk_sums, dv_sums):
            dk_ref[...] = (dk[...] * FACTOR).astype(bf16)
            dv_ref[...] = dv[...].astype(bf16)


def cross_back(queries, keys, values, grads, part):
    splits = len(queries)
    rows, width = queries[0].shape
    texts = keys[0].shape[0]
    block = min(512, rows)
    whole = whole_block((texts, width))
    split = pl.BlockSpec((block, width), lambda i: (i, 0))
    out = pl.pallas_call(
        partial(cross_back_kernel, part, splits),
        grid=(rows // block,),
        in_specs=[split] * splits + [whole] * (2 * splits) + [split] * splits,
        out_specs=[split] * splits + [whole] * (2 * splits),
        out_shape=[jax.ShapeDtypeStruct((rows, width), bf16)] * splits
        + [jax.ShapeDtypeStruct((texts, width), bf16)] * (2 * splits),
        scratch_shapes=[pltpu.VMEM((texts, width), f32)] * (2 * splits),
        compiler_params=pltpu.CompilerParams(vmem_limit_bytes=VMEM_LIMIT),
    )(*queries, *keys, *values, *grads)
    return (out[:splits], out[splits : 2 * splits], out[2 * splits :])


def assemble_kernel(plan, count, *refs):
    sources, outs, sems = refs[:count], refs[count:-1], refs[-1]
    copies = []
    for number, (source, start, rows, column, size, place, row, shift) in enumerate(plan):
        copies.append(
            pltpu.make_async_copy(
                sources[source].at[pl.ds(start, rows), pl.ds(column, size)],
                outs[place].at[pl.ds(row, rows), pl.ds(shift, size)],
                sems.at[number],
            )
        )
    for copy in copies:
        copy.start()
    for copy in copies:
        copy.wait()


def lay(sources, plan, shapes):
    anywhere = pl.BlockSpec(memory_space=pl.ANY)
    return list(
        pl.pallas_call(
            partial(assemble_kernel, plan, len(sources)),
            in_specs=[anywhere] * len(sources),
            out_specs=[pl.BlockSpec(memory_space=pltpu.VMEM)] * len(shapes),
            out_shape=[jax.ShapeDtypeStruct(shape, bf16) for shape in shapes],
            scratch_shapes=[pltpu.SemaphoreType.DMA((len(plan),))],
            compiler_params=pltpu.CompilerParams(vmem_limit_bytes=VMEM_LIMIT),
        )(*sources)
    )


def assemble(stacks):
    sources = [piece for stack in stacks for piece in stack]
    plan, shapes = [], []
    for stack in stacks:
        row, width = 0, stack[0].shape[1]
        for piece in stack:
            plan.append((len(plan), 0, piece.shape[0], 0, width, len(shapes), row, 0))
            row += piece.shape[0]
        shapes.append((row, width))
    return lay(sources, plan, shapes)


def cut(source, rows, columns):
    grid = [
        (place, row) for place in range(source.shape[1] // columns) for row in range(source.shape[0] // rows)
    ]
    plan = [
        (0, row * rows, rows, place * columns, columns, number, 0, 0)
        for number, (place, row) in enumerate(grid)
    ]
    out = lay([source], plan, [(rows, columns)] * len(grid))
    count = source.shape[0] // rows
    return [out[place : place + count] for place in range(0, len(out), count)]


def with_others(piece, axes):
    return [piece] + [send_xor(piece, axes, step) for step in range(1, lax.axis_size(axes))]


def gather(shard, tensor_first):
    start = jnp.concatenate(with_others(shard, "lat"))
    if tensor_first and lax.axis_size("tensor") * lax.axis_size(ROW) <= 8:
        stacks = [with_others(piece, ROW) for piece in with_others(start, "tensor")]
    else:
        half = assemble([with_others(start, ROW)])[0]
        stacks = [[piece] for piece in with_others(half, "tensor")]
    cores = range(1, lax.axis_size("fsdp"))
    stacks = [
        stack + [send_xor(piece, "fsdp", step) for step in cores for piece in stack] for stack in stacks
    ]
    return assemble(stacks), start


def gather_all(shard):
    return lax.all_gather(shard, EVERY, axis=shard.ndim - 2, tiled=True)


def scatter_all(pack):
    return lax.psum_scatter(pack, EVERY, scatter_dimension=0, tiled=True).astype(f32)


def sum_pieces(pieces, axes, dtype=bf16):
    total = pieces[0].astype(f32)
    for step in range(1, len(pieces)):
        total += send_xor(pieces[step], axes, step).astype(f32)
    return total.astype(dtype)


def sum_blocks(pack, axes, dtype=bf16):
    count = lax.axis_size(axes)
    size = pack.shape[0] // count
    blocks = [pack[place * size : (place + 1) * size] for place in range(count)]
    return sum_pieces(blocks, axes, dtype)


def pack_for(first, grads):
    splits, cores, ranks = (lax.axis_size(axes) for axes in ("tensor", "fsdp", ROW))
    rows, columns = grads[0][0].shape
    size = rows // cores // ranks
    plan = []
    for piece, row in enumerate(grads):
        for split in range(splits):
            for core in range(cores):
                for rank in range(ranks):
                    place = split * ranks + rank if first == "tensor" else rank * splits + split
                    source = (piece * splits + split, (core * ranks + rank) * size, size, 0, columns)
                    plan.append(source + (core, place * size, piece * columns))
    sources = [values for row in grads for values in row]
    return lay(sources, plan, [(splits * rows // cores, columns * len(grads))] * cores)


def pack_grid(grads):
    rows, columns = grads[0][0].shape
    count = len(grads[0])
    plan = [
        (place * count + row, 0, rows, 0, columns, 0, row * rows, place * columns)
        for place in range(len(grads))
        for row in range(count)
    ]
    return lay([values for row in grads for values in row], plan, [(rows * count, columns * len(grads))])[0]


def own_order(share, width):
    cores, lats, rows = (lax.axis_size(axes) for axes in ("fsdp", "lat", ROW))
    place = lax.iota(jnp.int32, width)
    block, rest = place // share, place % share
    lat = jnp.bitwise_xor(block % lats, lax.axis_index("lat"))
    row = jnp.bitwise_xor(block // lats % rows, lax.axis_index(ROW))
    core = jnp.bitwise_xor(block // (lats * rows), lax.axis_index("fsdp"))
    natural = ((core * lats + lat) * rows + row) * share + rest
    return (lax.broadcasted_iota(jnp.int32, (width, width), 0) == natural[None, :]).astype(bf16)


def local(
    latents, text, time_vector, table, w_qkv, w_out, w_cq, w_ckv, w_co, w_up, w_down, cotangent
):
    width = latents.shape[2]
    share = w_cq.shape[0]
    part = w_cq.shape[1]
    inner_part = w_up.shape[1]
    splits = lax.axis_size("tensor")
    ranks = lax.axis_size("hr")
    halves = lax.axis_size("sr")
    edge = part // ranks
    heads = edge // HEAD_DIM
    groups = ranks * splits
    piece_width = -(-(3 * edge + 6) // LANES) * LANES
    wide = -(-part // LANES) * LANES
    slot = lax.axis_index("lat")
    rank = lax.axis_index("hr")

    def padded(values):
        return jnp.pad(values, ((0, 0), (0, wide - part)))

    latents_got = exchange(partial(pick, latents), "lat")
    mid_shard = jnp.concatenate(
        [padded(piece) for piece in (w_out.T, w_ckv[:, 0], w_ckv[:, 1], w_cq, w_co.T)], axis=1
    )
    shard_qkv = jnp.transpose(w_qkv.reshape(share, 3, ranks, edge), (2, 0, 1, 3)).reshape(
        ranks, share, 3 * edge
    )
    fill = jnp.pad(table.T, ((0, 0), (0, piece_width - 3 * edge - 6)))
    qkv_got = [
        gather(jnp.concatenate((shard_qkv[place], fill), axis=1), place % 2 == 0)
        for place in range(ranks)
    ]
    qkv_full = [full for full, _ in qkv_got]
    mid_full = gather_all(mid_shard)
    two_full = gather_all(jnp.stack((w_up, w_down.T)))

    turn = own_order(share, width)
    residual = jnp.concatenate(latents_got, axis=0).astype(f32)
    cotangent, _ = tie(cotangent, qkv_full[0][0])
    grad_three = jnp.concatenate(exchange(partial(pick, cotangent), "lat"), axis=0).astype(f32)
    rows = residual.shape[0]
    caption = pick(text, slot)
    table_full = dot(qkv_full[0][0][:, 3 * edge : 3 * edge + 6].T, turn, NT)
    modulate = table_full + pick(time_vector, slot).astype(f32).reshape(6, width)
    shift_one, scale_one, gate_one, shift_two, scale_two, gate_two = (
        modulate[row : row + 1] for row in range(6)
    )

    normed_one, inverse_one = norm_parts(residual)
    hidden_one = (normed_one * (1.0 + scale_one) + shift_one).astype(bf16)
    hidden_turn = dot(hidden_one, turn).astype(bf16)
    mixed = [None] * groups
    for split in range(splits):
        pieces = [dot(hidden_turn, full[split]).astype(bf16) for full in qkv_full]
        for other in range(ranks):
            step = other * splits + split
            piece = choose(pieces, jnp.bitwise_xor(rank, other))
            mixed[step] = send_xor(piece, HEAD_GROUP, step) if step else piece
    for step in range(1, halves):
        mixed += [send_xor(piece, "sr", step) for piece in mixed[:groups]]
    out_full, key_full, val_full, cq_full, co_full = cut(mid_full, width, wide)
    cross_k = [dot(caption, full).astype(bf16) for full in key_full]
    cross_v = [dot(caption, full).astype(bf16) for full in val_full]
    (mixed[0], cross_k, cross_v) = lax.optimization_barrier((mixed[0], cross_k, cross_v))
    att_low, att_wide, logsum = attend(mixed, groups, heads)

    def by_split(pieces, split):
        own = [pieces[other * splits + split] for other in range(ranks)]
        return [choose(own, jnp.bitwise_xor(rank, place)) for place in range(ranks)]

    att_back = give_back(att_low, HEAD_GROUP)
    att_own = [
        padded(jnp.concatenate(by_split(att_back, split), axis=1)) for split in range(splits)
    ]
    col = lax.axis_index("tensor")

    def from_own(pieces):
        return [choose(pieces, jnp.bitwise_xor(col, place)) for place in range(splits)]

    att = from_own(att_own)
    up_full, down_full = (
        [two_full[place, split * width : (split + 1) * width] for split in range(splits)]
        for place in range(2)
    )

    out_one = sum(dot(att[split], out_full[split], NT) for split in range(splits))
    after_one = residual + gate_one * out_one
    mid_low = after_one.astype(bf16)
    cross_q = [dot(mid_low, full).astype(bf16) for full in cq_full]
    cross_low = cross(cross_q, cross_k, cross_v, part)
    out_two = sum(dot(cross_low[split], co_full[split], NT) for split in range(splits))
    after_two = after_one + out_two
    normed_two, inverse_two = norm_parts(after_two)
    hidden_two = (normed_two * (1.0 + scale_two) + shift_two).astype(bf16)
    inner = [dot(hidden_two, up_full[split]) for split in range(splits)]
    active = [jax.nn.gelu(values, approximate=True).astype(bf16) for values in inner]
    out_three = sum(dot(active[split], down_full[split], NT) for split in range(splits))
    result = (after_two + gate_two * out_three).astype(bf16)
    result_back = in_order(give_back(list(result.reshape(latents.shape)), "lat"), "lat")

    grad_gate_two = jnp.sum(grad_three * out_three, axis=0)
    grad_z = (gate_two * grad_three).astype(bf16)
    grad_inner = []
    for split in range(splits):
        grad_active = dot(grad_z, down_full[split])
        _, pull = jax.vjp(partial(jax.nn.gelu, approximate=True), inner[split])
        grad_inner.append(pull(grad_active)[0].astype(bf16))
    down_sum = scatter_all(pack_grid([[dot(grad_z, piece, TN).astype(bf16) for piece in active]]))
    up_sum = scatter_all(
        pack_grid([[dot(hidden_two, piece, TN).astype(bf16) for piece in grad_inner]])
    )
    grad_hidden_two = sum(dot(grad_inner[split], up_full[split], NT) for split in range(splits))
    grad_shift_two = jnp.sum(grad_hidden_two, axis=0)
    grad_scale_two = jnp.sum(grad_hidden_two * normed_two, axis=0)
    grad_two = grad_three + norm_back(grad_hidden_two * (1.0 + scale_two), normed_two, inverse_two)

    grad_out_two = grad_two.astype(bf16)
    grad_cross = [dot(grad_out_two, full).astype(bf16) for full in co_full]
    grad_cq, grad_ck, grad_cv = cross_back(cross_q, cross_k, cross_v, grad_cross, part)
    grad_one = grad_two + sum(dot(grad_cq[split], cq_full[split], NT) for split in range(splits))
    text_terms = sum(
        dot(grad_ck[split], key_full[split], NT) + dot(grad_cv[split], val_full[split], NT)
        for split in range(splits)
    )

    grad_gate_one = jnp.sum(grad_one * out_one, axis=0)
    grad_out_one = (gate_one * grad_one).astype(bf16)
    grad_att = from_own([dot(grad_out_one, full).astype(bf16) for full in out_full])
    grad_heads = [None] * groups
    for split in range(splits):
        cuts = [grad_att[split][:, place * edge : (place + 1) * edge] for place in range(ranks)]
        for other in range(ranks):
            step = other * splits + split
            piece = choose(cuts, jnp.bitwise_xor(rank, other))
            grad_heads[step] = send_xor(piece, HEAD_GROUP, step) if step else piece
    lefts = [mid_low, grad_out_two, grad_out_one]
    lefts, grad_ck, grad_cv, _ = lax.optimization_barrier((lefts, grad_ck, grad_cv, grad_att))
    caption_turn = dot(caption, turn).astype(bf16)
    mid_grads = [
        [dot(left, right, TN).astype(bf16) for right in rights]
        for left, rights in (
            (caption_turn, from_own(grad_ck)),
            (caption_turn, from_own(grad_cv)),
            (dot(lefts[0], turn).astype(bf16), from_own(grad_cq)),
            (dot(lefts[1], turn).astype(bf16), from_own(cross_low)),
            (dot(lefts[2], turn).astype(bf16), att_own),
        )
    ]
    pack_a = sum_pieces(pack_for("tensor", mid_grads[:3]), "fsdp")
    pack_b = sum_pieces(pack_for(ROW, mid_grads[3:]), "fsdp")
    (grad_heads[0], pack_a, pack_b, result_back) = lax.optimization_barrier(
        (grad_heads[0], pack_a, pack_b, result_back)
    )
    pack_a, pack_b = sum_blocks(pack_a, "tensor"), sum_blocks(pack_b, ROW)
    grad_mix = list(attend_back(mixed, groups, grad_heads, att_wide, logsum, heads))
    (grad_mix[0], pack_a, pack_b, down_sum) = lax.optimization_barrier(
        (grad_mix[0], pack_a, pack_b, down_sum)
    )
    for step in range(1, halves):
        for place in range(groups):
            more = send_xor(grad_mix[step * groups + place], "sr", step)
            grad_mix[place] = (grad_mix[place].astype(f32) + more.astype(f32)).astype(bf16)
    grad_proj = give_back(grad_mix[:groups], HEAD_GROUP)
    grad_proj = [by_split(grad_proj, split) for split in range(splits)]
    one_packs = [
        pack_for(
            ROW if place % 2 else "tensor",
            [[dot(hidden_turn, grad_proj[split][place], TN).astype(bf16) for split in range(splits)]],
        )
        for place in range(ranks)
    ]
    (grad_proj, one_packs) = tie(grad_proj, one_packs)
    pack_a, pack_b = sum_blocks(pack_a, ROW), sum_blocks(pack_b, "tensor")
    one_packs = [sum_pieces(pack, "fsdp") for pack in one_packs]
    text_sum = plane_sum(text_terms, bf16)
    grad_hidden_one = sum(
        dot(grad_proj[split][place], qkv_full[place][split], NT)
        for place in range(ranks)
        for split in range(splits)
    )
    grad_hidden_one = dot(grad_hidden_one.astype(bf16), turn, NT)
    grad_shift_one = jnp.sum(grad_hidden_one, axis=0)
    grad_scale_one = jnp.sum(grad_hidden_one * normed_one, axis=0)
    grad_latents = grad_one + norm_back(
        grad_hidden_one * (1.0 + scale_one), normed_one, inverse_one
    )
    grad_latents = grad_latents.astype(bf16).reshape(latents.shape)
    grad_latents = in_order(give_back(list(grad_latents), "lat"), "lat")

    time_terms = jnp.stack(
        (
            grad_shift_one,
            grad_scale_one,
            grad_gate_one,
            grad_shift_two,
            grad_scale_two,
            grad_gate_two,
        )
    )
    orders = [("tensor", ROW), (ROW, "tensor")]
    for stage in range(2):
        one_packs = [
            sum_blocks(pack, orders[place % 2][stage]) for place, pack in enumerate(one_packs)
        ]
    (one_packs, up_sum) = tie(one_packs, up_sum)
    one_sums = [sum_blocks(pack, "lat", f32) for pack in one_packs]
    pack_a, pack_b = sum_blocks(pack_a, "lat", f32), sum_blocks(pack_b, "lat", f32)
    key_sum, val_sum, cq_sum, co_sum, out_sum = (
        pack[:, place * wide : place * wide + part]
        for pack, count in ((pack_a, 3), (pack_b, 2))
        for place in range(count)
    )
    grad_time = over_latents(plane_sum(time_terms, f32))
    grad_table = jnp.sum(grad_time, axis=0)
    grad_table += send_xor(grad_table, "fsdp", 1)
    owner = lax.axis_index(("fsdp", "lat", "sr", "hr"))
    grad_table = lax.dynamic_slice_in_dim(grad_table, owner * share, share, 1)
    grad_text = over_latents(text_sum.astype(bf16)).astype(f32)
    grad_qkv = jnp.stack(
        [sums[:, : 3 * edge].reshape(share, 3, edge) for sums in one_sums], axis=2
    ).reshape(share, 3, part)
    return (
        result_back,
        grad_latents.astype(f32),
        grad_text,
        grad_time.reshape(-1, 6 * width),
        grad_table,
        grad_qkv,
        out_sum.T,
        cq_sum,
        jnp.stack((key_sum, val_sum), axis=1),
        co_sum.T,
        up_sum,
        down_sum.T,
    )


def solution(mesh):
    def run(latents, text, time_vector, table, w_qkv, *others):
        fsdp, context, tensor = (mesh.shape[name] for name in ("fsdp", "context", "tensor"))
        lat = latents.shape[0] // fsdp
        group = context // lat
        ranks = math.gcd(group, w_qkv.shape[2] // (tensor * HEAD_DIM))
        sizes = (fsdp, lat, group // ranks, ranks, tensor)
        finer = Mesh(mesh.devices.reshape(sizes), ("fsdp", "lat", "sr", "hr", "tensor"))
        line = ("lat", "sr", "hr")
        shard = ("fsdp",) + line
        tokens = P("fsdp", line + ("tensor",), None)
        by_row = P(shard, "tensor")
        by_row3 = P(shard, None, "tensor")
        by_column = P("tensor", shard)
        weights = (by_row3, by_column, by_row, by_row3, by_column, by_row, by_column)
        return jax.shard_map(
            local,
            mesh=finer,
            in_specs=(tokens, P("fsdp", None, None), P("fsdp", None), P(None, shard))
            + weights
            + (tokens,),
            out_specs=(tokens, tokens, P("fsdp", None, None), P("fsdp", None), P(None, shard))
            + weights,
            check_vma=False,
        )(latents, text, time_vector, table, w_qkv, *others)

    return run
```

```python
import math
from functools import partial

import jax
import jax.numpy as jnp
from jax import lax
from jax.experimental import pallas as pl
from jax.experimental.pallas import tpu as pltpu
from jax.sharding import Mesh
from jax.sharding import PartitionSpec as P

HEAD_DIM = 72
EPSILON = 1e-06
LANES = 128
FACTOR = HEAD_DIM ** (-0.5)
FACTOR2 = FACTOR * math.log2(math.e)
VMEM_LIMIT = 56 * 1024 * 1024

f32 = jnp.float32
bf16 = jnp.bfloat16

NT = (((1,), (1,)), ((), ()))
NN = (((1,), (0,)), ((), ()))
TN = (((0,), (0,)), ((), ()))

ROW = ("sr", "hr")
EVERY = ("tensor", "fsdp", "lat", "sr", "hr")
PLANE = ("sr", "hr", "tensor")
HEAD_GROUP = ("hr", "tensor")


def dot(left, right, dims=NN):
    return lax.dot_general(left, right, dims, preferred_element_type=f32)


def norm_parts(values):
    center = values - jnp.mean(values, axis=-1, keepdims=True)
    inverse = lax.rsqrt(jnp.mean(center * center, axis=-1, keepdims=True) + EPSILON)
    return (center * inverse, inverse)


def norm_back(grad_hat, normed, inverse):
    first = jnp.mean(grad_hat, axis=-1, keepdims=True)
    second = jnp.mean(grad_hat * normed, axis=-1, keepdims=True)
    return inverse * (grad_hat - first - normed * second)


def send_xor(piece, axes, step):
    size = lax.axis_size(axes)
    return lax.ppermute(piece, axes, [(rank, rank ^ step) for rank in range(size)])


def pick(stack, index):
    return lax.dynamic_index_in_dim(stack, index, 0, keepdims=False)


def exchange(piece_for, axes):
    me = lax.axis_index(axes)
    got = [piece_for(me)]
    for step in range(1, lax.axis_size(axes)):
        got.append(send_xor(piece_for(jnp.bitwise_xor(me, step)), axes, step))
    return got


def give_back(pieces, axes):
    return [send_xor(piece, axes, step) if step else piece for step, piece in enumerate(pieces)]


def in_order(pieces, axes):
    me = lax.axis_index(axes)
    places = range(len(pieces))
    return jnp.stack([choose(pieces, jnp.bitwise_xor(me, place)) for place in places])


def choose(pieces, index):
    out = pieces[0]
    for place in range(1, len(pieces)):
        out = jnp.where(index == place, pieces[place], out)
    return out


def plane_sum(values, dtype):
    sent = values.astype(dtype)
    total = sent.astype(f32)
    for step in range(1, lax.axis_size(PLANE)):
        total += send_xor(sent, PLANE, step).astype(f32)
    return total


def over_latents(values):
    return in_order(give_back([values] * lax.axis_size("lat"), "lat"), "lat")


def tie(first, second):
    return lax.optimization_barrier((first, second))


def attend_kernel(heads, chunks, own, *refs):
    pieces = refs[:chunks]
    low_refs = refs[chunks : chunks + own]
    att_ref, lse_ref, queries, keys, vals, lows, column = refs[chunks + own :]
    edge = heads * HEAD_DIM
    index = pl.program_id(0)
    block = att_ref.shape[1]

    @pl.when(index == 0)
    def _():
        lane = lax.broadcasted_iota(jnp.int32, vals.shape[1:], 1)
        column[...] = jnp.zeros_like(column)
        for head in range(heads):
            vals[head] = jnp.where(lane == HEAD_DIM, 1.0, 0.0).astype(bf16)
            low = head * HEAD_DIM
            for number, piece in enumerate(pieces):
                count = piece.shape[0]
                rows = slice(number * count, (number + 1) * count)
                if number < own:
                    queries[head, rows] = piece[:, low : low + HEAD_DIM]
                keys[head, rows] = piece[:, edge + low : edge + low + HEAD_DIM]
                vals[head, rows, :HEAD_DIM] = piece[:, 2 * edge + low : 2 * edge + low + HEAD_DIM]

    mine = pl.ds(pl.multiple_of(index * block, block), block)

    def score(head):
        return dot(queries[head, mine, :], keys[head], NT)

    ahead = score(0)
    for head in range(heads):
        scores = ahead
        if head + 1 < heads:
            ahead = score(head + 1)
        top = jnp.max(scores, axis=1, keepdims=True) * FACTOR2
        weights = jnp.exp2(scores * FACTOR2 - top).astype(bf16)
        out = dot(weights, vals[head])
        total = out[:, HEAD_DIM : HEAD_DIM + 1]
        out = out[:, :HEAD_DIM] / total
        att_ref[head] = out
        lows[head, mine, :] = out.astype(bf16)
        column[:, head : head + 1] = top + jnp.log2(total)
    lse_ref[...] = column[...].T[: lse_ref.shape[0]]

    @pl.when(index == pl.num_programs(0) - 1)
    def _():
        for head in range(heads):
            low = head * HEAD_DIM
            for number, ref in enumerate(low_refs):
                count = ref.shape[0]
                ref[:, low : low + HEAD_DIM] = lows[head, number * count : (number + 1) * count, :]


def whole_block(shape):
    return pl.BlockSpec(shape, lambda i: (0,) * len(shape))


def attend(pieces, own, heads):
    count, width = pieces[0].shape
    rows, total = own * count, len(pieces) * count
    block = min(256, rows)
    edge = heads * HEAD_DIM
    slots = -(-heads // 8) * 8
    out = pl.pallas_call(
        partial(attend_kernel, heads, len(pieces), own),
        grid=(rows // block,),
        in_specs=[whole_block((count, width))] * len(pieces),
        out_specs=[whole_block((count, edge))] * own
        + [
            pl.BlockSpec((heads, block, HEAD_DIM), lambda i: (0, i, 0)),
            pl.BlockSpec((slots, block), lambda i: (0, i)),
        ],
        out_shape=[jax.ShapeDtypeStruct((count, edge), bf16)] * own
        + [
            jax.ShapeDtypeStruct((heads, rows, HEAD_DIM), f32),
            jax.ShapeDtypeStruct((slots, rows), f32),
        ],
        scratch_shapes=[
            pltpu.VMEM((heads, rows, HEAD_DIM), bf16),
            pltpu.VMEM((heads, total, HEAD_DIM), bf16),
            pltpu.VMEM((heads, total, LANES), bf16),
            pltpu.VMEM((heads, rows, HEAD_DIM), bf16),
            pltpu.VMEM((block, LANES), f32),
        ],
        cost_estimate=pl.CostEstimate(
            flops=8 * heads * rows * total * LANES,
            transcendentals=heads * rows * total,
            bytes_accessed=4 * total * width,
        ),
        compiler_params=pltpu.CompilerParams(vmem_limit_bytes=VMEM_LIMIT),
    )(*pieces)
    return (out[:own], out[own], out[own + 1])


def attend_back_kernel(heads, chunk, chunks, own, *refs):
    pieces = refs[:chunks]
    grad_refs = refs[chunks : chunks + own]
    att_ref, lse_ref = refs[chunks + own : chunks + own + 2]
    outs = refs[chunks + own + 2 : 2 * chunks + own + 2]
    queries, keys, vals, grads, turned, dq, dk, dv, column = refs[2 * chunks + own + 2 :]
    edge = heads * HEAD_DIM
    index = pl.program_id(0)
    block = att_ref.shape[1]
    total = keys.shape[1]

    @pl.when(index == 0)
    def _():
        turned[...] = jnp.zeros_like(turned)
        column[...] = jnp.zeros_like(column)
        dk[...] = jnp.zeros_like(dk)
        dv[...] = jnp.zeros_like(dv)
        for head in range(heads):
            low = head * HEAD_DIM
            for number, piece in enumerate(pieces):
                count = piece.shape[0]
                rows = slice(number * count, (number + 1) * count)
                if number < own:
                    queries[head, rows] = piece[:, low : low + HEAD_DIM]
                    grads[head, rows] = grad_refs[number][:, low : low + HEAD_DIM]
                key = piece[:, edge + low : edge + low + HEAD_DIM]
                keys[head, rows] = key
                turned[head, :HEAD_DIM, rows] = key.astype(f32).T.astype(bf16)
                vals[head, rows] = piece[:, 2 * edge + low : 2 * edge + low + HEAD_DIM]

    mine = pl.ds(pl.multiple_of(index * block, block), block)
    for head in range(heads):
        column[:, head : head + 1] = jnp.sum(
            att_ref[head] * grads[head, mine, :].astype(f32), axis=1, keepdims=True
        )
    deltas = column[...].T
    for head in range(heads):
        query = queries[head, mine, :]
        grad = grads[head, mine, :]
        lse = lse_ref[head : head + 1, :]
        delta = deltas[head : head + 1, :]
        turned_grad = jnp.zeros((turned.shape[1], block), f32)
        for start in range(0, total, chunk):
            part = slice(start, start + chunk)
            scores = dot(keys[head, part, :], query, NT)
            grad_probs = dot(vals[head, part, :], grad, NT)
            probs = jnp.exp2(scores * FACTOR2 - lse)
            grad_scores = (probs * (grad_probs - delta)).astype(bf16)
            dv[head, part, :] += dot(probs.astype(bf16), grad)
            dk[head, part, :] += dot(grad_scores, query)
            turned_grad += dot(turned[head, :, part], grad_scores)
        dq[head, mine, :] = (turned_grad.T[:, :HEAD_DIM] * FACTOR).astype(bf16)

    @pl.when(index == pl.num_programs(0) - 1)
    def _():
        for number, ref in enumerate(outs):
            count = ref.shape[0]
            rows = slice(number * count, (number + 1) * count)
            ref[...] = jnp.zeros_like(ref)
            for head in range(heads):
                low = head * HEAD_DIM
                if number < own:
                    ref[:, low : low + HEAD_DIM] = dq[head, rows]
                ref[:, edge + low : edge + low + HEAD_DIM] = (dk[head, rows] * FACTOR).astype(bf16)
                ref[:, 2 * edge + low : 2 * edge + low + HEAD_DIM] = dv[head, rows].astype(bf16)


def attend_back(pieces, own, grads, att, lse, heads):
    count, width = pieces[0].shape
    rows, total = own * count, len(pieces) * count
    block = min(256, rows)
    edge = heads * HEAD_DIM
    slots = lse.shape[0]
    return pl.pallas_call(
        partial(attend_back_kernel, heads, min(512, total), len(pieces), own),
        grid=(rows // block,),
        in_specs=[whole_block((count, width))] * len(pieces)
        + [whole_block((count, edge))] * own
        + [
            pl.BlockSpec((heads, block, HEAD_DIM), lambda i: (0, i, 0)),
            pl.BlockSpec((slots, block), lambda i: (0, i)),
        ],
        out_specs=[whole_block((count, width))] * len(pieces),
        out_shape=[jax.ShapeDtypeStruct((count, width), bf16)] * len(pieces),
        scratch_shapes=[
            pltpu.VMEM((heads, rows, HEAD_DIM), bf16),
            pltpu.VMEM((heads, total, HEAD_DIM), bf16),
            pltpu.VMEM((heads, total, HEAD_DIM), bf16),
            pltpu.VMEM((heads, rows, HEAD_DIM), bf16),
            pltpu.VMEM((heads, LANES, total), bf16),
            pltpu.VMEM((heads, rows, HEAD_DIM), bf16),
            pltpu.VMEM((heads, total, HEAD_DIM), f32),
            pltpu.VMEM((heads, total, HEAD_DIM), f32),
            pltpu.VMEM((block, LANES), f32),
        ],
        cost_estimate=pl.CostEstimate(
            flops=20 * heads * rows * total * LANES,
            transcendentals=heads * rows * total,
            bytes_accessed=8 * total * width,
        ),
        compiler_params=pltpu.CompilerParams(vmem_limit_bytes=VMEM_LIMIT),
    )(*pieces, *grads, att, lse)


def head_lanes(part):
    return [slice(low, low + HEAD_DIM) for low in range(0, part, HEAD_DIM)]


def cross_kernel(part, splits, *refs):
    q_refs, k_refs, v_refs, out_refs = (refs[splits * i : splits * (i + 1)] for i in range(4))
    for q_ref, k_ref, v_ref, out_ref in zip(q_refs, k_refs, v_refs, out_refs):
        fill = out_ref.shape[1] - part
        if fill:
            out_ref[:, part:] = jnp.zeros((out_ref.shape[0], fill), bf16)
        for lanes in head_lanes(part):
            scores = dot(q_ref[:, lanes], k_ref[:, lanes], NT) * FACTOR
            weights = jnp.exp(scores - jnp.max(scores, axis=1, keepdims=True))
            probs = weights / jnp.sum(weights, axis=1, keepdims=True)
            out_ref[:, lanes] = dot(probs.astype(bf16), v_ref[:, lanes]).astype(bf16)


def cross(queries, keys, values, part):
    splits = len(queries)
    rows, width = queries[0].shape
    texts = keys[0].shape[0]
    block = min(512, rows)
    split = pl.BlockSpec((block, width), lambda i: (i, 0))
    return pl.pallas_call(
        partial(cross_kernel, part, splits),
        grid=(rows // block,),
        in_specs=[split] * splits + [whole_block((texts, width))] * (2 * splits),
        out_specs=[split] * splits,
        out_shape=[jax.ShapeDtypeStruct((rows, width), bf16)] * splits,
        compiler_params=pltpu.CompilerParams(vmem_limit_bytes=VMEM_LIMIT),
    )(*queries, *keys, *values)


def cross_back_kernel(part, splits, *refs):
    q_refs, k_refs, v_refs, grad_refs, dq_refs, dk_refs, dv_refs, dk_sums, dv_sums = (
        refs[splits * i : splits * (i + 1)] for i in range(9)
    )
    first = pl.program_id(0) == 0
    last = pl.program_id(0) == pl.num_programs(0) - 1
    for q_ref, k_ref, v_ref, grad_ref, dq_ref, dk, dv in zip(
        q_refs, k_refs, v_refs, grad_refs, dq_refs, dk_sums, dv_sums
    ):

        @pl.when(first)
        def _():
            dk[...] = jnp.zeros_like(dk)
            dv[...] = jnp.zeros_like(dv)

        fill = dq_ref.shape[1] - part
        if fill:
            dq_ref[:, part:] = jnp.zeros((dq_ref.shape[0], fill), bf16)
        for lanes in head_lanes(part):
            query = q_ref[:, lanes]
            key = k_ref[:, lanes]
            grad = grad_ref[:, lanes]
            scores = dot(query, key, NT) * FACTOR
            weights = jnp.exp(scores - jnp.max(scores, axis=1, keepdims=True))
            probs = weights / jnp.sum(weights, axis=1, keepdims=True)
            grad_probs = dot(grad, v_ref[:, lanes], NT)
            delta = jnp.sum(probs * grad_probs, axis=1, keepdims=True)
            grad_scores = (probs * (grad_probs - delta)).astype(bf16)
            dq_ref[:, lanes] = (dot(grad_scores, key) * FACTOR).astype(bf16)
            dk[:, lanes] += dot(grad_scores, query, TN)
            dv[:, lanes] += dot(probs.astype(bf16), grad, TN)

    @pl.when(last)
    def _():
        for dk_ref, dv_ref, dk, dv in zip(dk_refs, dv_refs, dk_sums, dv_sums):
            dk_ref[...] = (dk[...] * FACTOR).astype(bf16)
            dv_ref[...] = dv[...].astype(bf16)


def cross_back(queries, keys, values, grads, part):
    splits = len(queries)
    rows, width = queries[0].shape
    texts = keys[0].shape[0]
    block = min(512, rows)
    whole = whole_block((texts, width))
    split = pl.BlockSpec((block, width), lambda i: (i, 0))
    out = pl.pallas_call(
        partial(cross_back_kernel, part, splits),
        grid=(rows // block,),
        in_specs=[split] * splits + [whole] * (2 * splits) + [split] * splits,
        out_specs=[split] * splits + [whole] * (2 * splits),
        out_shape=[jax.ShapeDtypeStruct((rows, width), bf16)] * splits
        + [jax.ShapeDtypeStruct((texts, width), bf16)] * (2 * splits),
        scratch_shapes=[pltpu.VMEM((texts, width), f32)] * (2 * splits),
        compiler_params=pltpu.CompilerParams(vmem_limit_bytes=VMEM_LIMIT),
    )(*queries, *keys, *values, *grads)
    return (out[:splits], out[splits : 2 * splits], out[2 * splits :])


def assemble_kernel(plan, count, *refs):
    sources, outs, sems = refs[:count], refs[count:-1], refs[-1]
    copies = []
    for number, (source, start, rows, column, size, place, row, shift) in enumerate(plan):
        copies.append(
            pltpu.make_async_copy(
                sources[source].at[pl.ds(start, rows), pl.ds(column, size)],
                outs[place].at[pl.ds(row, rows), pl.ds(shift, size)],
                sems.at[number],
            )
        )
    for copy in copies:
        copy.start()
    for copy in copies:
        copy.wait()


def lay(sources, plan, shapes):
    anywhere = pl.BlockSpec(memory_space=pl.ANY)
    return list(
        pl.pallas_call(
            partial(assemble_kernel, plan, len(sources)),
            in_specs=[anywhere] * len(sources),
            out_specs=[pl.BlockSpec(memory_space=pltpu.VMEM)] * len(shapes),
            out_shape=[jax.ShapeDtypeStruct(shape, bf16) for shape in shapes],
            scratch_shapes=[pltpu.SemaphoreType.DMA((len(plan),))],
            compiler_params=pltpu.CompilerParams(vmem_limit_bytes=VMEM_LIMIT),
        )(*sources)
    )


def assemble(stacks):
    sources = [piece for stack in stacks for piece in stack]
    plan, shapes = [], []
    for stack in stacks:
        row, width = 0, stack[0].shape[1]
        for piece in stack:
            plan.append((len(plan), 0, piece.shape[0], 0, width, len(shapes), row, 0))
            row += piece.shape[0]
        shapes.append((row, width))
    return lay(sources, plan, shapes)


def cut(source, rows, columns):
    grid = [
        (place, row) for place in range(source.shape[1] // columns) for row in range(source.shape[0] // rows)
    ]
    plan = [
        (0, row * rows, rows, place * columns, columns, number, 0, 0)
        for number, (place, row) in enumerate(grid)
    ]
    out = lay([source], plan, [(rows, columns)] * len(grid))
    count = source.shape[0] // rows
    return [out[place : place + count] for place in range(0, len(out), count)]


def with_others(piece, axes):
    return [piece] + [send_xor(piece, axes, step) for step in range(1, lax.axis_size(axes))]


def gather(shard, tensor_first):
    start = jnp.concatenate(with_others(shard, "lat"))
    if tensor_first and lax.axis_size("tensor") * lax.axis_size(ROW) <= 8:
        stacks = [with_others(piece, ROW) for piece in with_others(start, "tensor")]
    else:
        half = assemble([with_others(start, ROW)])[0]
        stacks = [[piece] for piece in with_others(half, "tensor")]
    cores = range(1, lax.axis_size("fsdp"))
    stacks = [
        stack + [send_xor(piece, "fsdp", step) for step in cores for piece in stack] for stack in stacks
    ]
    return assemble(stacks), start


def gather_all(shard):
    return lax.all_gather(shard, EVERY, axis=shard.ndim - 2, tiled=True)


def scatter_all(pack):
    return lax.psum_scatter(pack, EVERY, scatter_dimension=0, tiled=True).astype(f32)


def sum_pieces(pieces, axes, dtype=bf16):
    total = pieces[0].astype(f32)
    for step in range(1, len(pieces)):
        total += send_xor(pieces[step], axes, step).astype(f32)
    return total.astype(dtype)


def sum_blocks(pack, axes, dtype=bf16):
    count = lax.axis_size(axes)
    size = pack.shape[0] // count
    blocks = [pack[place * size : (place + 1) * size] for place in range(count)]
    return sum_pieces(blocks, axes, dtype)


def pack_for(first, grads):
    splits, cores, ranks = (lax.axis_size(axes) for axes in ("tensor", "fsdp", ROW))
    rows, columns = grads[0][0].shape
    size = rows // cores // ranks
    plan = []
    for piece, row in enumerate(grads):
        for split in range(splits):
            for core in range(cores):
                for rank in range(ranks):
                    place = split * ranks + rank if first == "tensor" else rank * splits + split
                    source = (piece * splits + split, (core * ranks + rank) * size, size, 0, columns)
                    plan.append(source + (core, place * size, piece * columns))
    sources = [values for row in grads for values in row]
    return lay(sources, plan, [(splits * rows // cores, columns * len(grads))] * cores)


def pack_grid(grads):
    rows, columns = grads[0][0].shape
    count = len(grads[0])
    plan = [
        (place * count + row, 0, rows, 0, columns, 0, row * rows, place * columns)
        for place in range(len(grads))
        for row in range(count)
    ]
    return lay([values for row in grads for values in row], plan, [(rows * count, columns * len(grads))])[0]


def own_order(share, width):
    cores, lats, rows = (lax.axis_size(axes) for axes in ("fsdp", "lat", ROW))
    place = lax.iota(jnp.int32, width)
    block, rest = place // share, place % share
    lat = jnp.bitwise_xor(block % lats, lax.axis_index("lat"))
    row = jnp.bitwise_xor(block // lats % rows, lax.axis_index(ROW))
    core = jnp.bitwise_xor(block // (lats * rows), lax.axis_index("fsdp"))
    natural = ((core * lats + lat) * rows + row) * share + rest
    return (lax.broadcasted_iota(jnp.int32, (width, width), 0) == natural[None, :]).astype(bf16)


def local(
    latents, text, time_vector, table, w_qkv, w_out, w_cq, w_ckv, w_co, w_up, w_down, cotangent
):
    width = latents.shape[2]
    share = w_cq.shape[0]
    part = w_cq.shape[1]
    inner_part = w_up.shape[1]
    splits = lax.axis_size("tensor")
    ranks = lax.axis_size("hr")
    halves = lax.axis_size("sr")
    edge = part // ranks
    heads = edge // HEAD_DIM
    groups = ranks * splits
    piece_width = -(-(3 * edge + 6) // LANES) * LANES
    wide = -(-part // LANES) * LANES
    slot = lax.axis_index("lat")
    rank = lax.axis_index("hr")

    def padded(values):
        return jnp.pad(values, ((0, 0), (0, wide - part)))

    latents_got = exchange(partial(pick, latents), "lat")
    mid_shard = jnp.concatenate(
        [padded(piece) for piece in (w_out.T, w_ckv[:, 0], w_ckv[:, 1], w_cq, w_co.T)], axis=1
    )
    shard_qkv = jnp.transpose(w_qkv.reshape(share, 3, ranks, edge), (2, 0, 1, 3)).reshape(
        ranks, share, 3 * edge
    )
    fill = jnp.pad(table.T, ((0, 0), (0, piece_width - 3 * edge - 6)))
    qkv_got = [
        gather(jnp.concatenate((shard_qkv[place], fill), axis=1), place % 2 == 0)
        for place in range(ranks)
    ]
    qkv_full = [full for full, _ in qkv_got]
    mid_full = gather_all(mid_shard)
    two_full = gather_all(jnp.stack((w_up, w_down.T)))

    turn = own_order(share, width)
    residual = jnp.concatenate(latents_got, axis=0).astype(f32)
    cotangent, _ = tie(cotangent, qkv_full[0][0])
    grad_three = jnp.concatenate(exchange(partial(pick, cotangent), "lat"), axis=0).astype(f32)
    rows = residual.shape[0]
    caption = pick(text, slot)
    table_full = dot(qkv_full[0][0][:, 3 * edge : 3 * edge + 6].T, turn, NT)
    modulate = table_full + pick(time_vector, slot).astype(f32).reshape(6, width)
    shift_one, scale_one, gate_one, shift_two, scale_two, gate_two = (
        modulate[row : row + 1] for row in range(6)
    )

    normed_one, inverse_one = norm_parts(residual)
    hidden_one = (normed_one * (1.0 + scale_one) + shift_one).astype(bf16)
    hidden_turn = dot(hidden_one, turn).astype(bf16)
    mixed = [None] * groups
    for split in range(splits):
        pieces = [dot(hidden_turn, full[split]).astype(bf16) for full in qkv_full]
        for other in range(ranks):
            step = other * splits + split
            piece = choose(pieces, jnp.bitwise_xor(rank, other))
            mixed[step] = send_xor(piece, HEAD_GROUP, step) if step else piece
    for step in range(1, halves):
        mixed += [send_xor(piece, "sr", step) for piece in mixed[:groups]]
    out_full, key_full, val_full, cq_full, co_full = cut(mid_full, width, wide)
    cross_k = [dot(caption, full).astype(bf16) for full in key_full]
    cross_v = [dot(caption, full).astype(bf16) for full in val_full]
    (mixed[0], cross_k, cross_v) = lax.optimization_barrier((mixed[0], cross_k, cross_v))
    att_low, att_wide, logsum = attend(mixed, groups, heads)

    def by_split(pieces, split):
        own = [pieces[other * splits + split] for other in range(ranks)]
        return [choose(own, jnp.bitwise_xor(rank, place)) for place in range(ranks)]

    att_back = give_back(att_low, HEAD_GROUP)
    att_own = [
        padded(jnp.concatenate(by_split(att_back, split), axis=1)) for split in range(splits)
    ]
    col = lax.axis_index("tensor")

    def from_own(pieces):
        return [choose(pieces, jnp.bitwise_xor(col, place)) for place in range(splits)]

    att = from_own(att_own)
    up_full, down_full = (
        [two_full[place, split * width : (split + 1) * width] for split in range(splits)]
        for place in range(2)
    )

    out_one = sum(dot(att[split], out_full[split], NT) for split in range(splits))
    after_one = residual + gate_one * out_one
    mid_low = after_one.astype(bf16)
    cross_q = [dot(mid_low, full).astype(bf16) for full in cq_full]
    cross_low = cross(cross_q, cross_k, cross_v, part)
    out_two = sum(dot(cross_low[split], co_full[split], NT) for split in range(splits))
    after_two = after_one + out_two
    normed_two, inverse_two = norm_parts(after_two)
    hidden_two = (normed_two * (1.0 + scale_two) + shift_two).astype(bf16)
    inner = [dot(hidden_two, up_full[split]) for split in range(splits)]
    active = [jax.nn.gelu(values, approximate=True).astype(bf16) for values in inner]
    out_three = sum(dot(active[split], down_full[split], NT) for split in range(splits))
    result = (after_two + gate_two * out_three).astype(bf16)
    result_back = in_order(give_back(list(result.reshape(latents.shape)), "lat"), "lat")

    grad_gate_two = jnp.sum(grad_three * out_three, axis=0)
    grad_z = (gate_two * grad_three).astype(bf16)
    grad_inner = []
    for split in range(splits):
        grad_active = dot(grad_z, down_full[split])
        _, pull = jax.vjp(partial(jax.nn.gelu, approximate=True), inner[split])
        grad_inner.append(pull(grad_active)[0].astype(bf16))
    down_sum = scatter_all(pack_grid([[dot(grad_z, piece, TN).astype(bf16) for piece in active]]))
    up_sum = scatter_all(
        pack_grid([[dot(hidden_two, piece, TN).astype(bf16) for piece in grad_inner]])
    )
    grad_hidden_two = sum(dot(grad_inner[split], up_full[split], NT) for split in range(splits))
    grad_shift_two = jnp.sum(grad_hidden_two, axis=0)
    grad_scale_two = jnp.sum(grad_hidden_two * normed_two, axis=0)
    grad_two = grad_three + norm_back(grad_hidden_two * (1.0 + scale_two), normed_two, inverse_two)

    grad_out_two = grad_two.astype(bf16)
    grad_cross = [dot(grad_out_two, full).astype(bf16) for full in co_full]
    grad_cq, grad_ck, grad_cv = cross_back(cross_q, cross_k, cross_v, grad_cross, part)
    grad_one = grad_two + sum(dot(grad_cq[split], cq_full[split], NT) for split in range(splits))
    text_terms = sum(
        dot(grad_ck[split], key_full[split], NT) + dot(grad_cv[split], val_full[split], NT)
        for split in range(splits)
    )

    grad_gate_one = jnp.sum(grad_one * out_one, axis=0)
    grad_out_one = (gate_one * grad_one).astype(bf16)
    grad_att = from_own([dot(grad_out_one, full).astype(bf16) for full in out_full])
    grad_heads = [None] * groups
    for split in range(splits):
        cuts = [grad_att[split][:, place * edge : (place + 1) * edge] for place in range(ranks)]
        for other in range(ranks):
            step = other * splits + split
            piece = choose(cuts, jnp.bitwise_xor(rank, other))
            grad_heads[step] = send_xor(piece, HEAD_GROUP, step) if step else piece
    lefts = [mid_low, grad_out_two, grad_out_one]
    lefts, grad_ck, grad_cv, _ = lax.optimization_barrier((lefts, grad_ck, grad_cv, grad_att))
    lefts[0], caption_late, grad_heads = lax.optimization_barrier((lefts[0], caption, grad_heads))
    caption_turn = dot(caption_late, turn).astype(bf16)
    mid_grads = [
        [dot(left, right, TN).astype(bf16) for right in rights]
        for left, rights in (
            (caption_turn, from_own(grad_ck)),
            (caption_turn, from_own(grad_cv)),
            (dot(lefts[0], turn).astype(bf16), from_own(grad_cq)),
            (dot(lefts[1], turn).astype(bf16), from_own(cross_low)),
            (dot(lefts[2], turn).astype(bf16), att_own),
        )
    ]
    pack_a = sum_pieces(pack_for("tensor", mid_grads[:3]), "fsdp")
    pack_b = sum_pieces(pack_for(ROW, mid_grads[3:]), "fsdp")
    (grad_heads[0], pack_a, pack_b, result_back) = lax.optimization_barrier(
        (grad_heads[0], pack_a, pack_b, result_back)
    )
    pack_a, pack_b = sum_blocks(pack_a, "tensor"), sum_blocks(pack_b, ROW)
    text_sum = plane_sum(text_terms, bf16)
    grad_mix = list(attend_back(mixed, groups, grad_heads, att_wide, logsum, heads))
    (grad_mix[0], down_sum) = tie(grad_mix[0], down_sum)
    for step in range(1, halves):
        for place in range(groups):
            more = send_xor(grad_mix[step * groups + place], "sr", step)
            grad_mix[place] = (grad_mix[place].astype(f32) + more.astype(f32)).astype(bf16)
    grad_proj = give_back(grad_mix[:groups], HEAD_GROUP)
    grad_proj = [by_split(grad_proj, split) for split in range(splits)]
    one_packs = [
        pack_for(
            ROW if place % 2 else "tensor",
            [[dot(hidden_turn, grad_proj[split][place], TN).astype(bf16) for split in range(splits)]],
        )
        for place in range(ranks)
    ]
    (grad_proj, one_packs, pack_a, pack_b, text_sum) = lax.optimization_barrier(
        (grad_proj, one_packs, pack_a, pack_b, text_sum)
    )
    pack_a, pack_b = sum_blocks(pack_a, ROW), sum_blocks(pack_b, "tensor")
    one_packs = [sum_pieces(pack, "fsdp") for pack in one_packs]
    grad_hidden_one = sum(
        dot(grad_proj[split][place], qkv_full[place][split], NT)
        for place in range(ranks)
        for split in range(splits)
    )
    grad_hidden_one = dot(grad_hidden_one.astype(bf16), turn, NT)
    grad_shift_one = jnp.sum(grad_hidden_one, axis=0)
    grad_scale_one = jnp.sum(grad_hidden_one * normed_one, axis=0)
    grad_latents = grad_one + norm_back(
        grad_hidden_one * (1.0 + scale_one), normed_one, inverse_one
    )
    grad_latents = grad_latents.astype(bf16).reshape(latents.shape)
    grad_latents = in_order(give_back(list(grad_latents), "lat"), "lat")

    time_terms = jnp.stack(
        (
            grad_shift_one,
            grad_scale_one,
            grad_gate_one,
            grad_shift_two,
            grad_scale_two,
            grad_gate_two,
        )
    )
    orders = [("tensor", ROW), (ROW, "tensor")]
    for stage in range(2):
        one_packs = [
            sum_blocks(pack, orders[place % 2][stage]) for place, pack in enumerate(one_packs)
        ]
    (one_packs, up_sum) = tie(one_packs, up_sum)
    one_sums = [sum_blocks(pack, "lat", f32) for pack in one_packs]
    pack_a, pack_b = sum_blocks(pack_a, "lat", f32), sum_blocks(pack_b, "lat", f32)
    key_sum, val_sum, cq_sum, co_sum, out_sum = (
        pack[:, place * wide : place * wide + part]
        for pack, count in ((pack_a, 3), (pack_b, 2))
        for place in range(count)
    )
    grad_time = over_latents(plane_sum(time_terms, f32))
    grad_table = jnp.sum(grad_time, axis=0)
    grad_table += send_xor(grad_table, "fsdp", 1)
    owner = lax.axis_index(("fsdp", "lat", "sr", "hr"))
    grad_table = lax.dynamic_slice_in_dim(grad_table, owner * share, share, 1)
    grad_text = over_latents(text_sum.astype(bf16)).astype(f32)
    grad_qkv = jnp.stack(
        [sums[:, : 3 * edge].reshape(share, 3, edge) for sums in one_sums], axis=2
    ).reshape(share, 3, part)
    return (
        result_back,
        grad_latents.astype(f32),
        grad_text,
        grad_time.reshape(-1, 6 * width),
        grad_table,
        grad_qkv,
        out_sum.T,
        cq_sum,
        jnp.stack((key_sum, val_sum), axis=1),
        co_sum.T,
        up_sum,
        down_sum.T,
    )


def solution(mesh):
    def run(latents, text, time_vector, table, w_qkv, *others):
        fsdp, context, tensor = (mesh.shape[name] for name in ("fsdp", "context", "tensor"))
        lat = latents.shape[0] // fsdp
        group = context // lat
        ranks = math.gcd(group, w_qkv.shape[2] // (tensor * HEAD_DIM))
        sizes = (fsdp, lat, group // ranks, ranks, tensor)
        finer = Mesh(mesh.devices.reshape(sizes), ("fsdp", "lat", "sr", "hr", "tensor"))
        line = ("lat", "sr", "hr")
        shard = ("fsdp",) + line
        tokens = P("fsdp", line + ("tensor",), None)
        by_row = P(shard, "tensor")
        by_row3 = P(shard, None, "tensor")
        by_column = P("tensor", shard)
        weights = (by_row3, by_column, by_row, by_row3, by_column, by_row, by_column)
        return jax.shard_map(
            local,
            mesh=finer,
            in_specs=(tokens, P("fsdp", None, None), P("fsdp", None), P(None, shard))
            + weights
            + (tokens,),
            out_specs=(tokens, tokens, P("fsdp", None, None), P("fsdp", None), P(None, shard))
            + weights,
            check_vma=False,
        )(latents, text, time_vector, table, w_qkv, *others)

    return run
```

```python
import math
from functools import partial

import jax
import jax.numpy as jnp
from jax import lax
from jax.experimental import pallas as pl
from jax.experimental.pallas import tpu as pltpu
from jax.sharding import Mesh
from jax.sharding import PartitionSpec as P

HEAD_DIM = 72
EPSILON = 1e-06
LANES = 128
FACTOR = HEAD_DIM ** (-0.5)
FACTOR2 = FACTOR * math.log2(math.e)
VMEM_LIMIT = 56 * 1024 * 1024

f32 = jnp.float32
bf16 = jnp.bfloat16

NT = (((1,), (1,)), ((), ()))
NN = (((1,), (0,)), ((), ()))
TN = (((0,), (0,)), ((), ()))

ROW = ("sr", "hr")
EVERY = ("tensor", "fsdp", "lat", "sr", "hr")
PLANE = ("sr", "hr", "tensor")
HEAD_GROUP = ("hr", "tensor")


def dot(left, right, dims=NN):
    return lax.dot_general(left, right, dims, preferred_element_type=f32)


def norm_parts(values):
    center = values - jnp.mean(values, axis=-1, keepdims=True)
    inverse = lax.rsqrt(jnp.mean(center * center, axis=-1, keepdims=True) + EPSILON)
    return (center * inverse, inverse)


def norm_back(grad_hat, normed, inverse):
    first = jnp.mean(grad_hat, axis=-1, keepdims=True)
    second = jnp.mean(grad_hat * normed, axis=-1, keepdims=True)
    return inverse * (grad_hat - first - normed * second)


def send_xor(piece, axes, step):
    size = lax.axis_size(axes)
    return lax.ppermute(piece, axes, [(rank, rank ^ step) for rank in range(size)])


def pick(stack, index):
    return lax.dynamic_index_in_dim(stack, index, 0, keepdims=False)


def exchange(piece_for, axes):
    me = lax.axis_index(axes)
    got = [piece_for(me)]
    for step in range(1, lax.axis_size(axes)):
        got.append(send_xor(piece_for(jnp.bitwise_xor(me, step)), axes, step))
    return got


def give_back(pieces, axes):
    return [send_xor(piece, axes, step) if step else piece for step, piece in enumerate(pieces)]


def in_order(pieces, axes):
    me = lax.axis_index(axes)
    places = range(len(pieces))
    return jnp.stack([choose(pieces, jnp.bitwise_xor(me, place)) for place in places])


def choose(pieces, index):
    out = pieces[0]
    for place in range(1, len(pieces)):
        out = jnp.where(index == place, pieces[place], out)
    return out


def plane_sum(values, dtype):
    sent = values.astype(dtype)
    total = sent.astype(f32)
    for step in range(1, lax.axis_size(PLANE)):
        total += send_xor(sent, PLANE, step).astype(f32)
    return total


def over_latents(values):
    return in_order(give_back([values] * lax.axis_size("lat"), "lat"), "lat")


def tie(first, second):
    return lax.optimization_barrier((first, second))


def attend_kernel(heads, chunks, own, *refs):
    pieces = refs[:chunks]
    low_refs = refs[chunks : chunks + own]
    att_ref, lse_ref, queries, keys, vals, lows, column = refs[chunks + own :]
    edge = heads * HEAD_DIM
    index = pl.program_id(0)
    block = att_ref.shape[1]

    @pl.when(index == 0)
    def _():
        lane = lax.broadcasted_iota(jnp.int32, vals.shape[1:], 1)
        column[...] = jnp.zeros_like(column)
        for head in range(heads):
            vals[head] = jnp.where(lane == HEAD_DIM, 1.0, 0.0).astype(bf16)
            low = head * HEAD_DIM
            for number, piece in enumerate(pieces):
                count = piece.shape[0]
                rows = slice(number * count, (number + 1) * count)
                if number < own:
                    queries[head, rows] = piece[:, low : low + HEAD_DIM]
                keys[head, rows] = piece[:, edge + low : edge + low + HEAD_DIM]
                vals[head, rows, :HEAD_DIM] = piece[:, 2 * edge + low : 2 * edge + low + HEAD_DIM]

    mine = pl.ds(pl.multiple_of(index * block, block), block)

    def score(head):
        return dot(queries[head, mine, :], keys[head], NT)

    ahead = score(0)
    for head in range(heads):
        scores = ahead
        if head + 1 < heads:
            ahead = score(head + 1)
        top = jnp.max(scores, axis=1, keepdims=True) * FACTOR2
        weights = jnp.exp2(scores * FACTOR2 - top).astype(bf16)
        out = dot(weights, vals[head])
        total = out[:, HEAD_DIM : HEAD_DIM + 1]
        out = out[:, :HEAD_DIM] / total
        att_ref[head] = out
        lows[head, mine, :] = out.astype(bf16)
        column[:, head : head + 1] = top + jnp.log2(total)
    lse_ref[...] = column[...].T[: lse_ref.shape[0]]

    @pl.when(index == pl.num_programs(0) - 1)
    def _():
        for head in range(heads):
            low = head * HEAD_DIM
            for number, ref in enumerate(low_refs):
                count = ref.shape[0]
                ref[:, low : low + HEAD_DIM] = lows[head, number * count : (number + 1) * count, :]


def whole_block(shape):
    return pl.BlockSpec(shape, lambda i: (0,) * len(shape))


def attend(pieces, own, heads):
    count, width = pieces[0].shape
    rows, total = own * count, len(pieces) * count
    block = min(256, rows)
    edge = heads * HEAD_DIM
    slots = -(-heads // 8) * 8
    out = pl.pallas_call(
        partial(attend_kernel, heads, len(pieces), own),
        grid=(rows // block,),
        in_specs=[whole_block((count, width))] * len(pieces),
        out_specs=[whole_block((count, edge))] * own
        + [
            pl.BlockSpec((heads, block, HEAD_DIM), lambda i: (0, i, 0)),
            pl.BlockSpec((slots, block), lambda i: (0, i)),
        ],
        out_shape=[jax.ShapeDtypeStruct((count, edge), bf16)] * own
        + [
            jax.ShapeDtypeStruct((heads, rows, HEAD_DIM), f32),
            jax.ShapeDtypeStruct((slots, rows), f32),
        ],
        scratch_shapes=[
            pltpu.VMEM((heads, rows, HEAD_DIM), bf16),
            pltpu.VMEM((heads, total, HEAD_DIM), bf16),
            pltpu.VMEM((heads, total, LANES), bf16),
            pltpu.VMEM((heads, rows, HEAD_DIM), bf16),
            pltpu.VMEM((block, LANES), f32),
        ],
        cost_estimate=pl.CostEstimate(
            flops=8 * heads * rows * total * LANES,
            transcendentals=heads * rows * total,
            bytes_accessed=4 * total * width,
        ),
        compiler_params=pltpu.CompilerParams(vmem_limit_bytes=VMEM_LIMIT),
    )(*pieces)
    return (out[:own], out[own], out[own + 1])


def attend_back_kernel(heads, chunk, chunks, own, *refs):
    pieces = refs[:chunks]
    grad_refs = refs[chunks : chunks + own]
    att_ref, lse_ref = refs[chunks + own : chunks + own + 2]
    outs = refs[chunks + own + 2 : 2 * chunks + own + 2]
    queries, keys, vals, grads, turned, dq, dk, dv, column = refs[2 * chunks + own + 2 :]
    edge = heads * HEAD_DIM
    index = pl.program_id(0)
    block = att_ref.shape[1]
    total = keys.shape[1]

    @pl.when(index == 0)
    def _():
        turned[...] = jnp.zeros_like(turned)
        column[...] = jnp.zeros_like(column)
        dk[...] = jnp.zeros_like(dk)
        dv[...] = jnp.zeros_like(dv)
        for head in range(heads):
            low = head * HEAD_DIM
            for number, piece in enumerate(pieces):
                count = piece.shape[0]
                rows = slice(number * count, (number + 1) * count)
                if number < own:
                    queries[head, rows] = piece[:, low : low + HEAD_DIM]
                    grads[head, rows] = grad_refs[number][:, low : low + HEAD_DIM]
                key = piece[:, edge + low : edge + low + HEAD_DIM]
                keys[head, rows] = key
                turned[head, :HEAD_DIM, rows] = key.astype(f32).T.astype(bf16)
                vals[head, rows] = piece[:, 2 * edge + low : 2 * edge + low + HEAD_DIM]

    mine = pl.ds(pl.multiple_of(index * block, block), block)
    for head in range(heads):
        column[:, head : head + 1] = jnp.sum(
            att_ref[head] * grads[head, mine, :].astype(f32), axis=1, keepdims=True
        )
    deltas = column[...].T
    for head in range(heads):
        query = queries[head, mine, :]
        grad = grads[head, mine, :]
        lse = lse_ref[head : head + 1, :]
        delta = deltas[head : head + 1, :]
        turned_grad = jnp.zeros((turned.shape[1], block), f32)
        for start in range(0, total, chunk):
            part = slice(start, start + chunk)
            scores = dot(keys[head, part, :], query, NT)
            grad_probs = dot(vals[head, part, :], grad, NT)
            probs = jnp.exp2(scores * FACTOR2 - lse)
            grad_scores = (probs * (grad_probs - delta)).astype(bf16)
            dv[head, part, :] += dot(probs.astype(bf16), grad)
            dk[head, part, :] += dot(grad_scores, query)
            turned_grad += dot(turned[head, :, part], grad_scores)
        dq[head, mine, :] = (turned_grad.T[:, :HEAD_DIM] * FACTOR).astype(bf16)

    @pl.when(index == pl.num_programs(0) - 1)
    def _():
        for number, ref in enumerate(outs):
            count = ref.shape[0]
            rows = slice(number * count, (number + 1) * count)
            ref[...] = jnp.zeros_like(ref)
            for head in range(heads):
                low = head * HEAD_DIM
                if number < own:
                    ref[:, low : low + HEAD_DIM] = dq[head, rows]
                ref[:, edge + low : edge + low + HEAD_DIM] = (dk[head, rows] * FACTOR).astype(bf16)
                ref[:, 2 * edge + low : 2 * edge + low + HEAD_DIM] = dv[head, rows].astype(bf16)


def attend_back(pieces, own, grads, att, lse, heads):
    count, width = pieces[0].shape
    rows, total = own * count, len(pieces) * count
    block = min(256, rows)
    edge = heads * HEAD_DIM
    slots = lse.shape[0]
    return pl.pallas_call(
        partial(attend_back_kernel, heads, min(512, total), len(pieces), own),
        grid=(rows // block,),
        in_specs=[whole_block((count, width))] * len(pieces)
        + [whole_block((count, edge))] * own
        + [
            pl.BlockSpec((heads, block, HEAD_DIM), lambda i: (0, i, 0)),
            pl.BlockSpec((slots, block), lambda i: (0, i)),
        ],
        out_specs=[whole_block((count, width))] * len(pieces),
        out_shape=[jax.ShapeDtypeStruct((count, width), bf16)] * len(pieces),
        scratch_shapes=[
            pltpu.VMEM((heads, rows, HEAD_DIM), bf16),
            pltpu.VMEM((heads, total, HEAD_DIM), bf16),
            pltpu.VMEM((heads, total, HEAD_DIM), bf16),
            pltpu.VMEM((heads, rows, HEAD_DIM), bf16),
            pltpu.VMEM((heads, LANES, total), bf16),
            pltpu.VMEM((heads, rows, HEAD_DIM), bf16),
            pltpu.VMEM((heads, total, HEAD_DIM), f32),
            pltpu.VMEM((heads, total, HEAD_DIM), f32),
            pltpu.VMEM((block, LANES), f32),
        ],
        cost_estimate=pl.CostEstimate(
            flops=20 * heads * rows * total * LANES,
            transcendentals=heads * rows * total,
            bytes_accessed=8 * total * width,
        ),
        compiler_params=pltpu.CompilerParams(vmem_limit_bytes=VMEM_LIMIT),
    )(*pieces, *grads, att, lse)


def head_lanes(part):
    return [slice(low, low + HEAD_DIM) for low in range(0, part, HEAD_DIM)]


def cross_kernel(part, splits, *refs):
    q_refs, k_refs, v_refs, out_refs = (refs[splits * i : splits * (i + 1)] for i in range(4))
    for q_ref, k_ref, v_ref, out_ref in zip(q_refs, k_refs, v_refs, out_refs):
        fill = out_ref.shape[1] - part
        if fill:
            out_ref[:, part:] = jnp.zeros((out_ref.shape[0], fill), bf16)
        for lanes in head_lanes(part):
            scores = dot(q_ref[:, lanes], k_ref[:, lanes], NT) * FACTOR
            weights = jnp.exp(scores - jnp.max(scores, axis=1, keepdims=True))
            probs = weights / jnp.sum(weights, axis=1, keepdims=True)
            out_ref[:, lanes] = dot(probs.astype(bf16), v_ref[:, lanes]).astype(bf16)


def cross(queries, keys, values, part):
    splits = len(queries)
    rows, width = queries[0].shape
    texts = keys[0].shape[0]
    block = min(512, rows)
    split = pl.BlockSpec((block, width), lambda i: (i, 0))
    return pl.pallas_call(
        partial(cross_kernel, part, splits),
        grid=(rows // block,),
        in_specs=[split] * splits + [whole_block((texts, width))] * (2 * splits),
        out_specs=[split] * splits,
        out_shape=[jax.ShapeDtypeStruct((rows, width), bf16)] * splits,
        compiler_params=pltpu.CompilerParams(vmem_limit_bytes=VMEM_LIMIT),
    )(*queries, *keys, *values)


def cross_back_kernel(part, splits, *refs):
    q_refs, k_refs, v_refs, grad_refs, dq_refs, dk_refs, dv_refs, dk_sums, dv_sums = (
        refs[splits * i : splits * (i + 1)] for i in range(9)
    )
    first = pl.program_id(0) == 0
    last = pl.program_id(0) == pl.num_programs(0) - 1
    for q_ref, k_ref, v_ref, grad_ref, dq_ref, dk, dv in zip(
        q_refs, k_refs, v_refs, grad_refs, dq_refs, dk_sums, dv_sums
    ):

        @pl.when(first)
        def _():
            dk[...] = jnp.zeros_like(dk)
            dv[...] = jnp.zeros_like(dv)

        fill = dq_ref.shape[1] - part
        if fill:
            dq_ref[:, part:] = jnp.zeros((dq_ref.shape[0], fill), bf16)
        for lanes in head_lanes(part):
            query = q_ref[:, lanes]
            key = k_ref[:, lanes]
            grad = grad_ref[:, lanes]
            scores = dot(query, key, NT) * FACTOR
            weights = jnp.exp(scores - jnp.max(scores, axis=1, keepdims=True))
            probs = weights / jnp.sum(weights, axis=1, keepdims=True)
            grad_probs = dot(grad, v_ref[:, lanes], NT)
            delta = jnp.sum(probs * grad_probs, axis=1, keepdims=True)
            grad_scores = (probs * (grad_probs - delta)).astype(bf16)
            dq_ref[:, lanes] = (dot(grad_scores, key) * FACTOR).astype(bf16)
            dk[:, lanes] += dot(grad_scores, query, TN)
            dv[:, lanes] += dot(probs.astype(bf16), grad, TN)

    @pl.when(last)
    def _():
        for dk_ref, dv_ref, dk, dv in zip(dk_refs, dv_refs, dk_sums, dv_sums):
            dk_ref[...] = (dk[...] * FACTOR).astype(bf16)
            dv_ref[...] = dv[...].astype(bf16)


def cross_back(queries, keys, values, grads, part):
    splits = len(queries)
    rows, width = queries[0].shape
    texts = keys[0].shape[0]
    block = min(512, rows)
    whole = whole_block((texts, width))
    split = pl.BlockSpec((block, width), lambda i: (i, 0))
    out = pl.pallas_call(
        partial(cross_back_kernel, part, splits),
        grid=(rows // block,),
        in_specs=[split] * splits + [whole] * (2 * splits) + [split] * splits,
        out_specs=[split] * splits + [whole] * (2 * splits),
        out_shape=[jax.ShapeDtypeStruct((rows, width), bf16)] * splits
        + [jax.ShapeDtypeStruct((texts, width), bf16)] * (2 * splits),
        scratch_shapes=[pltpu.VMEM((texts, width), f32)] * (2 * splits),
        compiler_params=pltpu.CompilerParams(vmem_limit_bytes=VMEM_LIMIT),
    )(*queries, *keys, *values, *grads)
    return (out[:splits], out[splits : 2 * splits], out[2 * splits :])


def assemble_kernel(plan, count, *refs):
    sources, outs, sems = refs[:count], refs[count:-1], refs[-1]
    copies = []
    for number, (source, start, rows, column, size, place, row, shift) in enumerate(plan):
        copies.append(
            pltpu.make_async_copy(
                sources[source].at[pl.ds(start, rows), pl.ds(column, size)],
                outs[place].at[pl.ds(row, rows), pl.ds(shift, size)],
                sems.at[number],
            )
        )
    for copy in copies:
        copy.start()
    for copy in copies:
        copy.wait()


def lay(sources, plan, shapes):
    anywhere = pl.BlockSpec(memory_space=pl.ANY)
    return list(
        pl.pallas_call(
            partial(assemble_kernel, plan, len(sources)),
            in_specs=[anywhere] * len(sources),
            out_specs=[pl.BlockSpec(memory_space=pltpu.VMEM)] * len(shapes),
            out_shape=[jax.ShapeDtypeStruct(shape, bf16) for shape in shapes],
            scratch_shapes=[pltpu.SemaphoreType.DMA((len(plan),))],
            compiler_params=pltpu.CompilerParams(vmem_limit_bytes=VMEM_LIMIT),
        )(*sources)
    )


def assemble(stacks):
    sources = [piece for stack in stacks for piece in stack]
    plan, shapes = [], []
    for stack in stacks:
        row, width = 0, stack[0].shape[1]
        for piece in stack:
            plan.append((len(plan), 0, piece.shape[0], 0, width, len(shapes), row, 0))
            row += piece.shape[0]
        shapes.append((row, width))
    return lay(sources, plan, shapes)


def cut(source, rows, columns):
    grid = [
        (place, row) for place in range(source.shape[1] // columns) for row in range(source.shape[0] // rows)
    ]
    plan = [
        (0, row * rows, rows, place * columns, columns, number, 0, 0)
        for number, (place, row) in enumerate(grid)
    ]
    out = lay([source], plan, [(rows, columns)] * len(grid))
    count = source.shape[0] // rows
    return [out[place : place + count] for place in range(0, len(out), count)]


def with_others(piece, axes):
    return [piece] + [send_xor(piece, axes, step) for step in range(1, lax.axis_size(axes))]


def gather(shard, tensor_first):
    start = jnp.concatenate(with_others(shard, "lat"))
    if tensor_first and lax.axis_size("tensor") * lax.axis_size(ROW) <= 8:
        stacks = [with_others(piece, ROW) for piece in with_others(start, "tensor")]
    else:
        half = assemble([with_others(start, ROW)])[0]
        stacks = [[piece] for piece in with_others(half, "tensor")]
    cores = range(1, lax.axis_size("fsdp"))
    stacks = [
        stack + [send_xor(piece, "fsdp", step) for step in cores for piece in stack] for stack in stacks
    ]
    return assemble(stacks), start


def gather_all(shard):
    return lax.all_gather(shard, EVERY, axis=shard.ndim - 2, tiled=True)


def scatter_all(pack):
    return lax.psum_scatter(pack, EVERY, scatter_dimension=0, tiled=True).astype(f32)


def sum_pieces(pieces, axes, dtype=bf16):
    total = pieces[0].astype(f32)
    for step in range(1, len(pieces)):
        total += send_xor(pieces[step], axes, step).astype(f32)
    return total.astype(dtype)


def sum_blocks(pack, axes, dtype=bf16):
    count = lax.axis_size(axes)
    size = pack.shape[0] // count
    blocks = [pack[place * size : (place + 1) * size] for place in range(count)]
    return sum_pieces(blocks, axes, dtype)


def pack_for(first, grads):
    splits, cores, ranks = (lax.axis_size(axes) for axes in ("tensor", "fsdp", ROW))
    rows, columns = grads[0][0].shape
    size = rows // cores // ranks
    plan = []
    for piece, row in enumerate(grads):
        for split in range(splits):
            for core in range(cores):
                for rank in range(ranks):
                    place = split * ranks + rank if first == "tensor" else rank * splits + split
                    source = (piece * splits + split, (core * ranks + rank) * size, size, 0, columns)
                    plan.append(source + (core, place * size, piece * columns))
    sources = [values for row in grads for values in row]
    return lay(sources, plan, [(splits * rows // cores, columns * len(grads))] * cores)


def pack_grid(grads):
    rows, columns = grads[0][0].shape
    count = len(grads[0])
    plan = [
        (place * count + row, 0, rows, 0, columns, 0, row * rows, place * columns)
        for place in range(len(grads))
        for row in range(count)
    ]
    return lay([values for row in grads for values in row], plan, [(rows * count, columns * len(grads))])[0]


def own_order(share, width):
    cores, lats, rows = (lax.axis_size(axes) for axes in ("fsdp", "lat", ROW))
    place = lax.iota(jnp.int32, width)
    block, rest = place // share, place % share
    lat = jnp.bitwise_xor(block % lats, lax.axis_index("lat"))
    row = jnp.bitwise_xor(block // lats % rows, lax.axis_index(ROW))
    core = jnp.bitwise_xor(block // (lats * rows), lax.axis_index("fsdp"))
    natural = ((core * lats + lat) * rows + row) * share + rest
    return (lax.broadcasted_iota(jnp.int32, (width, width), 0) == natural[None, :]).astype(bf16)


def local(
    latents, text, time_vector, table, w_qkv, w_out, w_cq, w_ckv, w_co, w_up, w_down, cotangent
):
    width = latents.shape[2]
    share = w_cq.shape[0]
    part = w_cq.shape[1]
    inner_part = w_up.shape[1]
    splits = lax.axis_size("tensor")
    ranks = lax.axis_size("hr")
    halves = lax.axis_size("sr")
    edge = part // ranks
    heads = edge // HEAD_DIM
    groups = ranks * splits
    piece_width = -(-(3 * edge + 6) // LANES) * LANES
    wide = -(-part // LANES) * LANES
    slot = lax.axis_index("lat")
    rank = lax.axis_index("hr")

    def padded(values):
        return jnp.pad(values, ((0, 0), (0, wide - part)))

    latents_got = exchange(partial(pick, latents), "lat")
    mid_shard = jnp.concatenate(
        [padded(piece) for piece in (w_out.T, w_ckv[:, 0], w_ckv[:, 1], w_cq, w_co.T)], axis=1
    )
    shard_qkv = jnp.transpose(w_qkv.reshape(share, 3, ranks, edge), (2, 0, 1, 3)).reshape(
        ranks, share, 3 * edge
    )
    fill = jnp.pad(table.T, ((0, 0), (0, piece_width - 3 * edge - 6)))
    qkv_got = [
        gather(jnp.concatenate((shard_qkv[place], fill), axis=1), place % 2 == 0)
        for place in range(ranks)
    ]
    qkv_full = [full for full, _ in qkv_got]
    mid_full = gather_all(mid_shard)
    two_full = gather_all(jnp.stack((w_up, w_down.T)))

    turn = own_order(share, width)
    residual = jnp.concatenate(latents_got, axis=0).astype(f32)
    cotangent, _ = tie(cotangent, qkv_full[0][0])
    grad_three = jnp.concatenate(exchange(partial(pick, cotangent), "lat"), axis=0).astype(f32)
    rows = residual.shape[0]
    caption = pick(text, slot)
    table_full = dot(qkv_full[0][0][:, 3 * edge : 3 * edge + 6].T, turn, NT)
    modulate = table_full + pick(time_vector, slot).astype(f32).reshape(6, width)
    shift_one, scale_one, gate_one, shift_two, scale_two, gate_two = (
        modulate[row : row + 1] for row in range(6)
    )

    normed_one, inverse_one = norm_parts(residual)
    hidden_one = (normed_one * (1.0 + scale_one) + shift_one).astype(bf16)
    hidden_turn = dot(hidden_one, turn).astype(bf16)
    mixed = [None] * groups
    for split in range(splits):
        pieces = [dot(hidden_turn, full[split]).astype(bf16) for full in qkv_full]
        for other in range(ranks):
            step = other * splits + split
            piece = choose(pieces, jnp.bitwise_xor(rank, other))
            mixed[step] = send_xor(piece, HEAD_GROUP, step) if step else piece
    for step in range(1, halves):
        mixed += [send_xor(piece, "sr", step) for piece in mixed[:groups]]
    out_full, key_full, val_full, cq_full, co_full = cut(mid_full, width, wide)
    cross_k = [dot(caption, full).astype(bf16) for full in key_full]
    cross_v = [dot(caption, full).astype(bf16) for full in val_full]
    (mixed[0], cross_k, cross_v) = lax.optimization_barrier((mixed[0], cross_k, cross_v))
    att_low, att_wide, logsum = attend(mixed, groups, heads)

    def by_split(pieces, split):
        own = [pieces[other * splits + split] for other in range(ranks)]
        return [choose(own, jnp.bitwise_xor(rank, place)) for place in range(ranks)]

    att_back = give_back(att_low, HEAD_GROUP)
    att_own = [
        padded(jnp.concatenate(by_split(att_back, split), axis=1)) for split in range(splits)
    ]
    col = lax.axis_index("tensor")

    def from_own(pieces):
        return [choose(pieces, jnp.bitwise_xor(col, place)) for place in range(splits)]

    att = from_own(att_own)
    up_full, down_full = (
        [two_full[place, split * width : (split + 1) * width] for split in range(splits)]
        for place in range(2)
    )

    out_one = sum(dot(att[split], out_full[split], NT) for split in range(splits))
    after_one = residual + gate_one * out_one
    mid_low = after_one.astype(bf16)
    cross_q = [dot(mid_low, full).astype(bf16) for full in cq_full]
    cross_low = cross(cross_q, cross_k, cross_v, part)
    out_two = sum(dot(cross_low[split], co_full[split], NT) for split in range(splits))
    after_two = after_one + out_two
    normed_two, inverse_two = norm_parts(after_two)
    hidden_two = (normed_two * (1.0 + scale_two) + shift_two).astype(bf16)
    inner = [dot(hidden_two, up_full[split]) for split in range(splits)]
    active = [jax.nn.gelu(values, approximate=True).astype(bf16) for values in inner]
    out_three = sum(dot(active[split], down_full[split], NT) for split in range(splits))
    result = (after_two + gate_two * out_three).astype(bf16)
    result_back = in_order(give_back(list(result.reshape(latents.shape)), "lat"), "lat")

    grad_gate_two = jnp.sum(grad_three * out_three, axis=0)
    grad_z = (gate_two * grad_three).astype(bf16)
    grad_inner = []
    for split in range(splits):
        grad_active = dot(grad_z, down_full[split])
        _, pull = jax.vjp(partial(jax.nn.gelu, approximate=True), inner[split])
        grad_inner.append(pull(grad_active)[0].astype(bf16))
    down_sum = scatter_all(pack_grid([[dot(grad_z, piece, TN).astype(bf16) for piece in active]]))
    up_sum = scatter_all(
        pack_grid([[dot(hidden_two, piece, TN).astype(bf16) for piece in grad_inner]])
    )
    grad_hidden_two = sum(dot(grad_inner[split], up_full[split], NT) for split in range(splits))
    grad_shift_two = jnp.sum(grad_hidden_two, axis=0)
    grad_scale_two = jnp.sum(grad_hidden_two * normed_two, axis=0)
    grad_two = grad_three + norm_back(grad_hidden_two * (1.0 + scale_two), normed_two, inverse_two)

    grad_out_two = grad_two.astype(bf16)
    grad_cross = [dot(grad_out_two, full).astype(bf16) for full in co_full]
    grad_cq, grad_ck, grad_cv = cross_back(cross_q, cross_k, cross_v, grad_cross, part)
    grad_one = grad_two + sum(dot(grad_cq[split], cq_full[split], NT) for split in range(splits))
    text_terms = sum(
        dot(grad_ck[split], key_full[split], NT) + dot(grad_cv[split], val_full[split], NT)
        for split in range(splits)
    )

    grad_gate_one = jnp.sum(grad_one * out_one, axis=0)
    grad_out_one = (gate_one * grad_one).astype(bf16)
    grad_att = from_own([dot(grad_out_one, full).astype(bf16) for full in out_full])
    grad_heads = [None] * groups
    for split in range(splits):
        cuts = [grad_att[split][:, place * edge : (place + 1) * edge] for place in range(ranks)]
        for other in range(ranks):
            step = other * splits + split
            piece = choose(cuts, jnp.bitwise_xor(rank, other))
            grad_heads[step] = send_xor(piece, HEAD_GROUP, step) if step else piece
    lefts = [mid_low, grad_out_two, grad_out_one]
    lefts, grad_ck, grad_cv, _ = lax.optimization_barrier((lefts, grad_ck, grad_cv, grad_att))
    lefts[0], caption_late, grad_heads = lax.optimization_barrier((lefts[0], caption, grad_heads))
    caption_turn = dot(caption_late, turn).astype(bf16)
    mid_grads = [
        [dot(left, right, TN).astype(bf16) for right in rights]
        for left, rights in (
            (caption_turn, from_own(grad_ck)),
            (caption_turn, from_own(grad_cv)),
            (dot(lefts[0], turn).astype(bf16), from_own(grad_cq)),
            (dot(lefts[1], turn).astype(bf16), from_own(cross_low)),
            (dot(lefts[2], turn).astype(bf16), att_own),
        )
    ]
    pack_a = sum_pieces(pack_for("tensor", mid_grads[:3]), "fsdp")
    pack_b = sum_pieces(pack_for(ROW, mid_grads[3:]), "fsdp")
    (grad_heads[0], pack_a, pack_b, result_back) = lax.optimization_barrier(
        (grad_heads[0], pack_a, pack_b, result_back)
    )
    pack_a, pack_b = sum_blocks(pack_a, "tensor"), sum_blocks(pack_b, ROW)
    text_sum = plane_sum(text_terms, bf16)
    grad_mix = list(attend_back(mixed, groups, grad_heads, att_wide, logsum, heads))
    (grad_mix[0], pack_a, pack_b, down_sum) = lax.optimization_barrier(
        (grad_mix[0], pack_a, pack_b, down_sum)
    )
    for step in range(1, halves):
        for place in range(groups):
            more = send_xor(grad_mix[step * groups + place], "sr", step)
            grad_mix[place] = (grad_mix[place].astype(f32) + more.astype(f32)).astype(bf16)
    grad_proj = give_back(grad_mix[:groups], HEAD_GROUP)
    grad_proj = [by_split(grad_proj, split) for split in range(splits)]
    one_packs = [
        pack_for(
            ROW if place % 2 else "tensor",
            [[dot(hidden_turn, grad_proj[split][place], TN).astype(bf16) for split in range(splits)]],
        )
        for place in range(ranks)
    ]
    (grad_proj, one_packs, pack_a, pack_b, text_sum) = lax.optimization_barrier(
        (grad_proj, one_packs, pack_a, pack_b, text_sum)
    )
    pack_a, pack_b = sum_blocks(pack_a, ROW), sum_blocks(pack_b, "tensor")
    one_packs = [sum_pieces(pack, "fsdp") for pack in one_packs]
    grad_hidden_one = sum(
        dot(grad_proj[split][place], qkv_full[place][split], NT)
        for place in range(ranks)
        for split in range(splits)
    )
    grad_hidden_one = dot(grad_hidden_one.astype(bf16), turn, NT)
    grad_shift_one = jnp.sum(grad_hidden_one, axis=0)
    grad_scale_one = jnp.sum(grad_hidden_one * normed_one, axis=0)
    grad_latents = grad_one + norm_back(
        grad_hidden_one * (1.0 + scale_one), normed_one, inverse_one
    )
    grad_latents = grad_latents.astype(bf16).reshape(latents.shape)
    grad_latents = in_order(give_back(list(grad_latents), "lat"), "lat")

    time_terms = jnp.stack(
        (
            grad_shift_one,
            grad_scale_one,
            grad_gate_one,
            grad_shift_two,
            grad_scale_two,
            grad_gate_two,
        )
    )
    orders = [("tensor", ROW), (ROW, "tensor")]
    for stage in range(2):
        one_packs = [
            sum_blocks(pack, orders[place % 2][stage]) for place, pack in enumerate(one_packs)
        ]
    (one_packs, up_sum) = tie(one_packs, up_sum)
    one_sums = [sum_blocks(pack, "lat", f32) for pack in one_packs]
    pack_a, pack_b = sum_blocks(pack_a, "lat", f32), sum_blocks(pack_b, "lat", f32)
    key_sum, val_sum, cq_sum, co_sum, out_sum = (
        pack[:, place * wide : place * wide + part]
        for pack, count in ((pack_a, 3), (pack_b, 2))
        for place in range(count)
    )
    grad_time = over_latents(plane_sum(time_terms, f32))
    grad_table = jnp.sum(grad_time, axis=0)
    grad_table += send_xor(grad_table, "fsdp", 1)
    owner = lax.axis_index(("fsdp", "lat", "sr", "hr"))
    grad_table = lax.dynamic_slice_in_dim(grad_table, owner * share, share, 1)
    grad_text = over_latents(text_sum.astype(bf16)).astype(f32)
    grad_qkv = jnp.stack(
        [sums[:, : 3 * edge].reshape(share, 3, edge) for sums in one_sums], axis=2
    ).reshape(share, 3, part)
    return (
        result_back,
        grad_latents.astype(f32),
        grad_text,
        grad_time.reshape(-1, 6 * width),
        grad_table,
        grad_qkv,
        out_sum.T,
        cq_sum,
        jnp.stack((key_sum, val_sum), axis=1),
        co_sum.T,
        up_sum,
        down_sum.T,
    )


def solution(mesh):
    def run(latents, text, time_vector, table, w_qkv, *others):
        fsdp, context, tensor = (mesh.shape[name] for name in ("fsdp", "context", "tensor"))
        lat = latents.shape[0] // fsdp
        group = context // lat
        ranks = math.gcd(group, w_qkv.shape[2] // (tensor * HEAD_DIM))
        sizes = (fsdp, lat, group // ranks, ranks, tensor)
        finer = Mesh(mesh.devices.reshape(sizes), ("fsdp", "lat", "sr", "hr", "tensor"))
        line = ("lat", "sr", "hr")
        shard = ("fsdp",) + line
        tokens = P("fsdp", line + ("tensor",), None)
        by_row = P(shard, "tensor")
        by_row3 = P(shard, None, "tensor")
        by_column = P("tensor", shard)
        weights = (by_row3, by_column, by_row, by_row3, by_column, by_row, by_column)
        return jax.shard_map(
            local,
            mesh=finer,
            in_specs=(tokens, P("fsdp", None, None), P("fsdp", None), P(None, shard))
            + weights
            + (tokens,),
            out_specs=(tokens, tokens, P("fsdp", None, None), P("fsdp", None), P(None, shard))
            + weights,
            check_vma=False,
        )(latents, text, time_vector, table, w_qkv, *others)

    return run
```
